128 devices in a mesh: dp: 16 (over x, z), seq: 8 (over y, core).
Axes of the slice: x: 4, y: 4, z: 4, core: 2. Of those that a mesh axis runs over, the one named last changes fastest.
Arguments:
- hidden: bfloat16 [16, 2048, 4096], P('dp', 'seq'), may hold values from -6 to 6
- frozen_queries: bfloat16 [16, 2048, 2048], P('dp', 'seq'), may hold values from -200 to 200
- frozen_keys: bfloat16 [16, 2048, 2048], P('dp', 'seq'), may hold values from -8 to 8
- frozen_values: bfloat16 [16, 2048, 2048], P('dp', 'seq'), may hold values from -6 to 6
- document_length_list: int32 [16, 8], P('dp'), may hold values from 1 to 1024, 2048 in all within a row
- query_down_weight: bfloat16 [4096, 64], replicated, may hold values from -0.09375 to 0.09375
- query_up_weight: bfloat16 [64, 2048], replicated, may hold values from -0.75 to 0.75
- value_down_weight: bfloat16 [4096, 64], replicated, may hold values from -0.09375 to 0.09375
- value_up_weight: bfloat16 [64, 2048], replicated, may hold values from -0.75 to 0.75
- output_gradient: bfloat16 [16, 2048, 2048], P('dp', 'seq'), may hold values from -0.59765625 to 0.59765625
Outputs:
- attn_out: bfloat16 [16, 2048, 2048], P('dp', 'seq')
- grad_a_q: float32 [4096, 64], replicated
- query_up_gradient: float32 [64, 2048], replicated
- grad_a_v: float32 [4096, 64], replicated
- value_up_gradient: float32 [64, 2048], replicated
The draws below stay inside these ranges and needn't reach their ends.
Inputs may be any that keep to these rules, and one draw needn't show every extreme that they name: `document_length_list`: the 8 lengths of a micro-batch sum to 2048.
All inputs are finite; a program needn't handle non-finite values.
Results may differ from the reference program's by a relative error of at most 0.017.
Values may be sent and summed in bfloat16 or wider, within the bound.
No kernel may reach another device: no remote copies, remote signals or barrier semaphores. Data moves between devices by JAX's collectives and lax.ppermute only.
A program may use at most 128 MiB of HBM per device.

```python
import math
import jax
import jax.numpy as jnp
import numpy as np
from jax import lax

MODEL_WIDTH = 4096
HEAD_COUNT = 16
HEAD_SIZE = 128
ADAPTER_RANK = 64
NDOC = 8
LENGTH = 2048
MB = 16


def shared_draw(key):
    base_rows = jnp.clip(jax.random.normal(jax.random.fold_in(key, 11), (MB, LENGTH, HEAD_COUNT * HEAD_SIZE), jnp.float32), -6.0, 6.0)
    return base_rows


def draw_frozen_keys(key, part):
    base_rows = shared_draw(key)
    return base_rows.astype(jnp.bfloat16)


def draw_frozen_queries(key, part):
    key = jax.random.fold_in(key, 4)
    drawn_rows = jnp.clip(jax.random.normal(key, (MB, LENGTH, HEAD_COUNT * HEAD_SIZE), jnp.float32), -6.0, 6.0)
    return drawn_rows.astype(jnp.bfloat16)


def level_of(key, extent, pieces, smallest, largest):
    gain, own = 1.0, jax.random.fold_in(key, 6)
    for dim, parts in pieces:
        draws = jnp.exp(jax.random.uniform(jax.random.fold_in(own, dim), (parts,), jnp.float32, smallest / len(pieces), largest / len(pieces)))
        gain = gain * jnp.repeat(draws, extent[dim] // parts).reshape([-1 if axis == dim else 1 for axis in range(len(extent))])
    return gain


def profile(count, total, bound, lean):
    weights = [(1 << 20) // math.isqrt(rank ** lean) + 1 for rank in range(2, count + 1)]
    rest, holding = total - bound - (count - 1), [1] * (count - 1)
    while rest > 0:
        candidates = [i for i in range(count - 1) if holding[i] < bound]
        mass, budget = sum([weights[i] for i in candidates]), rest
        for i in candidates:
            addition = min(bound - holding[i], max(1, budget * weights[i] // mass), rest)
            holding[i] = holding[i] + addition
            rest = rest - addition
    return np.array([bound] + holding)


def uneven_parts(key, number_of, total, limit, slope):
    if number_of == 2:
        one = jax.random.randint(key, (), max(1, total - limit), min(limit, total - 1) + 1)
        return jnp.stack([one, total - one])
    lengths = jnp.asarray(profile(number_of, total, limit, slope), jnp.int32)
    couples = (number_of - 1) // 2
    donor, sink = lengths[1:1 + 2 * couples:2], lengths[2:2 + 2 * couples:2]
    room = jnp.minimum(donor - 1, limit - sink)
    shifted = jax.random.randint(jax.random.fold_in(key, 1), (couples,), 0, 1 << 20) % (room + 1)
    lengths = lengths.at[1:1 + 2 * couples:2].set(donor - shifted).at[2:2 + 2 * couples:2].set(sink + shifted)
    return lengths[jax.random.permutation(jax.random.fold_in(key, 2), number_of)]


def noise(rng, extent, spread, limit, split=(), held_as=jnp.bfloat16):
    gain = level_of(rng, extent, split, -0.22, 0.18) if split else 1.0
    drawn = jax.random.normal(rng, extent, jnp.float32) * spread * gain
    return jnp.minimum(jnp.maximum(drawn, -limit), limit).astype(held_as)


def setup_inputs(seed: int = 0) -> dict:
    key_of = jax.random.split(jax.random.key(seed), 11)
    hidden = noise(key_of[0], (MB, LENGTH, MODEL_WIDTH), 1.0, 6.0, ((0, 16), (1, 8)))
    frozen_queries = draw_frozen_queries(jax.random.fold_in(key_of[10], 71), 0)
    frozen_keys = draw_frozen_keys(jax.random.fold_in(key_of[10], 71), 0)
    frozen_values = noise(key_of[3], (MB, LENGTH, HEAD_COUNT * HEAD_SIZE), 1.0, 6.0, ((0, 16), (1, 8)))
    document_length_list = jax.vmap(lambda own: uneven_parts(own, NDOC, LENGTH, LENGTH // 2, 2))(jax.random.split(key_of[4], MB)).reshape((MB, NDOC)).astype(jnp.int32)
    query_down_weight = noise(key_of[5], (MODEL_WIDTH, ADAPTER_RANK), MODEL_WIDTH ** -0.5, 0.09375)
    query_up_weight = noise(key_of[6], (ADAPTER_RANK, HEAD_COUNT * HEAD_SIZE), ADAPTER_RANK ** -0.5, 0.75)
    value_down_weight = noise(key_of[7], (MODEL_WIDTH, ADAPTER_RANK), MODEL_WIDTH ** -0.5, 0.09375)
    value_up_weight = noise(key_of[8], (ADAPTER_RANK, HEAD_COUNT * HEAD_SIZE), ADAPTER_RANK ** -0.5, 0.75)
    output_gradient = noise(key_of[9], (MB, LENGTH, HEAD_COUNT * HEAD_SIZE), 0.1, 0.59765625, ((0, 16), (1, 8)))
    return dict(hidden=hidden, frozen_queries=frozen_queries, frozen_keys=frozen_keys, frozen_values=frozen_values, document_length_list=document_length_list, query_down_weight=query_down_weight, query_up_weight=query_up_weight, value_down_weight=value_down_weight, value_up_weight=value_up_weight, output_gradient=output_gradient)


ADAPTER_SCALE = 2.0
NEG_FILL = -1e30


def document_ids(doc_sizes, length_all):
    doc_ends = jnp.cumsum(doc_sizes)
    position = jnp.arange(length_all, dtype=jnp.int32)
    return jnp.sum((position[:, None] >= doc_ends[None, :]).astype(jnp.int32), axis=1)


def head_pass(operands, documents):
    query_row_list, key_rows, value_row_list, upstream = operands
    scaling = HEAD_SIZE ** -0.5
    scores = jnp.dot(query_row_list, key_rows.T, preferred_element_type=jnp.float32) * scaling
    position = jnp.arange(LENGTH, dtype=jnp.int32)
    allowed = (position[None, :] <= position[:, None]) & (documents[None, :] == documents[:, None])
    scores = jnp.where(allowed, scores, NEG_FILL)
    maximum = jnp.max(scores, axis=1, keepdims=True)
    powers = jnp.exp(scores - maximum)
    probability = powers / jnp.sum(powers, axis=1, keepdims=True)
    rounded_w = probability.astype(jnp.bfloat16)
    result_rows = jnp.dot(rounded_w, value_row_list, preferred_element_type=jnp.float32).astype(jnp.bfloat16)
    row_dot = jnp.sum(upstream.astype(jnp.float32) * result_rows.astype(jnp.float32), axis=1)
    prob_grad = jnp.dot(upstream, value_row_list.T, preferred_element_type=jnp.float32)
    score_grad = (probability * (prob_grad - row_dot[:, None])).astype(jnp.bfloat16)
    query_gradient = (jnp.dot(score_grad, key_rows, preferred_element_type=jnp.float32) * scaling).astype(jnp.bfloat16)
    value_gradient = jnp.dot(rounded_w.T, upstream, preferred_element_type=jnp.float32).astype(jnp.bfloat16)
    return result_rows, query_gradient, value_gradient


def split_heads(matrix):
    return matrix.reshape(LENGTH, HEAD_COUNT, HEAD_SIZE).transpose(1, 0, 2)


def merge_heads(stacked):
    return stacked.transpose(1, 0, 2).reshape(LENGTH, HEAD_COUNT * HEAD_SIZE)


def reference(hidden, frozen_queries, frozen_keys, frozen_values, document_length_list, query_down_weight, query_up_weight, value_down_weight, value_up_weight, output_gradient):
    def one_batch(inputs):
        token_total, query_plain, k_base, value_plain, doc_sizes, upstream = inputs
        query_reduced = jnp.dot(token_total, query_down_weight, preferred_element_type=jnp.float32).astype(jnp.bfloat16)
        value_reduced = jnp.dot(token_total, value_down_weight, preferred_element_type=jnp.float32).astype(jnp.bfloat16)
        query_tensor = (query_plain.astype(jnp.float32) + ADAPTER_SCALE * jnp.dot(query_reduced, query_up_weight, preferred_element_type=jnp.float32)).astype(jnp.bfloat16)
        value_tensor = (value_plain.astype(jnp.float32) + ADAPTER_SCALE * jnp.dot(value_reduced, value_up_weight, preferred_element_type=jnp.float32)).astype(jnp.bfloat16)
        documents = document_ids(doc_sizes, LENGTH)

        def per_head(operands):
            return head_pass(operands, documents)

        result_h, query_h, value_h = lax.map(per_head, (split_heads(query_tensor), split_heads(k_base), split_heads(value_tensor), split_heads(upstream)))
        attended = merge_heads(result_h)
        query_gradient = merge_heads(query_h)
        value_gradient = merge_heads(value_h)
        query_return = (ADAPTER_SCALE * jnp.dot(query_gradient, query_up_weight.T, preferred_element_type=jnp.float32)).astype(jnp.bfloat16)
        value_return = (ADAPTER_SCALE * jnp.dot(value_gradient, value_up_weight.T, preferred_element_type=jnp.float32)).astype(jnp.bfloat16)
        grad_a_q = jnp.dot(token_total.T, query_return, preferred_element_type=jnp.float32)
        grad_a_v = jnp.dot(token_total.T, value_return, preferred_element_type=jnp.float32)
        query_up_gradient = ADAPTER_SCALE * jnp.dot(query_reduced.T, query_gradient, preferred_element_type=jnp.float32)
        value_up_gradient = ADAPTER_SCALE * jnp.dot(value_reduced.T, value_gradient, preferred_element_type=jnp.float32)
        return attended, grad_a_q, query_up_gradient, grad_a_v, value_up_gradient

    attended, sum_aq, sum_bq, sum_av, sum_bv = lax.map(one_batch, (hidden, frozen_queries, frozen_keys, frozen_values, document_length_list, output_gradient))
    return attended, jnp.sum(sum_aq, axis=0), jnp.sum(sum_bq, axis=0), jnp.sum(sum_av, axis=0), jnp.sum(sum_bv, axis=0)
```

```python
import functools

import jax
import jax.numpy as jnp
from jax import lax
from jax.experimental import pallas as pl
from jax.experimental.pallas import tpu as pltpu
from jax.sharding import Mesh
from jax.sharding import PartitionSpec as P

HEAD_COUNT = 16
HEAD_SIZE = 128
RANK = 64
NDOC = 8
TILE = 256
MAX_TILES = 5
ADAPTER_SCALE = 2.0
NEG_FILL = -1e30
SCALING = HEAD_SIZE ** (-0.5)
LOG2_E = 1.4426950408889634

DOWN_ROWS, DOWN_COLS = 16, 256
UP_ROWS, UP_COLS = 16, 128

DP = ("x", "z")
SEQ = ("y", "core")
ALL = ("x", "z", "y", "core")
NT = (((1,), (1,)), ((), ()))


def dot(a, b):
    return jnp.dot(a, b, preferred_element_type=jnp.float32)


def dot_nt(a, b):
    return lax.dot_general(a, b, NT, preferred_element_type=jnp.float32)


def pack_kernel(hidden, wq_down, wv_down, fq, fk, fv, grad, wq_up, wv_up, out, low):
    width = fq.shape[1]

    @pl.when(pl.program_id(0) == 0)
    def _():
        low[:, :RANK] = dot_nt(hidden[...], wq_down[...]).astype(jnp.bfloat16)
        low[:, RANK:] = dot_nt(hidden[...], wv_down[...]).astype(jnp.bfloat16)

    q_add = ADAPTER_SCALE * dot(low[:, :RANK], wq_up[...])
    v_add = ADAPTER_SCALE * dot(low[:, RANK:], wv_up[...])
    out[0, :, 0:width] = (fq[...].astype(jnp.float32) + q_add).astype(jnp.bfloat16)
    out[0, :, width : 2 * width] = fk[...]
    out[0, :, 2 * width : 3 * width] = (fv[...].astype(jnp.float32) + v_add).astype(jnp.bfloat16)
    out[0, :, 3 * width : 4 * width] = grad[...]
    out[0, :, 4 * width :] = low[...]


def pack(hidden, wq_down_t, wv_down_t, fq, fk, fv, grad, wq_up, wv_up, seq_size):
    rows, model = hidden.shape
    width = fq.shape[1] // seq_size
    whole = lambda s: pl.BlockSpec(s, lambda d: (0, 0))
    column = lambda r: pl.BlockSpec((r, width), lambda d: (0, d))
    packed = 4 * width + 2 * RANK
    return pl.pallas_call(
        pack_kernel,
        grid=(seq_size,),
        in_specs=[
            whole((rows, model)),
            whole((RANK, model)),
            whole((RANK, model)),
            column(rows),
            column(rows),
            column(rows),
            column(rows),
            column(RANK),
            column(RANK),
        ],
        out_specs=pl.BlockSpec((1, rows, packed), lambda d: (d, 0, 0)),
        out_shape=jax.ShapeDtypeStruct((seq_size, rows, packed), jnp.bfloat16),
        scratch_shapes=[pltpu.VMEM((rows, 2 * RANK), jnp.bfloat16)],
        compiler_params=pltpu.CompilerParams(vmem_limit_bytes=40 << 20),
        name="pack",
    )(hidden, wq_down_t, wv_down_t, fq, fk, fv, grad, wq_up, wv_up)


def attention_kernel(
    meta, packed, wq_up, wv_up, out, back, up, q_t, k_t, v_t, g_t, dq_t, dv, dv_t
):
    length = packed.shape[0]
    heads = out.shape[1] // HEAD_SIZE
    width = heads * HEAD_SIZE
    blocks = length // TILE

    def columns(which, head):
        begin = which * width + head * HEAD_SIZE
        return slice(begin, begin + HEAD_SIZE)

    for head in range(heads):
        q_t[...] = packed[:, columns(0, head)].T
        k_t[...] = packed[:, columns(1, head)].T
        v_t[...] = packed[:, columns(2, head)].T
        g_t[...] = packed[:, columns(3, head)].T
        dv[...] = jnp.zeros_like(dv)

        def block(index, _, head=head):
            row0 = pl.multiple_of(index * TILE, TILE)
            q_rows = pl.ds(row0, TILE)
            position = row0 + lax.broadcasted_iota(jnp.int32, (1, TILE), 1)
            begin = jnp.zeros((1, TILE), jnp.int32)
            first = jnp.int32(0)
            end = jnp.int32(0)
            for doc in range(NDOC):
                end = end + meta[doc]
                begin = jnp.where(position >= end, end, begin)
                first = jnp.where(row0 >= end, end, first)
            first_tile = lax.div(first, TILE)
            tiles = index - first_tile + 1

            def body(count):
                key0 = pl.multiple_of((index + 1 - count) * TILE, TILE)
                k_rows = pl.ds(key0, count * TILE)
                keys = packed[k_rows, columns(1, head)]
                values = packed[k_rows, columns(2, head)]
                scores = dot(keys, q_t[:, q_rows])
                key_position = key0 + lax.broadcasted_iota(jnp.int32, (count * TILE, TILE), 0)
                allowed = (key_position >= begin) & (key_position <= position)
                scores = jnp.where(allowed, scores, NEG_FILL)
                maximum = jnp.max(scores, axis=0, keepdims=True)
                powers = jnp.exp2((scores - maximum) * (SCALING * LOG2_E))
                inverse = 1.0 / jnp.sum(powers, axis=0, keepdims=True)
                rounded = powers.astype(jnp.bfloat16)
                result = (dot(v_t[:, k_rows], rounded) * inverse).astype(jnp.bfloat16)
                g_block = g_t[:, q_rows]
                g_wide = g_block.astype(jnp.float32)
                row_dot = jnp.sum(g_wide * result.astype(jnp.float32), axis=0, keepdims=True)
                prob_grad = dot(values, g_block)
                score_grad = (powers * (prob_grad - row_dot)).astype(jnp.bfloat16)
                query_grad = dot(k_t[:, k_rows], score_grad) * (inverse * SCALING)
                dq_t[head * HEAD_SIZE : (head + 1) * HEAD_SIZE, q_rows] = query_grad.astype(
                    jnp.bfloat16
                )
                out[q_rows, head * HEAD_SIZE : (head + 1) * HEAD_SIZE] = result.T
                g_scaled = (g_wide * inverse).astype(jnp.bfloat16).T
                dv[k_rows, :] += dot(rounded, g_scaled)

            for count in range(1, min(MAX_TILES, blocks) + 1):
                pl.when(tiles == count)(functools.partial(body, count))
            return 0

        lax.fori_loop(0, blocks, block, 0)
        dv_t[head * HEAD_SIZE : (head + 1) * HEAD_SIZE, :] = dv[...].astype(jnp.bfloat16).T

    low = packed[:, 4 * width :]
    seq_size = back.shape[0]
    rows = back.shape[2]
    for part, (grads, weight) in enumerate(((dq_t, wq_up), (dv_t, wv_up))):
        returned = (ADAPTER_SCALE * dot(weight[...], grads[...])).astype(jnp.bfloat16)
        for device in range(seq_size):
            back[device, part * RANK : (part + 1) * RANK, :] = returned[
                :, device * rows : (device + 1) * rows
            ]
        up_t = dot(grads[...], low) * ADAPTER_SCALE
        up_part = up_t.T[part * RANK : (part + 1) * RANK, :].astype(jnp.bfloat16)
        across = width // UP_COLS
        for row in range(RANK // UP_ROWS):
            for column in range(across):
                up[(part * (RANK // UP_ROWS) + row) * across + column] = up_part[
                    row * UP_ROWS : (row + 1) * UP_ROWS, column * UP_COLS : (column + 1) * UP_COLS
                ]


def attention(meta, packed, wq_up, wv_up, seq_size):
    length = packed.shape[0]
    width = (packed.shape[1] - 2 * RANK) // 4
    rows = length // seq_size
    column = pl.BlockSpec((RANK, width), lambda i, meta: (0, meta[NDOC]))
    whole = lambda *s: pl.BlockSpec(s, lambda i, meta: (0,) * len(s))
    head_t = pltpu.VMEM((HEAD_SIZE, length), jnp.bfloat16)
    return pl.pallas_call(
        attention_kernel,
        grid_spec=pltpu.PrefetchScalarGridSpec(
            num_scalar_prefetch=1,
            grid=(1,),
            in_specs=[whole(*packed.shape), column, column],
            out_specs=[
                whole(length, width),
                whole(seq_size, 2 * RANK, rows),
                whole(2 * RANK * width // (UP_ROWS * UP_COLS), UP_ROWS, UP_COLS),
            ],
            scratch_shapes=[
                head_t,
                head_t,
                head_t,
                head_t,
                pltpu.VMEM((width, length), jnp.bfloat16),
                pltpu.VMEM((length, HEAD_SIZE), jnp.float32),
                pltpu.VMEM((width, length), jnp.bfloat16),
            ],
        ),
        out_shape=[
            jax.ShapeDtypeStruct((length, width), jnp.bfloat16),
            jax.ShapeDtypeStruct((seq_size, 2 * RANK, rows), jnp.bfloat16),
            jax.ShapeDtypeStruct(
                (2 * RANK * width // (UP_ROWS * UP_COLS), UP_ROWS, UP_COLS), jnp.bfloat16
            ),
        ],
        compiler_params=pltpu.CompilerParams(vmem_limit_bytes=56 << 20),
        name="attention",
    )(meta, packed, wq_up, wv_up)


def down_kernel(parts, hidden, out):
    total = parts[0].astype(jnp.float32)
    for source in range(1, parts.shape[0]):
        total += parts[source].astype(jnp.float32)
    back = total.astype(jnp.bfloat16)
    grad = dot(back, hidden[...]).astype(out.dtype)
    for column in range(out.shape[0]):
        for row in range(out.shape[1]):
            out[column, row] = grad[
                row * DOWN_ROWS : (row + 1) * DOWN_ROWS,
                column * DOWN_COLS : (column + 1) * DOWN_COLS,
            ]


def down_gradient(parts, hidden):
    seq_size, columns, rows = parts.shape
    model = hidden.shape[1]
    step = 1024
    tiles = (step // DOWN_COLS, columns // DOWN_ROWS, DOWN_ROWS, DOWN_COLS)
    return pl.pallas_call(
        down_kernel,
        grid=(model // step,),
        in_specs=[
            pl.BlockSpec((seq_size, columns, rows), lambda i: (0, 0, 0)),
            pl.BlockSpec((rows, step), lambda i: (0, i)),
        ],
        out_specs=pl.BlockSpec(tiles, lambda i: (i, 0, 0, 0)),
        out_shape=jax.ShapeDtypeStruct((model // DOWN_COLS,) + tiles[1:], jnp.bfloat16),
        compiler_params=pltpu.CompilerParams(vmem_limit_bytes=40 << 20),
        name="down_gradient",
    )(parts, hidden)


def place_kernel(parts, grad_a_q, up_q, grad_a_v, up_v):
    dp_size, seq_size = parts.shape[:2]
    half = RANK // DOWN_ROWS
    for p in range(dp_size):
        for s in range(seq_size):
            target = (grad_a_q, grad_a_v)[s // half]
            target[
                s % half * DOWN_ROWS : (s % half + 1) * DOWN_ROWS,
                p * DOWN_COLS : (p + 1) * DOWN_COLS,
            ] = parts[p, s, :, :DOWN_COLS].astype(jnp.float32)
            row, column = p // 2, p % 2
            target = (up_q, up_v)[row // half]
            target[
                row % half * UP_ROWS : (row % half + 1) * UP_ROWS,
                (2 * s + column) * UP_COLS : (2 * s + column + 1) * UP_COLS,
            ] = parts[p, s, :, DOWN_COLS:].astype(jnp.float32)


def place(parts, model, width):
    vmem = pl.BlockSpec(memory_space=pltpu.VMEM)
    shapes = [(RANK, model), (RANK, width), (RANK, model), (RANK, width)]
    return pl.pallas_call(
        place_kernel,
        in_specs=[vmem],
        out_specs=[vmem] * 4,
        out_shape=[jax.ShapeDtypeStruct(shape, jnp.float32) for shape in shapes],
        compiler_params=pltpu.CompilerParams(vmem_limit_bytes=40 << 20),
        name="place",
    )(parts)


def swap(x, axes):
    return lax.all_to_all(x, axes, 0, 0, tiled=True)


def spread(x, axes, size):
    return swap(jnp.broadcast_to(x[None], (size,) + x.shape), axes)


def per_device(
    sizes,
    hidden,
    frozen_queries,
    frozen_keys,
    frozen_values,
    document_length_list,
    query_down_weight,
    query_up_weight,
    value_down_weight,
    value_up_weight,
    output_gradient,
):
    dp_size, seq_size = sizes
    packed = pack(
        hidden[0],
        query_down_weight.T,
        value_down_weight.T,
        frozen_queries[0],
        frozen_keys[0],
        frozen_values[0],
        output_gradient[0],
        query_up_weight,
        value_up_weight,
        seq_size,
    )
    rows = packed.shape[1]
    received = swap(packed, SEQ)
    received = received.reshape(seq_size * rows, packed.shape[2])
    me = lax.axis_index(SEQ).astype(jnp.int32)
    meta = jnp.concatenate([document_length_list[0], me[None]])
    result, back, up = attention(meta, received, query_up_weight, value_up_weight, seq_size)
    width = result.shape[1]

    back = swap(back, SEQ)
    down = down_gradient(back, hidden[0])
    attended = swap(result.reshape(seq_size, rows, width), SEQ)
    attended = attended.transpose(1, 0, 2).reshape(1, rows, seq_size * width)

    up = swap(up, DP)
    up = jnp.sum(up.astype(jnp.float32), axis=0).astype(jnp.bfloat16)
    model = hidden.shape[2]
    devices = dp_size * seq_size
    down = swap(down.reshape(devices, DOWN_ROWS, DOWN_COLS), ALL)
    down = jnp.sum(down.astype(jnp.float32), axis=0).astype(jnp.bfloat16)
    both = jnp.concatenate([down, up], axis=1)
    both = spread(both, ALL, devices)
    both = both.reshape(dp_size, seq_size, DOWN_ROWS, DOWN_COLS + UP_COLS)
    grad_a_q, up_q, grad_a_v, up_v = place(both, model, seq_size * width)
    return attended, grad_a_q.T, up_q, grad_a_v.T, up_v


def solution(mesh):
    dp_size, seq_size = mesh.shape["dp"], mesh.shape["seq"]
    fine = Mesh(mesh.devices.reshape(4, 4, 4, 2), ALL)
    rows = P(DP, SEQ, None)
    in_specs = (rows, rows, rows, rows, P(DP, None), P(), P(), P(), P(), rows)
    out_specs = (rows, P(), P(), P(), P())
    return jax.shard_map(
        functools.partial(per_device, (dp_size, seq_size)),
        mesh=fine,
        in_specs=in_specs,
        out_specs=out_specs,
        check_vma=False,
    )
```

```python
import functools

import jax
import jax.numpy as jnp
from jax import lax
from jax.experimental import pallas as pl
from jax.experimental.pallas import tpu as pltpu
from jax.sharding import Mesh
from jax.sharding import PartitionSpec as P

HEAD_COUNT = 16
HEAD_SIZE = 128
RANK = 64
NDOC = 8
TILE = 256
MAX_TILES = 5
ADAPTER_SCALE = 2.0
NEG_FILL = -1e30
SCALING = HEAD_SIZE ** (-0.5)
LOG2_E = 1.4426950408889634

SHARE_ROWS = 16
DOWN_COLS = 256
UP_COLS = 32

DP = ("x", "z")
SEQ = ("y", "core")
PLANE = ("x", "z", "y")
ALL = ("x", "z", "y", "core")
NT = (((1,), (1,)), ((), ()))


def dot(a, b):
    return jnp.dot(a, b, preferred_element_type=jnp.float32)


def dot_nt(a, b):
    return lax.dot_general(a, b, NT, preferred_element_type=jnp.float32)


def pack_kernel(hidden, wq_down, wv_down, fq, fk, fv, grad, wq_up, wv_up, out, low):
    width = fq.shape[1]

    @pl.when(pl.program_id(0) == 0)
    def _():
        low[:, :RANK] = dot_nt(hidden[...], wq_down[...]).astype(jnp.bfloat16)
        low[:, RANK:] = dot_nt(hidden[...], wv_down[...]).astype(jnp.bfloat16)

    q_add = ADAPTER_SCALE * dot(low[:, :RANK], wq_up[...])
    v_add = ADAPTER_SCALE * dot(low[:, RANK:], wv_up[...])
    out[0, :, 0:width] = (fq[...].astype(jnp.float32) + q_add).astype(jnp.bfloat16)
    out[0, :, width : 2 * width] = fk[...]
    out[0, :, 2 * width : 3 * width] = (fv[...].astype(jnp.float32) + v_add).astype(jnp.bfloat16)
    out[0, :, 3 * width : 4 * width] = grad[...]
    out[0, :, 4 * width :] = low[...]


def pack(hidden, wq_down_t, wv_down_t, fq, fk, fv, grad, wq_up, wv_up, seq_size):
    rows, model = hidden.shape
    width = fq.shape[1] // seq_size
    whole = lambda s: pl.BlockSpec(s, lambda d: (0, 0))
    column = lambda r: pl.BlockSpec((r, width), lambda d: (0, d))
    packed = 4 * width + 2 * RANK
    return pl.pallas_call(
        pack_kernel,
        grid=(seq_size,),
        in_specs=[
            whole((rows, model)),
            whole((RANK, model)),
            whole((RANK, model)),
            column(rows),
            column(rows),
            column(rows),
            column(rows),
            column(RANK),
            column(RANK),
        ],
        out_specs=pl.BlockSpec((1, rows, packed), lambda d: (d, 0, 0)),
        out_shape=jax.ShapeDtypeStruct((seq_size, rows, packed), jnp.bfloat16),
        scratch_shapes=[pltpu.VMEM((rows, 2 * RANK), jnp.bfloat16)],
        compiler_params=pltpu.CompilerParams(vmem_limit_bytes=60 << 20),
        name="pack",
    )(hidden, wq_down_t, wv_down_t, fq, fk, fv, grad, wq_up, wv_up)


def attention_kernel(
    meta, packed, wq_up, wv_up, out, back_0, back_1, back_2, back_3, up,
    q_t, k_t, v_t, g_t, dq_t, dv, dv_t, returned,
):
    length = packed.shape[0]
    heads = out.shape[1] // HEAD_SIZE
    width = heads * HEAD_SIZE
    blocks = length // TILE
    chip = meta[NDOC]
    span = [slice(head * HEAD_SIZE, (head + 1) * HEAD_SIZE) for head in range(heads)]

    def columns(which, head):
        begin = which * width + head * HEAD_SIZE
        return slice(begin, begin + HEAD_SIZE)

    for head in range(heads):
        q_t[span[head], :] = packed[:, columns(0, head)].T
        k_t[span[head], :] = packed[:, columns(1, head)].T
        v_t[span[head], :] = packed[:, columns(2, head)].T
        g_t[span[head], :] = packed[:, columns(3, head)].T
    dv[...] = jnp.zeros_like(dv)

    def block(index, _):
        row0 = pl.multiple_of(index * TILE, TILE)
        q_rows = pl.ds(row0, TILE)
        position = row0 + lax.broadcasted_iota(jnp.int32, (1, TILE), 1)
        begin = jnp.zeros((1, TILE), jnp.int32)
        first = jnp.int32(0)
        end = jnp.int32(0)
        for doc in range(NDOC):
            end = end + meta[doc]
            begin = jnp.where(position >= end, end, begin)
            first = jnp.where(row0 >= end, end, first)
        tiles = index - lax.div(first, TILE) + 1

        def body(count):
            key0 = pl.multiple_of((index + 1 - count) * TILE, TILE)
            k_rows = pl.ds(key0, count * TILE)
            key_index = lax.broadcasted_iota(jnp.int32, (count * TILE, TILE), 0)
            in_document = key_index >= begin - key0
            causal = lax.broadcasted_iota(jnp.int32, (TILE, TILE), 0) <= (
                lax.broadcasted_iota(jnp.int32, (TILE, TILE), 1)
            )
            held = []
            for head in range(heads):
                scores = dot(packed[k_rows, columns(1, head)], q_t[span[head], q_rows])
                prob_grad = dot(packed[k_rows, columns(2, head)], g_t[span[head], q_rows])
                scores = jnp.where(in_document, scores, NEG_FILL)
                last = jnp.where(causal, scores[(count - 1) * TILE :], NEG_FILL)
                if count > 1:
                    scores = jnp.concatenate([scores[: (count - 1) * TILE], last], axis=0)
                else:
                    scores = last
                maximum = jnp.max(scores, axis=0, keepdims=True)
                powers = jnp.exp2((scores - maximum) * (SCALING * LOG2_E))
                inverse = 1.0 / jnp.sum(powers, axis=0, keepdims=True)
                held.append((prob_grad, powers.astype(jnp.bfloat16), inverse))
            for head in range(heads):
                prob_grad, rounded, inverse = held[head]
                result = (dot(v_t[span[head], k_rows], rounded) * inverse).astype(jnp.bfloat16)
                g_wide = g_t[span[head], q_rows].astype(jnp.float32)
                row_dot = jnp.sum(g_wide * result.astype(jnp.float32), axis=0, keepdims=True)
                score_grad = rounded * (prob_grad - row_dot).astype(jnp.bfloat16)
                query_grad = dot(k_t[span[head], k_rows], score_grad) * (inverse * SCALING)
                dq_t[span[head], q_rows] = query_grad.astype(jnp.bfloat16)
                out[q_rows, span[head]] = result.T
                g_scaled = (g_wide * inverse).astype(jnp.bfloat16).T
                dv[head, k_rows, :] += dot(rounded, g_scaled)

        for count in range(1, min(MAX_TILES, blocks) + 1):
            pl.when(tiles == count)(functools.partial(body, count))
        return 0

    lax.fori_loop(0, blocks, block, 0)
    for head in range(heads):
        dv_t[span[head], :] = dv[head].astype(jnp.bfloat16).T

    for part, (grads, weight) in enumerate(((dq_t, wq_up), (dv_t, wv_up))):
        returned[part * RANK : (part + 1) * RANK, :] = (
            ADAPTER_SCALE * dot(weight[...], grads[...])
        ).astype(jnp.bfloat16)
    backs = (back_0, back_1, back_2, back_3)
    rows = back_0.shape[2]
    for step in range(len(backs)):
        target = lax.rem(chip + step, len(backs))
        for core in range(2):
            begin = pl.multiple_of((target * 2 + core) * rows, rows)
            backs[step][core] = returned[:, pl.ds(begin, rows)]

    low = packed[:, 4 * width :]
    lane = lax.broadcasted_iota(jnp.int32, (width, up.shape[1]), 1)
    source = lax.broadcasted_iota(jnp.int32, (width, up.shape[1]), 0)
    mine = (source == (lane // 128) * UP_COLS + lane % UP_COLS) & (
        (lane % 128) // UP_COLS == chip
    )
    mine = jnp.where(mine, 1.0, 0.0).astype(jnp.bfloat16)
    for part, grads in enumerate((dq_t, dv_t)):
        up_part = (dot(grads[...], low) * ADAPTER_SCALE).T[part * RANK : (part + 1) * RANK, :]
        up[part * RANK : (part + 1) * RANK, :] = dot(up_part.astype(jnp.bfloat16), mine).astype(
            jnp.bfloat16
        )


VMEM = pl.BlockSpec(memory_space=pltpu.VMEM)
SMEM = pl.BlockSpec(memory_space=pltpu.SMEM)


def attention(meta, packed, wq_up, wv_up, seq_size):
    length = packed.shape[0]
    width = (packed.shape[1] - 2 * RANK) // 4
    rows = length // seq_size
    heads = width // HEAD_SIZE
    chips = seq_size // 2
    wide_t = pltpu.VMEM((width, length), jnp.bfloat16)
    back = jax.ShapeDtypeStruct((2, 2 * RANK, rows), jnp.bfloat16)
    return pl.pallas_call(
        attention_kernel,
        in_specs=[SMEM, VMEM, VMEM, VMEM],
        out_specs=[VMEM] * (2 + chips),
        scratch_shapes=[
            wide_t,
            wide_t,
            wide_t,
            wide_t,
            wide_t,
            pltpu.VMEM((heads, length, HEAD_SIZE), jnp.float32),
            wide_t,
            pltpu.VMEM((2 * RANK, length), jnp.bfloat16),
        ],
        out_shape=[jax.ShapeDtypeStruct((length, width), jnp.bfloat16)]
        + [back] * chips
        + [jax.ShapeDtypeStruct((2 * RANK, width // UP_COLS * 128), jnp.bfloat16)],
        compiler_params=pltpu.CompilerParams(vmem_limit_bytes=40 << 20),
        name="attention",
    )(meta, packed, wq_up, wv_up)


def chips_kernel(part_0, part_1, part_2, part_3, out):
    total = part_0[...].astype(jnp.float32)
    for part in (part_1, part_2, part_3):
        total += part[...].astype(jnp.float32)
    out[...] = total.astype(out.dtype)


def sum_chips(parts):
    return pl.pallas_call(
        chips_kernel,
        in_specs=[VMEM] * len(parts),
        out_specs=VMEM,
        out_shape=jax.ShapeDtypeStruct(parts[0].shape, parts[0].dtype),
        name="sum_chips",
    )(*parts)


def down_kernel(core, own, other, hidden, hidden_other, up, out):
    total = (own[...].astype(jnp.float32) + other[...].astype(jnp.float32)).astype(jnp.bfloat16)
    first = core[0] == 0
    here = jnp.where(first, total[0], total[1])
    there = jnp.where(first, total[1], total[0])
    grad = (dot(here, hidden[...]) + dot(there, hidden_other[...])).astype(out.dtype)
    for row in range(out.shape[0]):
        across = slice(row * SHARE_ROWS, (row + 1) * SHARE_ROWS)
        for column in range(out.shape[1]):
            out[row, column, :, :DOWN_COLS] = grad[
                across, column * DOWN_COLS : (column + 1) * DOWN_COLS
            ]
            out[row, column, :, DOWN_COLS:] = up[across, column * 128 : (column + 1) * 128]


def down_gradient(core, own, other, hidden, hidden_other, up):
    rows, half = hidden_other.shape
    steps = 4
    step = half // steps
    columns = half // DOWN_COLS
    across = 2 * RANK // SHARE_ROWS
    return pl.pallas_call(
        down_kernel,
        grid_spec=pltpu.PrefetchScalarGridSpec(
            num_scalar_prefetch=1,
            grid=(steps,),
            in_specs=[
                pl.BlockSpec(own.shape, lambda i, core: (0, 0, 0)),
                pl.BlockSpec(own.shape, lambda i, core: (0, 0, 0)),
                pl.BlockSpec((rows, step), lambda i, core: (0, core[0] * steps + i)),
                pl.BlockSpec((rows, step), lambda i, core: (0, i)),
                pl.BlockSpec((2 * RANK, columns // steps * 128), lambda i, core: (0, i)),
            ],
            out_specs=pl.BlockSpec(
                (across, columns // steps, SHARE_ROWS, DOWN_COLS + 128),
                lambda i, core: (0, i, 0, 0),
            ),
        ),
        out_shape=jax.ShapeDtypeStruct(
            (across, columns, SHARE_ROWS, DOWN_COLS + 128), jnp.bfloat16
        ),
        compiler_params=pltpu.CompilerParams(vmem_limit_bytes=24 << 20),
        name="down_gradient",
    )(core, own, other, hidden, hidden_other, up)


def share_kernel(parts, out):
    total = parts[0].astype(jnp.float32)
    for part in range(1, parts.shape[0]):
        total += parts[part].astype(jnp.float32)
    total = total.astype(out.dtype)
    for part in range(out.shape[0]):
        out[part] = total


def sum_share(parts):
    return pl.pallas_call(
        share_kernel,
        in_specs=[VMEM],
        out_specs=VMEM,
        out_shape=jax.ShapeDtypeStruct(parts.shape, parts.dtype),
        name="sum_share",
    )(parts)


def place_kernel(core, own, other, grad_a_q, up_q, grad_a_v, up_v, wide):
    half = own.shape[0] // 2
    columns = own.shape[1]
    for part, shares in enumerate((own, other)):
        which = core[0] if part == 0 else 1 - core[0]
        for row in range(own.shape[0]):
            across = slice(row % half * SHARE_ROWS, (row % half + 1) * SHARE_ROWS)
            target = (grad_a_q, grad_a_v)[row // half]
            for column in range(columns):
                begin = pl.multiple_of((which * columns + column) * DOWN_COLS, DOWN_COLS)
                target[across, pl.ds(begin, DOWN_COLS)] = shares[
                    row, column, :, :DOWN_COLS
                ].astype(jnp.float32)
                wide[
                    row * SHARE_ROWS : (row + 1) * SHARE_ROWS, column * 128 : (column + 1) * 128
                ] = shares[row, column, :, DOWN_COLS:]
        width = columns * UP_COLS
        source = lax.broadcasted_iota(jnp.int32, (columns * 128, width), 0)
        lane = lax.broadcasted_iota(jnp.int32, (columns * 128, width), 1)
        lane = (lane // UP_COLS) * 128 + lane % UP_COLS
        for chip in range(128 // UP_COLS):
            pick = jnp.where(source == lane + chip * UP_COLS, 1.0, 0.0).astype(jnp.bfloat16)
            picked = dot(wide[...], pick)
            begin = pl.multiple_of((2 * chip + which) * width, width)
            up_q[:, pl.ds(begin, width)] = picked[:RANK]
            up_v[:, pl.ds(begin, width)] = picked[RANK:]


def place(core, own, other, model, width):
    shapes = [(RANK, model), (RANK, width), (RANK, model), (RANK, width)]
    return pl.pallas_call(
        place_kernel,
        in_specs=[SMEM, VMEM, VMEM],
        out_specs=[VMEM] * 4,
        out_shape=[jax.ShapeDtypeStruct(shape, jnp.float32) for shape in shapes],
        scratch_shapes=[pltpu.VMEM((2 * RANK, own.shape[1] * 128), jnp.bfloat16)],
        compiler_params=pltpu.CompilerParams(vmem_limit_bytes=30 << 20),
        name="place",
    )(core, own, other)


def swap(x, axes):
    return lax.all_to_all(x, axes, 0, 0, tiled=True)


def to_other_core(x):
    return lax.ppermute(x, "core", [(0, 1), (1, 0)])


def per_device(
    sizes,
    hidden,
    frozen_queries,
    frozen_keys,
    frozen_values,
    document_length_list,
    query_down_weight,
    query_up_weight,
    value_down_weight,
    value_up_weight,
    output_gradient,
):
    dp_size, seq_size = sizes
    chips = seq_size // 2
    rows, model = hidden.shape[1:]
    half = model // 2
    chip = lax.axis_index("y").astype(jnp.int32)
    core = lax.axis_index("core").astype(jnp.int32)
    packed = pack(
        hidden[0],
        query_down_weight.T,
        value_down_weight.T,
        frozen_queries[0],
        frozen_keys[0],
        frozen_values[0],
        output_gradient[0],
        query_up_weight,
        value_up_weight,
        seq_size,
    )
    received = swap(packed, SEQ).reshape(seq_size * rows, packed.shape[2])
    hidden_other = to_other_core(
        lax.dynamic_slice(hidden[0], (0, (1 - core) * half), (rows, half))
    )
    width = frozen_queries.shape[2] // seq_size
    own_columns = (0, (chip * 2 + core) * width)
    wq_up = lax.dynamic_slice(query_up_weight, own_columns, (RANK, width))
    wv_up = lax.dynamic_slice(value_up_weight, own_columns, (RANK, width))
    meta = jnp.concatenate([document_length_list[0], chip[None]])
    result, *backs, up = attention(meta, received, wq_up, wv_up, seq_size)

    arrived = [backs[0]] + [
        lax.ppermute(backs[step], "y", [(c, (c + step) % chips) for c in range(chips)])
        for step in range(1, chips)
    ]
    back = sum_chips(arrived)
    back_other = to_other_core(back)
    result, back_other = lax.optimization_barrier((result, back_other))
    down = down_gradient(core[None], back, back_other, hidden[0], hidden_other, up)
    attended = swap(result.reshape(seq_size, rows, width), SEQ)
    attended = attended.transpose(1, 0, 2).reshape(1, rows, seq_size * width)

    shares = swap(down.reshape((-1,) + down.shape[2:]), PLANE)
    shares = swap(sum_share(shares), PLANE).reshape(down.shape)
    shares_other = to_other_core(shares)
    grad_a_q, up_q, grad_a_v, up_v = place(
        core[None], shares, shares_other, model, seq_size * width
    )
    return attended, grad_a_q.T, up_q, grad_a_v.T, up_v


def solution(mesh):
    dp_size, seq_size = mesh.shape["dp"], mesh.shape["seq"]
    fine = Mesh(mesh.devices.reshape(4, 4, 4, 2), ALL)
    rows = P(DP, SEQ, None)
    in_specs = (rows, rows, rows, rows, P(DP, None), P(), P(), P(), P(), rows)
    out_specs = (rows, P(), P(), P(), P())
    return jax.shard_map(
        functools.partial(per_device, (dp_size, seq_size)),
        mesh=fine,
        in_specs=in_specs,
        out_specs=out_specs,
        check_vma=False,
    )
```

```python
import functools

import jax
import jax.numpy as jnp
from jax import lax
from jax.experimental import pallas as pl
from jax.experimental.pallas import tpu as pltpu
from jax.sharding import Mesh
from jax.sharding import PartitionSpec as P

HEAD_COUNT = 16
HEAD_SIZE = 128
RANK = 64
NDOC = 8
TILE = 256
MAX_TILES = 5
ADAPTER_SCALE = 2.0
NEG_FILL = -1e30
SCALING = HEAD_SIZE ** (-0.5)
LOG2_E = 1.4426950408889634

SHARE_ROWS = 16
DOWN_COLS = 256
UP_COLS = 32

DP = ("x", "z")
SEQ = ("y", "core")
PLANE = ("x", "z", "y")
ALL = ("x", "z", "y", "core")
NT = (((1,), (1,)), ((), ()))


def dot(a, b):
    return jnp.dot(a, b, preferred_element_type=jnp.float32)


def dot_nt(a, b):
    return lax.dot_general(a, b, NT, preferred_element_type=jnp.float32)


HIDDEN_PARTS = 4


def pack_kernel(
    hidden, wq_down, wv_down, fq, fk, fv, grad, wq_up, wv_up, out, low,
    hidden_v, wq_down_v, wv_down_v, fq_v, fv_v, wq_up_v, wv_up_v, q_v, v_v, low_v,
    down_sems, hidden_sems, row_sems, through_sems, out_sems, low_sem,
):
    devices, rows, packed = out.shape
    width = packed // 4
    model = hidden.shape[1]
    step = model // HIDDEN_PARTS

    def part(index):
        return pl.ds(index * step, step)

    def columns(index):
        return pl.ds(index * width, width)

    downs = [
        pltpu.make_async_copy(wq_down, wq_down_v, down_sems.at[0]),
        pltpu.make_async_copy(wv_down, wv_down_v, down_sems.at[1]),
    ]
    hiddens = [
        pltpu.make_async_copy(
            hidden.at[:, part(index)], hidden_v.at[:, part(index)], hidden_sems.at[index]
        )
        for index in range(HIDDEN_PARTS)
    ]
    whole = [
        pltpu.make_async_copy(wq_up, wq_up_v, row_sems.at[0]),
        pltpu.make_async_copy(fq, fq_v, row_sems.at[1]),
        pltpu.make_async_copy(wv_up, wv_up_v, row_sems.at[2]),
        pltpu.make_async_copy(fv, fv_v, row_sems.at[3]),
    ]
    through = []
    for device in range(devices):
        for which, source in ((1, fk), (3, grad)):
            through.append(
                pltpu.make_async_copy(
                    source.at[:, columns(device)],
                    out.at[device, :, columns(which)],
                    through_sems.at[len(through)],
                )
            )
    for copy in downs + hiddens + whole + through:
        copy.start()

    for copy in downs:
        copy.wait()
    low_q = jnp.zeros((rows, RANK), jnp.float32)
    low_v_ = jnp.zeros((rows, RANK), jnp.float32)
    for index in range(HIDDEN_PARTS):
        hiddens[index].wait()
        low_q += dot_nt(hidden_v[:, part(index)], wq_down_v[:, part(index)])
        low_v_ += dot_nt(hidden_v[:, part(index)], wv_down_v[:, part(index)])
    low_v[:, :RANK] = low_q.astype(jnp.bfloat16)
    low_v[:, RANK:] = low_v_.astype(jnp.bfloat16)
    low_copy = pltpu.make_async_copy(low_v, low, low_sem)
    low_copy.start()

    outs = []
    for which, (frozen, weight, ready, begin) in enumerate(
        ((fq_v, wq_up_v, q_v, 0), (fv_v, wv_up_v, v_v, RANK))
    ):
        whole[2 * which].wait()
        whole[2 * which + 1].wait()
        for device in range(devices):
            at = slice(device * width, (device + 1) * width)
            added = ADAPTER_SCALE * dot(low_v[:, begin : begin + RANK], weight[:, at])
            ready[device] = (frozen[:, at].astype(jnp.float32) + added).astype(jnp.bfloat16)
            copy = pltpu.make_async_copy(
                ready.at[device],
                out.at[device, :, columns(2 * which)],
                out_sems.at[len(outs)],
            )
            copy.start()
            outs.append(copy)
    for copy in through + outs:
        copy.wait()
    low_copy.wait()


def pack(hidden, wq_down_t, wv_down_t, fq, fk, fv, grad, wq_up, wv_up, seq_size):
    rows, model = hidden.shape
    columns = fq.shape[1]
    width = columns // seq_size
    bf16 = jnp.bfloat16
    any_space = pl.BlockSpec(memory_space=pl.ANY)
    return pl.pallas_call(
        pack_kernel,
        in_specs=[any_space] * 9,
        out_specs=[any_space] * 2,
        out_shape=[
            jax.ShapeDtypeStruct((seq_size, rows, 4 * width), bf16),
            jax.ShapeDtypeStruct((rows, 2 * RANK), bf16),
        ],
        scratch_shapes=[
            pltpu.VMEM((rows, model), bf16),
            pltpu.VMEM((RANK, model), bf16),
            pltpu.VMEM((RANK, model), bf16),
            pltpu.VMEM((rows, columns), bf16),
            pltpu.VMEM((rows, columns), bf16),
            pltpu.VMEM((RANK, columns), bf16),
            pltpu.VMEM((RANK, columns), bf16),
            pltpu.VMEM((seq_size, rows, width), bf16),
            pltpu.VMEM((seq_size, rows, width), bf16),
            pltpu.VMEM((rows, 2 * RANK), bf16),
            pltpu.SemaphoreType.DMA((2,)),
            pltpu.SemaphoreType.DMA((HIDDEN_PARTS,)),
            pltpu.SemaphoreType.DMA((4,)),
            pltpu.SemaphoreType.DMA((2 * seq_size,)),
            pltpu.SemaphoreType.DMA((2 * seq_size,)),
            pltpu.SemaphoreType.DMA,
        ],
        compiler_params=pltpu.CompilerParams(vmem_limit_bytes=60 << 20),
        name="pack",
    )(hidden, wq_down_t, wv_down_t, fq, fk, fv, grad, wq_up, wv_up)


def attention_kernel(
    meta, packed, wq_up, wv_up, *refs
):
    out, back_0, back_1, back_2, back_3, dq_t, dv_t, q_t, k_t, v_t, g_t, dv, returned = refs[-13:]
    length = packed.shape[0]
    heads = out.shape[1] // HEAD_SIZE
    width = heads * HEAD_SIZE
    blocks = length // TILE
    chip = meta[NDOC]
    span = [slice(head * HEAD_SIZE, (head + 1) * HEAD_SIZE) for head in range(heads)]

    def columns(which, head):
        begin = which * width + head * HEAD_SIZE
        return slice(begin, begin + HEAD_SIZE)

    for head in range(heads):
        q_t[span[head], :] = packed[:, columns(0, head)].T
        k_t[span[head], :] = packed[:, columns(1, head)].T
        v_t[span[head], :] = packed[:, columns(2, head)].T
        g_t[span[head], :] = packed[:, columns(3, head)].T
    dv[...] = jnp.zeros_like(dv)

    def block(index, _):
        row0 = pl.multiple_of(index * TILE, TILE)
        q_rows = pl.ds(row0, TILE)
        position = row0 + lax.broadcasted_iota(jnp.int32, (1, TILE), 1)
        begin = jnp.zeros((1, TILE), jnp.int32)
        first = jnp.int32(0)
        end = jnp.int32(0)
        for doc in range(NDOC):
            end = end + meta[doc]
            begin = jnp.where(position >= end, end, begin)
            first = jnp.where(row0 >= end, end, first)
        tiles = index - lax.div(first, TILE) + 1

        def body(count):
            key0 = pl.multiple_of((index + 1 - count) * TILE, TILE)
            k_rows = pl.ds(key0, count * TILE)
            key_index = lax.broadcasted_iota(jnp.int32, (count * TILE, TILE), 0)
            in_document = key_index >= begin - key0
            causal = lax.broadcasted_iota(jnp.int32, (TILE, TILE), 0) <= (
                lax.broadcasted_iota(jnp.int32, (TILE, TILE), 1)
            )
            held = []
            for head in range(heads):
                scores = dot(packed[k_rows, columns(1, head)], q_t[span[head], q_rows])
                prob_grad = dot(packed[k_rows, columns(2, head)], g_t[span[head], q_rows])
                scores = jnp.where(in_document, scores, NEG_FILL)
                last = jnp.where(causal, scores[(count - 1) * TILE :], NEG_FILL)
                if count > 1:
                    scores = jnp.concatenate([scores[: (count - 1) * TILE], last], axis=0)
                else:
                    scores = last
                maximum = jnp.max(scores, axis=0, keepdims=True)
                powers = jnp.exp2((scores - maximum) * (SCALING * LOG2_E))
                inverse = 1.0 / jnp.sum(powers, axis=0, keepdims=True)
                held.append((prob_grad, powers.astype(jnp.bfloat16), inverse))
            for head in range(heads):
                prob_grad, rounded, inverse = held[head]
                result = (dot(v_t[span[head], k_rows], rounded) * inverse).astype(jnp.bfloat16)
                g_wide = g_t[span[head], q_rows].astype(jnp.float32)
                row_dot = jnp.sum(g_wide * result.astype(jnp.float32), axis=0, keepdims=True)
                score_grad = rounded * (prob_grad - row_dot).astype(jnp.bfloat16)
                query_grad = dot(k_t[span[head], k_rows], score_grad) * (inverse * SCALING)
                dq_t[span[head], q_rows] = query_grad.astype(jnp.bfloat16)
                out[q_rows, span[head]] = result.T
                g_scaled = (g_wide * inverse).astype(jnp.bfloat16).T
                dv[head, k_rows, :] += dot(rounded, g_scaled)

        for count in range(1, min(MAX_TILES, blocks) + 1):
            pl.when(tiles == count)(functools.partial(body, count))
        return 0

    lax.fori_loop(0, blocks, block, 0)
    for head in range(heads):
        dv_t[span[head], :] = dv[head].astype(jnp.bfloat16).T

    for part, (grads, weight) in enumerate(((dq_t, wq_up), (dv_t, wv_up))):
        returned[part * RANK : (part + 1) * RANK, :] = (
            ADAPTER_SCALE * dot(weight[...], grads[...])
        ).astype(jnp.bfloat16)
    backs = (back_0, back_1, back_2, back_3)
    rows = back_0.shape[2]
    for step in range(len(backs)):
        target = lax.rem(chip + step, len(backs))
        for core in range(2):
            begin = pl.multiple_of((target * 2 + core) * rows, rows)
            backs[step][core] = returned[:, pl.ds(begin, rows)]


VMEM = pl.BlockSpec(memory_space=pltpu.VMEM)
SMEM = pl.BlockSpec(memory_space=pltpu.SMEM)
ANY = pl.BlockSpec(memory_space=pl.ANY)


def attention(meta, packed, wq_up, wv_up, seq_size, after):
    length = packed.shape[0]
    width = packed.shape[1] // 4
    rows = length // seq_size
    heads = width // HEAD_SIZE
    chips = seq_size // 2
    wide_t = pltpu.VMEM((width, length), jnp.bfloat16)
    back = jax.ShapeDtypeStruct((2, 2 * RANK, rows), jnp.bfloat16)
    grad_t = jax.ShapeDtypeStruct((width, length), jnp.bfloat16)
    return pl.pallas_call(
        attention_kernel,
        in_specs=[SMEM, VMEM, VMEM, VMEM] + [ANY] * len(after),
        out_specs=[VMEM] * (3 + chips),
        scratch_shapes=[
            wide_t,
            wide_t,
            wide_t,
            wide_t,
            pltpu.VMEM((heads, length, HEAD_SIZE), jnp.float32),
            pltpu.VMEM((2 * RANK, length), jnp.bfloat16),
        ],
        out_shape=[jax.ShapeDtypeStruct((length, width), jnp.bfloat16)]
        + [back] * chips
        + [grad_t, grad_t],
        compiler_params=pltpu.CompilerParams(vmem_limit_bytes=40 << 20),
        cost_estimate=pl.CostEstimate(
            flops=8 << 30, bytes_accessed=16 << 20, transcendentals=4 << 20
        ),
        name="attention",
    )(meta, packed, wq_up, wv_up, *after)


def up_kernel(where, *refs):
    chip, core = where[0], where[1]
    *lows, dq_t, dv_t, up = refs
    steps = len(lows) // 2
    rows = lows[0].shape[0]
    width = dq_t.shape[0]
    lane = lax.broadcasted_iota(jnp.int32, (width, up.shape[1]), 1)
    source = lax.broadcasted_iota(jnp.int32, (width, up.shape[1]), 0)
    mine = (source == (lane // 128) * UP_COLS + lane % UP_COLS) & (
        (lane % 128) // UP_COLS == chip
    )
    mine = jnp.where(mine, 1.0, 0.0).astype(jnp.bfloat16)
    for part, grads in enumerate((dq_t, dv_t)):
        total = jnp.zeros((width, 2 * RANK), jnp.float32)
        for index, low in enumerate(lows):
            origin = lax.rem(chip + steps - index % steps, steps)
            holder = core if index < steps else 1 - core
            begin = pl.multiple_of((origin * 2 + holder) * rows, rows)
            total += dot(grads[:, pl.ds(begin, rows)], low[...])
        share = (total * ADAPTER_SCALE).T[part * RANK : (part + 1) * RANK, :]
        up[part * RANK : (part + 1) * RANK, :] = dot(share.astype(jnp.bfloat16), mine).astype(
            jnp.bfloat16
        )


def up_gradient(where, lows, dq_t, dv_t):
    width = dq_t.shape[0]
    return pl.pallas_call(
        up_kernel,
        in_specs=[SMEM] + [VMEM] * (len(lows) + 2),
        out_specs=VMEM,
        out_shape=jax.ShapeDtypeStruct((2 * RANK, width // UP_COLS * 128), jnp.bfloat16),
        compiler_params=pltpu.CompilerParams(vmem_limit_bytes=24 << 20),
        name="up_gradient",
    )(where, *lows, dq_t, dv_t)


def leaving_kernel(where, result, out):
    chip, core = where[0], where[1]
    chips, rows, _ = out.shape
    for step in range(chips):
        target = lax.rem(chip + step, chips)
        begin = pl.multiple_of((target * 2 + 1 - core) * rows, rows)
        out[step] = result[pl.ds(begin, rows), :]


def leaving(where, result, seq_size):
    length, width = result.shape
    shape = (seq_size // 2, length // seq_size, width)
    return pl.pallas_call(
        leaving_kernel,
        in_specs=[SMEM, VMEM],
        out_specs=VMEM,
        out_shape=jax.ShapeDtypeStruct(shape, result.dtype),
        name="leaving",
    )(where, result)


def join_kernel(where, result, other, *refs):
    chip, core = where[0], where[1]
    chips, rows, width = other.shape
    outs = refs[-chips:]
    here = pl.multiple_of(core * width, width)
    there = pl.multiple_of((1 - core) * width, width)
    for step in range(chips):
        target = lax.rem(chip + step, chips)
        begin = pl.multiple_of((target * 2 + core) * rows, rows)
        outs[step][:, pl.ds(here, width)] = result[pl.ds(begin, rows), :]
        outs[step][:, pl.ds(there, width)] = other[step]


def join(where, result, other, after):
    chips, rows, width = other.shape
    return pl.pallas_call(
        join_kernel,
        in_specs=[SMEM, VMEM, VMEM] + [ANY] * len(after),
        out_specs=[VMEM] * chips,
        out_shape=[jax.ShapeDtypeStruct((rows, 2 * width), other.dtype)] * chips,
        name="join",
    )(where, result, other, *after)


def arrive_kernel(where, part_0, part_1, part_2, part_3, out):
    chip = where[0]
    parts = (part_0, part_1, part_2, part_3)
    width = part_0.shape[1]
    for step in range(len(parts)):
        origin = lax.rem(chip + len(parts) - step, len(parts))
        out[0, :, pl.ds(pl.multiple_of(origin * width, width), width)] = parts[step][...]


def arrive(where, parts):
    rows, width = parts[0].shape
    return pl.pallas_call(
        arrive_kernel,
        in_specs=[SMEM] + [VMEM] * len(parts),
        out_specs=VMEM,
        out_shape=jax.ShapeDtypeStruct((1, rows, len(parts) * width), parts[0].dtype),
        name="arrive",
    )(where, *parts)


def down_kernel(core, *refs):
    *parts, hidden, hidden_other, up, out, back = refs

    @pl.when(pl.program_id(0) == 0)
    def _():
        total = parts[0][...].astype(jnp.float32)
        for part in parts[1:]:
            total += part[...].astype(jnp.float32)
        back[...] = total.astype(jnp.bfloat16)

    grad = dot(back[core[0]], hidden[...]) + dot(back[1 - core[0]], hidden_other[...])
    grad = grad.astype(out.dtype)
    for row in range(out.shape[0]):
        across = slice(row * SHARE_ROWS, (row + 1) * SHARE_ROWS)
        for column in range(out.shape[1]):
            out[row, column, :, :DOWN_COLS] = grad[
                across, column * DOWN_COLS : (column + 1) * DOWN_COLS
            ]
            out[row, column, :, DOWN_COLS:] = up[across, column * 128 : (column + 1) * 128]


def down_gradient(core, parts, hidden, hidden_other, up):
    rows, half = hidden_other.shape
    steps = 2
    step = half // steps
    columns = half // DOWN_COLS
    across = 2 * RANK // SHARE_ROWS
    shape = parts[0].shape
    return pl.pallas_call(
        down_kernel,
        grid_spec=pltpu.PrefetchScalarGridSpec(
            num_scalar_prefetch=1,
            grid=(steps,),
            in_specs=[pl.BlockSpec(shape, lambda i, core: (0, 0, 0))] * len(parts)
            + [
                pl.BlockSpec((rows, step), lambda i, core: (0, core[0] * steps + i)),
                pl.BlockSpec((rows, step), lambda i, core: (0, i)),
                pl.BlockSpec((2 * RANK, columns // steps * 128), lambda i, core: (0, i)),
            ],
            out_specs=pl.BlockSpec(
                (across, columns // steps, SHARE_ROWS, DOWN_COLS + 128),
                lambda i, core: (0, i, 0, 0),
            ),
            scratch_shapes=[pltpu.VMEM(shape, jnp.bfloat16)],
        ),
        out_shape=jax.ShapeDtypeStruct(
            (across, columns, SHARE_ROWS, DOWN_COLS + 128), jnp.bfloat16
        ),
        compiler_params=pltpu.CompilerParams(vmem_limit_bytes=24 << 20),
        name="down_gradient",
    )(core, *parts, hidden, hidden_other, up)


def share_kernel(parts, *refs):
    out = refs[-1]
    total = parts[0].astype(jnp.float32)
    for part in range(1, parts.shape[0]):
        total += parts[part].astype(jnp.float32)
    total = total.astype(out.dtype)
    for part in range(out.shape[0]):
        out[part] = total


def sum_share(parts, after):
    return pl.pallas_call(
        share_kernel,
        in_specs=[VMEM] + [ANY] * len(after),
        out_specs=VMEM,
        out_shape=jax.ShapeDtypeStruct(parts.shape, parts.dtype),
        name="sum_share",
    )(parts, *after)


def place_kernel(core, own, other, grad_a_q, up_q, grad_a_v, up_v, wide):
    half = own.shape[0] // 2
    columns = own.shape[1]
    for part, shares in enumerate((own, other)):
        which = core[0] if part == 0 else 1 - core[0]
        for row in range(own.shape[0]):
            across = slice(row % half * SHARE_ROWS, (row % half + 1) * SHARE_ROWS)
            target = (grad_a_q, grad_a_v)[row // half]
            for column in range(columns):
                begin = pl.multiple_of((which * columns + column) * DOWN_COLS, DOWN_COLS)
                target[across, pl.ds(begin, DOWN_COLS)] = shares[
                    row, column, :, :DOWN_COLS
                ].astype(jnp.float32)
                wide[
                    row * SHARE_ROWS : (row + 1) * SHARE_ROWS, column * 128 : (column + 1) * 128
                ] = shares[row, column, :, DOWN_COLS:]
        width = columns * UP_COLS
        source = lax.broadcasted_iota(jnp.int32, (columns * 128, width), 0)
        lane = lax.broadcasted_iota(jnp.int32, (columns * 128, width), 1)
        lane = (lane // UP_COLS) * 128 + lane % UP_COLS
        for chip in range(128 // UP_COLS):
            pick = jnp.where(source == lane + chip * UP_COLS, 1.0, 0.0).astype(jnp.bfloat16)
            picked = dot(wide[...], pick)
            begin = pl.multiple_of((2 * chip + which) * width, width)
            up_q[:, pl.ds(begin, width)] = picked[:RANK]
            up_v[:, pl.ds(begin, width)] = picked[RANK:]


def place(core, own, other, model, width):
    shapes = [(RANK, model), (RANK, width), (RANK, model), (RANK, width)]
    return pl.pallas_call(
        place_kernel,
        in_specs=[SMEM, VMEM, VMEM],
        out_specs=[VMEM] * 4,
        out_shape=[jax.ShapeDtypeStruct(shape, jnp.float32) for shape in shapes],
        scratch_shapes=[pltpu.VMEM((2 * RANK, own.shape[1] * 128), jnp.bfloat16)],
        compiler_params=pltpu.CompilerParams(vmem_limit_bytes=30 << 20),
        name="place",
    )(core, own, other)


def swap(x, axes):
    return lax.all_to_all(x, axes, 0, 0, tiled=True)


def to_other_core(x):
    return lax.ppermute(x, "core", [(0, 1), (1, 0)])


def per_device(
    sizes,
    hidden,
    frozen_queries,
    frozen_keys,
    frozen_values,
    document_length_list,
    query_down_weight,
    query_up_weight,
    value_down_weight,
    value_up_weight,
    output_gradient,
):
    dp_size, seq_size = sizes
    chips = seq_size // 2
    rows, model = hidden.shape[1:]
    half = model // 2
    chip = lax.axis_index("y").astype(jnp.int32)
    core = lax.axis_index("core").astype(jnp.int32)
    where = jnp.stack([chip, core])

    def to_chip(x, step):
        return lax.ppermute(x, "y", [(c, (c + step) % chips) for c in range(chips)])

    packed, low = pack(
        hidden[0],
        query_down_weight.T,
        value_down_weight.T,
        frozen_queries[0],
        frozen_keys[0],
        frozen_values[0],
        output_gradient[0],
        query_up_weight,
        value_up_weight,
        seq_size,
    )
    received = swap(packed, SEQ).reshape(seq_size * rows, packed.shape[2])
    hidden_other = to_other_core(
        lax.dynamic_slice(hidden[0], (0, (1 - core) * half), (rows, half))
    )
    lows = [low] + [to_chip(low, step) for step in range(1, chips)]
    lows = lows + [to_other_core(low) for low in lows]
    width = frozen_queries.shape[2] // seq_size
    own_columns = (0, (chip * 2 + core) * width)
    wq_up = lax.dynamic_slice(query_up_weight, own_columns, (RANK, width))
    wv_up = lax.dynamic_slice(value_up_weight, own_columns, (RANK, width))
    meta = jnp.concatenate([document_length_list[0], chip[None]])
    result, *backs, dq_t, dv_t = attention(meta, received, wq_up, wv_up, seq_size, after=lows)

    backs = [backs[0]] + [to_chip(backs[step], step) for step in range(1, chips)]
    backs_other = [to_other_core(back) for back in backs]
    up = up_gradient(where, lows, dq_t, dv_t)
    joined = join(where, result, to_other_core(leaving(where, result, seq_size)), after=backs)
    parts = [joined[0]] + [to_chip(joined[step], step) for step in range(1, chips)]
    attended = arrive(where, parts)
    down = down_gradient(core[None], backs + backs_other, hidden[0], hidden_other, up)

    shares = swap(down.reshape((-1,) + down.shape[2:]), PLANE)
    shares = swap(sum_share(shares, after=parts[1:]), PLANE).reshape(down.shape)
    shares_other = to_other_core(shares)
    grad_a_q, up_q, grad_a_v, up_v = place(
        core[None], shares, shares_other, model, seq_size * width
    )
    return attended, grad_a_q.T, up_q, grad_a_v.T, up_v


def solution(mesh):
    dp_size, seq_size = mesh.shape["dp"], mesh.shape["seq"]
    fine = Mesh(mesh.devices.reshape(4, 4, 4, 2), ALL)
    rows = P(DP, SEQ, None)
    in_specs = (rows, rows, rows, rows, P(DP, None), P(), P(), P(), P(), rows)
    out_specs = (rows, P(), P(), P(), P())
    return jax.shard_map(
        functools.partial(per_device, (dp_size, seq_size)),
        mesh=fine,
        in_specs=in_specs,
        out_specs=out_specs,
        check_vma=False,
    )
```

```python
import functools

import jax
import jax.numpy as jnp
from jax import lax
from jax.experimental import pallas as pl
from jax.experimental.pallas import tpu as pltpu
from jax.sharding import Mesh
from jax.sharding import PartitionSpec as P

HEAD_COUNT = 16
HEAD_SIZE = 128
RANK = 64
NDOC = 8
TILE = 256
MAX_TILES = 5
ADAPTER_SCALE = 2.0
NEG_FILL = -1e30
SCALING = HEAD_SIZE ** (-0.5)
LOG2_E = 1.4426950408889634

SHARE_ROWS = 16
DOWN_COLS = 256
UP_COLS = 32

DP = ("x", "z")
SEQ = ("y", "core")
PLANE = ("x", "z", "y")
ALL = ("x", "z", "y", "core")
NT = (((1,), (1,)), ((), ()))


def dot(a, b):
    return jnp.dot(a, b, preferred_element_type=jnp.float32)


def dot_nt(a, b):
    return lax.dot_general(a, b, NT, preferred_element_type=jnp.float32)


HIDDEN_PARTS = 4
PACK_VMEM = 56 << 20
SMALL_VMEM = 8 << 20
VMEM = pl.BlockSpec(memory_space=pltpu.VMEM)
SMEM = pl.BlockSpec(memory_space=pltpu.SMEM)
ANY = pl.BlockSpec(memory_space=pl.ANY)


def pack_kernel(
    hidden, wq_down, wv_down, fq, fk, fv, grad, wq_up, wv_up, out, low,
    hidden_v, wq_down_v, wv_down_v, fq_v, fv_v, wq_up_v, wv_up_v, out_v,
    down_sems, hidden_sems, row_sems, through_sems, out_sems,
):
    devices, rows, packed = out.shape
    width = packed // 4
    model = hidden.shape[1]
    step = model // HIDDEN_PARTS

    def part(index):
        return pl.ds(index * step, step)

    def columns(index):
        return pl.ds(index * width, width)

    downs = [
        pltpu.make_async_copy(wq_down, wq_down_v, down_sems.at[0]),
        pltpu.make_async_copy(wv_down, wv_down_v, down_sems.at[1]),
    ]
    hiddens = [
        pltpu.make_async_copy(
            hidden.at[:, part(index)], hidden_v.at[:, part(index)], hidden_sems.at[index]
        )
        for index in range(HIDDEN_PARTS)
    ]
    whole = [
        pltpu.make_async_copy(wq_up, wq_up_v, row_sems.at[0]),
        pltpu.make_async_copy(fq, fq_v, row_sems.at[1]),
        pltpu.make_async_copy(wv_up, wv_up_v, row_sems.at[2]),
        pltpu.make_async_copy(fv, fv_v, row_sems.at[3]),
    ]
    through = []
    for device in range(devices):
        for which, source in ((1, fk), (3, grad)):
            through.append(
                pltpu.make_async_copy(
                    source.at[:, columns(device)],
                    out_v.at[device, :, columns(which)],
                    through_sems.at[len(through)],
                )
            )
    for copy in downs + hiddens + whole + through:
        copy.start()

    for copy in downs:
        copy.wait()
    low_q = jnp.zeros((rows, RANK), jnp.float32)
    low_v = jnp.zeros((rows, RANK), jnp.float32)
    for index in range(HIDDEN_PARTS):
        hiddens[index].wait()
        low_q += dot_nt(hidden_v[:, part(index)], wq_down_v[:, part(index)])
        low_v += dot_nt(hidden_v[:, part(index)], wv_down_v[:, part(index)])
    low[:, :RANK] = low_q.astype(jnp.bfloat16)
    low[:, RANK:] = low_v.astype(jnp.bfloat16)

    for copy in whole:
        copy.wait()
    outs = []
    for device in range(devices):
        at = slice(device * width, (device + 1) * width)
        for which, (frozen, weight, begin) in enumerate(
            ((fq_v, wq_up_v, 0), (fv_v, wv_up_v, RANK))
        ):
            added = ADAPTER_SCALE * dot(low[:, begin : begin + RANK], weight[:, at])
            out_v[device, :, 2 * which * width : (2 * which + 1) * width] = (
                frozen[:, at].astype(jnp.float32) + added
            ).astype(jnp.bfloat16)
        through[2 * device].wait()
        through[2 * device + 1].wait()
        outs.append(pltpu.make_async_copy(out_v.at[device], out.at[device], out_sems.at[device]))
        outs[-1].start()
    for copy in outs:
        copy.wait()


def pack(hidden, wq_down_t, wv_down_t, fq, fk, fv, grad, wq_up, wv_up, seq_size):
    rows, model = hidden.shape
    columns = fq.shape[1]
    width = columns // seq_size
    bf16 = jnp.bfloat16
    return pl.pallas_call(
        pack_kernel,
        in_specs=[ANY] * 9,
        out_specs=[ANY, VMEM],
        out_shape=[
            jax.ShapeDtypeStruct((seq_size, rows, 4 * width), bf16),
            jax.ShapeDtypeStruct((rows, 2 * RANK), bf16),
        ],
        scratch_shapes=[
            pltpu.VMEM((rows, model), bf16),
            pltpu.VMEM((RANK, model), bf16),
            pltpu.VMEM((RANK, model), bf16),
            pltpu.VMEM((rows, columns), bf16),
            pltpu.VMEM((rows, columns), bf16),
            pltpu.VMEM((RANK, columns), bf16),
            pltpu.VMEM((RANK, columns), bf16),
            pltpu.VMEM((seq_size, rows, 4 * width), bf16),
            pltpu.SemaphoreType.DMA((2,)),
            pltpu.SemaphoreType.DMA((HIDDEN_PARTS,)),
            pltpu.SemaphoreType.DMA((4,)),
            pltpu.SemaphoreType.DMA((2 * seq_size,)),
            pltpu.SemaphoreType.DMA((seq_size,)),
        ],
        compiler_params=pltpu.CompilerParams(vmem_limit_bytes=PACK_VMEM),
        name="pack",
    )(hidden, wq_down_t, wv_down_t, fq, fk, fv, grad, wq_up, wv_up)


def attention_kernel(
    meta, packed, wq_up, wv_up, *refs
):
    out, leaving, back_0, back_1, back_2, back_3, dq_t, dv_t, q_t, k_t, v_t, g_t, dv, returned = (
        refs[-14:]
    )
    length = packed.shape[0]
    heads = out.shape[1] // HEAD_SIZE
    width = heads * HEAD_SIZE
    blocks = length // TILE
    chip, core = meta[NDOC], meta[NDOC + 1]
    span = [slice(head * HEAD_SIZE, (head + 1) * HEAD_SIZE) for head in range(heads)]

    def columns(which, head):
        begin = which * width + head * HEAD_SIZE
        return slice(begin, begin + HEAD_SIZE)

    for head in range(heads):
        q_t[span[head], :] = packed[:, columns(0, head)].T
        k_t[span[head], :] = packed[:, columns(1, head)].T
        v_t[span[head], :] = packed[:, columns(2, head)].T
        g_t[span[head], :] = packed[:, columns(3, head)].T
    dv[...] = jnp.zeros_like(dv)

    def block(index, _):
        row0 = pl.multiple_of(index * TILE, TILE)
        q_rows = pl.ds(row0, TILE)
        position = row0 + lax.broadcasted_iota(jnp.int32, (1, TILE), 1)
        begin = jnp.zeros((1, TILE), jnp.int32)
        first = jnp.int32(0)
        end = jnp.int32(0)
        for doc in range(NDOC):
            end = end + meta[doc]
            begin = jnp.where(position >= end, end, begin)
            first = jnp.where(row0 >= end, end, first)
        tiles = index - lax.div(first, TILE) + 1

        def body(count):
            key0 = pl.multiple_of((index + 1 - count) * TILE, TILE)
            k_rows = pl.ds(key0, count * TILE)
            key_index = lax.broadcasted_iota(jnp.int32, (count * TILE, TILE), 0)
            in_document = key_index >= begin - key0
            causal = lax.broadcasted_iota(jnp.int32, (TILE, TILE), 0) <= (
                lax.broadcasted_iota(jnp.int32, (TILE, TILE), 1)
            )
            held = []
            for head in range(heads):
                scores = dot(packed[k_rows, columns(1, head)], q_t[span[head], q_rows])
                prob_grad = dot(packed[k_rows, columns(2, head)], g_t[span[head], q_rows])
                scores = jnp.where(in_document, scores, NEG_FILL)
                last = jnp.where(causal, scores[(count - 1) * TILE :], NEG_FILL)
                if count > 1:
                    scores = jnp.concatenate([scores[: (count - 1) * TILE], last], axis=0)
                else:
                    scores = last
                maximum = jnp.max(scores, axis=0, keepdims=True)
                powers = jnp.exp2((scores - maximum) * (SCALING * LOG2_E))
                inverse = 1.0 / jnp.sum(powers, axis=0, keepdims=True)
                held.append((prob_grad, powers.astype(jnp.bfloat16), inverse))
            for head in range(heads):
                prob_grad, rounded, inverse = held[head]
                result = (dot(v_t[span[head], k_rows], rounded) * inverse).astype(jnp.bfloat16)
                g_wide = g_t[span[head], q_rows].astype(jnp.float32)
                row_dot = jnp.sum(g_wide * result.astype(jnp.float32), axis=0, keepdims=True)
                score_grad = rounded * (prob_grad - row_dot).astype(jnp.bfloat16)
                query_grad = dot(k_t[span[head], k_rows], score_grad) * (inverse * SCALING)
                dq_t[span[head], q_rows] = query_grad.astype(jnp.bfloat16)
                out[q_rows, span[head]] = result.T
                g_scaled = (g_wide * inverse).astype(jnp.bfloat16).T
                dv[head, k_rows, :] += dot(rounded, g_scaled)

        for count in range(1, min(MAX_TILES, blocks) + 1):
            pl.when(tiles == count)(functools.partial(body, count))
        return 0

    lax.fori_loop(0, blocks, block, 0)
    for head in range(heads):
        dv_t[span[head], :] = dv[head].astype(jnp.bfloat16).T

    for part, (grads, weight) in enumerate(((dq_t, wq_up), (dv_t, wv_up))):
        returned[part * RANK : (part + 1) * RANK, :] = (
            ADAPTER_SCALE * dot(weight[...], grads[...])
        ).astype(jnp.bfloat16)
    backs = (back_0, back_1, back_2, back_3)
    rows = back_0.shape[2]
    for step in range(len(backs)):
        target = lax.rem(chip + step, len(backs))
        for holder in range(2):
            begin = pl.multiple_of((target * 2 + holder) * rows, rows)
            backs[step][holder] = returned[:, pl.ds(begin, rows)]
        begin = pl.multiple_of((target * 2 + 1 - core) * rows, rows)
        leaving[step] = out[pl.ds(begin, rows), :]


def attention(meta, packed, wq_up, wv_up, seq_size, after):
    length = packed.shape[0]
    width = packed.shape[1] // 4
    rows = length // seq_size
    heads = width // HEAD_SIZE
    chips = seq_size // 2
    wide_t = pltpu.VMEM((width, length), jnp.bfloat16)
    back = jax.ShapeDtypeStruct((2, 2 * RANK, rows), jnp.bfloat16)
    grad_t = jax.ShapeDtypeStruct((width, length), jnp.bfloat16)
    return pl.pallas_call(
        attention_kernel,
        in_specs=[SMEM, VMEM, VMEM, VMEM] + [VMEM] * len(after),
        out_specs=[VMEM] * (4 + chips),
        scratch_shapes=[
            wide_t,
            wide_t,
            wide_t,
            wide_t,
            pltpu.VMEM((heads, length, HEAD_SIZE), jnp.float32),
            pltpu.VMEM((2 * RANK, length), jnp.bfloat16),
        ],
        out_shape=[
            jax.ShapeDtypeStruct((length, width), jnp.bfloat16),
            jax.ShapeDtypeStruct((chips, rows, width), jnp.bfloat16),
        ]
        + [back] * chips
        + [grad_t, grad_t],
        compiler_params=pltpu.CompilerParams(vmem_limit_bytes=40 << 20),
        cost_estimate=pl.CostEstimate(
            flops=8 << 30, bytes_accessed=16 << 20, transcendentals=4 << 20
        ),
        name="attention",
    )(meta, packed, wq_up, wv_up, *after)


def up_kernel(where, *refs):
    chip, core = where[0], where[1]
    *lows, dq_t, dv_t, up = refs
    steps = len(lows) // 2
    rows = lows[0].shape[0]
    width = dq_t.shape[0]
    lane = lax.broadcasted_iota(jnp.int32, (width, up.shape[1]), 1)
    source = lax.broadcasted_iota(jnp.int32, (width, up.shape[1]), 0)
    mine = (source == (lane // 128) * UP_COLS + lane % UP_COLS) & (
        (lane % 128) // UP_COLS == chip
    )
    mine = jnp.where(mine, 1.0, 0.0).astype(jnp.bfloat16)
    for part, grads in enumerate((dq_t, dv_t)):
        total = jnp.zeros((width, 2 * RANK), jnp.float32)
        for index, low in enumerate(lows):
            origin = lax.rem(chip + steps - index % steps, steps)
            holder = core if index < steps else 1 - core
            begin = pl.multiple_of((origin * 2 + holder) * rows, rows)
            total += dot(grads[:, pl.ds(begin, rows)], low[...])
        share = (total * ADAPTER_SCALE).T[part * RANK : (part + 1) * RANK, :]
        up[part * RANK : (part + 1) * RANK, :] = dot(share.astype(jnp.bfloat16), mine).astype(
            jnp.bfloat16
        )


def up_gradient(where, lows, dq_t, dv_t):
    width = dq_t.shape[0]
    return pl.pallas_call(
        up_kernel,
        in_specs=[SMEM] + [VMEM] * (len(lows) + 2),
        out_specs=VMEM,
        out_shape=jax.ShapeDtypeStruct((2 * RANK, width // UP_COLS * 128), jnp.bfloat16),
        compiler_params=pltpu.CompilerParams(vmem_limit_bytes=24 << 20),
        name="up_gradient",
    )(where, *lows, dq_t, dv_t)


def join_kernel(where, result, other, *outs):
    chip, core = where[0], where[1]
    chips, rows, width = other.shape
    here = pl.multiple_of(core * width, width)
    there = pl.multiple_of((1 - core) * width, width)
    for step in range(chips):
        target = lax.rem(chip + step, chips)
        begin = pl.multiple_of((target * 2 + core) * rows, rows)
        outs[step][:, pl.ds(here, width)] = result[pl.ds(begin, rows), :]
        outs[step][:, pl.ds(there, width)] = other[step]


def join(where, result, other):
    chips, rows, width = other.shape
    return pl.pallas_call(
        join_kernel,
        in_specs=[SMEM, VMEM, VMEM],
        out_specs=[VMEM] * chips,
        out_shape=[jax.ShapeDtypeStruct((rows, 2 * width), other.dtype)] * chips,
        compiler_params=pltpu.CompilerParams(vmem_limit_bytes=SMALL_VMEM),
        name="join",
    )(where, result, other)


def arrive_kernel(where, part_0, part_1, part_2, part_3, out):
    chip = where[0]
    parts = (part_0, part_1, part_2, part_3)
    width = part_0.shape[1]
    for step in range(len(parts)):
        origin = lax.rem(chip + len(parts) - step, len(parts))
        out[0, :, pl.ds(pl.multiple_of(origin * width, width), width)] = parts[step][...]


def arrive(where, parts):
    rows, width = parts[0].shape
    return pl.pallas_call(
        arrive_kernel,
        in_specs=[SMEM] + [VMEM] * len(parts),
        out_specs=VMEM,
        out_shape=jax.ShapeDtypeStruct((1, rows, len(parts) * width), parts[0].dtype),
        compiler_params=pltpu.CompilerParams(vmem_limit_bytes=SMALL_VMEM),
        name="arrive",
    )(where, *parts)


def down_kernel(core, *refs):
    parts, (hidden, hidden_other, up) = refs[:8], refs[8:11]
    out, back = refs[-2:]

    @pl.when(pl.program_id(0) == 0)
    def _():
        total = parts[0][...].astype(jnp.float32)
        for part in parts[1:]:
            total += part[...].astype(jnp.float32)
        back[...] = total.astype(jnp.bfloat16)

    grad = dot(back[core[0]], hidden[...]) + dot(back[1 - core[0]], hidden_other[...])
    grad = grad.astype(out.dtype)
    for row in range(out.shape[0]):
        across = slice(row * SHARE_ROWS, (row + 1) * SHARE_ROWS)
        for column in range(out.shape[1]):
            out[row, column, :, :DOWN_COLS] = grad[
                across, column * DOWN_COLS : (column + 1) * DOWN_COLS
            ]
            out[row, column, :, DOWN_COLS:] = up[across, column * 128 : (column + 1) * 128]


def down_gradient(core, parts, hidden, hidden_other, up, after):
    rows, half = hidden_other.shape
    steps = 2
    step = half // steps
    columns = half // DOWN_COLS
    across = 2 * RANK // SHARE_ROWS
    shape = parts[0].shape
    return pl.pallas_call(
        down_kernel,
        grid_spec=pltpu.PrefetchScalarGridSpec(
            num_scalar_prefetch=1,
            grid=(steps,),
            in_specs=[pl.BlockSpec(shape, lambda i, core: (0, 0, 0))] * len(parts)
            + [
                pl.BlockSpec((rows, step), lambda i, core: (0, core[0] * steps + i)),
                pl.BlockSpec((rows, step), lambda i, core: (0, i)),
                pl.BlockSpec((2 * RANK, columns // steps * 128), lambda i, core: (0, i)),
            ]
            + [VMEM] * len(after),
            out_specs=pl.BlockSpec(
                (across, columns // steps, SHARE_ROWS, DOWN_COLS + 128),
                lambda i, core: (0, i, 0, 0),
            ),
            scratch_shapes=[pltpu.VMEM(shape, jnp.bfloat16)],
        ),
        out_shape=jax.ShapeDtypeStruct(
            (across, columns, SHARE_ROWS, DOWN_COLS + 128), jnp.bfloat16
        ),
        compiler_params=pltpu.CompilerParams(vmem_limit_bytes=24 << 20),
        name="down_gradient",
    )(core, *parts, hidden, hidden_other, up, *after)


def share_kernel(parts, *refs):
    out = refs[-1]
    total = parts[0].astype(jnp.float32)
    for part in range(1, parts.shape[0]):
        total += parts[part].astype(jnp.float32)
    total = total.astype(out.dtype)
    for part in range(out.shape[0]):
        out[part] = total


def sum_share(parts, after):
    return pl.pallas_call(
        share_kernel,
        in_specs=[VMEM] + [VMEM] * len(after),
        out_specs=VMEM,
        out_shape=jax.ShapeDtypeStruct(parts.shape, parts.dtype),
        compiler_params=pltpu.CompilerParams(vmem_limit_bytes=SMALL_VMEM),
        name="sum_share",
    )(parts, *after)


def place_kernel(core, own, other, grad_a_q, up_q, grad_a_v, up_v, wide):
    half = own.shape[0] // 2
    columns = own.shape[1]
    for part, shares in enumerate((own, other)):
        which = core[0] if part == 0 else 1 - core[0]
        for row in range(own.shape[0]):
            across = slice(row % half * SHARE_ROWS, (row % half + 1) * SHARE_ROWS)
            target = (grad_a_q, grad_a_v)[row // half]
            for column in range(columns):
                begin = pl.multiple_of((which * columns + column) * DOWN_COLS, DOWN_COLS)
                target[across, pl.ds(begin, DOWN_COLS)] = shares[
                    row, column, :, :DOWN_COLS
                ].astype(jnp.float32)
                wide[
                    row * SHARE_ROWS : (row + 1) * SHARE_ROWS, column * 128 : (column + 1) * 128
                ] = shares[row, column, :, DOWN_COLS:]
        width = columns * UP_COLS
        source = lax.broadcasted_iota(jnp.int32, (columns * 128, width), 0)
        lane = lax.broadcasted_iota(jnp.int32, (columns * 128, width), 1)
        lane = (lane // UP_COLS) * 128 + lane % UP_COLS
        for chip in range(128 // UP_COLS):
            pick = jnp.where(source == lane + chip * UP_COLS, 1.0, 0.0).astype(jnp.bfloat16)
            picked = dot(wide[...], pick)
            begin = pl.multiple_of((2 * chip + which) * width, width)
            up_q[:, pl.ds(begin, width)] = picked[:RANK]
            up_v[:, pl.ds(begin, width)] = picked[RANK:]


def place(core, own, other, model, width):
    shapes = [(RANK, model), (RANK, width), (RANK, model), (RANK, width)]
    return pl.pallas_call(
        place_kernel,
        in_specs=[SMEM, VMEM, VMEM],
        out_specs=[VMEM] * 4,
        out_shape=[jax.ShapeDtypeStruct(shape, jnp.float32) for shape in shapes],
        scratch_shapes=[pltpu.VMEM((2 * RANK, own.shape[1] * 128), jnp.bfloat16)],
        compiler_params=pltpu.CompilerParams(vmem_limit_bytes=30 << 20),
        name="place",
    )(core, own, other)


def swap(x, axes):
    return lax.all_to_all(x, axes, 0, 0, tiled=True)


def to_other_core(x):
    return lax.ppermute(x, "core", [(0, 1), (1, 0)])


def per_device(
    sizes,
    hidden,
    frozen_queries,
    frozen_keys,
    frozen_values,
    document_length_list,
    query_down_weight,
    query_up_weight,
    value_down_weight,
    value_up_weight,
    output_gradient,
):
    dp_size, seq_size = sizes
    chips = seq_size // 2
    rows, model = hidden.shape[1:]
    half = model // 2
    chip = lax.axis_index("y").astype(jnp.int32)
    core = lax.axis_index("core").astype(jnp.int32)
    where = jnp.stack([chip, core])

    def to_chip(x, step):
        return lax.ppermute(x, "y", [(c, (c + step) % chips) for c in range(chips)])

    packed, low = pack(
        hidden[0],
        query_down_weight.T,
        value_down_weight.T,
        frozen_queries[0],
        frozen_keys[0],
        frozen_values[0],
        output_gradient[0],
        query_up_weight,
        value_up_weight,
        seq_size,
    )
    received = swap(packed, SEQ).reshape(seq_size * rows, packed.shape[2])
    hidden_other = to_other_core(
        lax.dynamic_slice(hidden[0], (0, (1 - core) * half), (rows, half))
    )
    lows = [low] + [to_chip(low, step) for step in range(1, chips)]
    lows = lows + [to_other_core(low) for low in lows]
    width = frozen_queries.shape[2] // seq_size
    own_columns = (0, (chip * 2 + core) * width)
    wq_up = lax.dynamic_slice(query_up_weight, own_columns, (RANK, width))
    wv_up = lax.dynamic_slice(value_up_weight, own_columns, (RANK, width))
    meta = jnp.concatenate([document_length_list[0], where])
    result, leaving, *backs, dq_t, dv_t = attention(
        meta, received, wq_up, wv_up, seq_size, after=lows[1:chips]
    )

    backs = [backs[0]] + [to_chip(backs[step], step) for step in range(1, chips)]
    backs_other = [to_other_core(back) for back in backs]
    up = up_gradient(where, lows, dq_t, dv_t)
    joined = join(where, result, to_other_core(leaving))
    parts = [joined[0]] + [to_chip(joined[step], step) for step in range(1, chips)]
    attended = arrive(where, parts)
    down = down_gradient(core[None], backs + backs_other, hidden[0], hidden_other, up, after=joined)

    shares = swap(down.reshape((-1,) + down.shape[2:]), PLANE)
    shares = swap(sum_share(shares, after=parts[1:]), PLANE).reshape(down.shape)
    shares_other = to_other_core(shares)
    grad_a_q, up_q, grad_a_v, up_v = place(
        core[None], shares, shares_other, model, seq_size * width
    )
    return attended, grad_a_q.T, up_q, grad_a_v.T, up_v


def solution(mesh):
    dp_size, seq_size = mesh.shape["dp"], mesh.shape["seq"]
    fine = Mesh(mesh.devices.reshape(4, 4, 4, 2), ALL)
    rows = P(DP, SEQ, None)
    in_specs = (rows, rows, rows, rows, P(DP, None), P(), P(), P(), P(), rows)
    out_specs = (rows, P(), P(), P(), P())
    return jax.shard_map(
        functools.partial(per_device, (dp_size, seq_size)),
        mesh=fine,
        in_specs=in_specs,
        out_specs=out_specs,
        check_vma=False,
    )
```

```python
import functools

import jax
import jax.numpy as jnp
from jax import lax
from jax.experimental import pallas as pl
from jax.experimental.pallas import tpu as pltpu
from jax.sharding import Mesh
from jax.sharding import PartitionSpec as P

HEAD_COUNT = 16
HEAD_SIZE = 128
RANK = 64
NDOC = 8
TILE = 256
MAX_TILES = 5
ADAPTER_SCALE = 2.0
NEG_FILL = -1e30
SCALING = HEAD_SIZE ** (-0.5)
LOG2_E = 1.4426950408889634

SHARE_ROWS = 16
DOWN_COLS = 256
UP_COLS = 32

DP = ("x", "z")
SEQ = ("y", "core")
PLANE = ("x", "z", "y")
ALL = ("x", "z", "y", "core")
NT = (((1,), (1,)), ((), ()))


def dot(a, b):
    return jnp.dot(a, b, preferred_element_type=jnp.float32)


def dot_nt(a, b):
    return lax.dot_general(a, b, NT, preferred_element_type=jnp.float32)


HIDDEN_PARTS = 4
PACK_VMEM = 56 << 20
SMALL_VMEM = 8 << 20
VMEM = pl.BlockSpec(memory_space=pltpu.VMEM)
SMEM = pl.BlockSpec(memory_space=pltpu.SMEM)
ANY = pl.BlockSpec(memory_space=pl.ANY)


def pack_kernel(
    hidden, wq_down, wv_down, fq, fk, fv, grad, wq_up, wv_up, out,
    hidden_v, wq_down_v, wv_down_v, fq_v, fv_v, wq_up_v, wv_up_v, out_v, low,
    down_sems, hidden_sems, row_sems, through_sems, out_sems,
):
    devices, rows, packed = out.shape
    width = (packed - 2 * RANK) // 4
    model = hidden.shape[1]
    step = model // HIDDEN_PARTS

    def part(index):
        return pl.ds(index * step, step)

    def columns(index):
        return pl.ds(index * width, width)

    downs = [
        pltpu.make_async_copy(wq_down, wq_down_v, down_sems.at[0]),
        pltpu.make_async_copy(wv_down, wv_down_v, down_sems.at[1]),
    ]
    hiddens = [
        pltpu.make_async_copy(
            hidden.at[:, part(index)], hidden_v.at[:, part(index)], hidden_sems.at[index]
        )
        for index in range(HIDDEN_PARTS)
    ]
    whole = [
        pltpu.make_async_copy(wq_up, wq_up_v, row_sems.at[0]),
        pltpu.make_async_copy(fq, fq_v, row_sems.at[1]),
        pltpu.make_async_copy(wv_up, wv_up_v, row_sems.at[2]),
        pltpu.make_async_copy(fv, fv_v, row_sems.at[3]),
    ]
    through = []
    for device in range(devices):
        for which, source in ((1, fk), (3, grad)):
            through.append(
                pltpu.make_async_copy(
                    source.at[:, columns(device)],
                    out_v.at[device, :, columns(which)],
                    through_sems.at[len(through)],
                )
            )
    for copy in downs + hiddens + whole + through:
        copy.start()

    for copy in downs:
        copy.wait()
    low_q = jnp.zeros((rows, RANK), jnp.float32)
    low_v = jnp.zeros((rows, RANK), jnp.float32)
    for index in range(HIDDEN_PARTS):
        hiddens[index].wait()
        low_q += dot_nt(hidden_v[:, part(index)], wq_down_v[:, part(index)])
        low_v += dot_nt(hidden_v[:, part(index)], wv_down_v[:, part(index)])
    low[:, :RANK] = low_q.astype(jnp.bfloat16)
    low[:, RANK:] = low_v.astype(jnp.bfloat16)

    for copy in whole:
        copy.wait()
    outs = []
    for device in range(devices):
        at = slice(device * width, (device + 1) * width)
        for which, (frozen, weight, begin) in enumerate(
            ((fq_v, wq_up_v, 0), (fv_v, wv_up_v, RANK))
        ):
            added = ADAPTER_SCALE * dot(low[:, begin : begin + RANK], weight[:, at])
            out_v[device, :, 2 * which * width : (2 * which + 1) * width] = (
                frozen[:, at].astype(jnp.float32) + added
            ).astype(jnp.bfloat16)
        out_v[device, :, 4 * width :] = low[...]
        through[2 * device].wait()
        through[2 * device + 1].wait()
        outs.append(pltpu.make_async_copy(out_v.at[device], out.at[device], out_sems.at[device]))
        outs[-1].start()
    for copy in outs:
        copy.wait()


def pack(hidden, wq_down_t, wv_down_t, fq, fk, fv, grad, wq_up, wv_up, seq_size):
    rows, model = hidden.shape
    columns = fq.shape[1]
    width = columns // seq_size
    bf16 = jnp.bfloat16
    return pl.pallas_call(
        pack_kernel,
        in_specs=[ANY] * 9,
        out_specs=ANY,
        out_shape=jax.ShapeDtypeStruct((seq_size, rows, 4 * width + 2 * RANK), bf16),
        scratch_shapes=[
            pltpu.VMEM((rows, model), bf16),
            pltpu.VMEM((RANK, model), bf16),
            pltpu.VMEM((RANK, model), bf16),
            pltpu.VMEM((rows, columns), bf16),
            pltpu.VMEM((rows, columns), bf16),
            pltpu.VMEM((RANK, columns), bf16),
            pltpu.VMEM((RANK, columns), bf16),
            pltpu.VMEM((seq_size, rows, 4 * width + 2 * RANK), bf16),
            pltpu.VMEM((rows, 2 * RANK), bf16),
            pltpu.SemaphoreType.DMA((2,)),
            pltpu.SemaphoreType.DMA((HIDDEN_PARTS,)),
            pltpu.SemaphoreType.DMA((4,)),
            pltpu.SemaphoreType.DMA((2 * seq_size,)),
            pltpu.SemaphoreType.DMA((seq_size,)),
        ],
        compiler_params=pltpu.CompilerParams(vmem_limit_bytes=PACK_VMEM),
        name="pack",
    )(hidden, wq_down_t, wv_down_t, fq, fk, fv, grad, wq_up, wv_up)


def attention_kernel(
    meta, packed, wq_up, wv_up, *refs
):
    *outs, dq_t, dv_t, low, q_t, k_t, v_t, g_t, dv, returned, out = refs
    outs, backs = outs[: len(outs) // 2], outs[len(outs) // 2 :]
    length = packed.shape[0]
    heads = out.shape[1] // HEAD_SIZE
    width = heads * HEAD_SIZE
    blocks = length // TILE
    chip = meta[NDOC]
    span = [slice(head * HEAD_SIZE, (head + 1) * HEAD_SIZE) for head in range(heads)]

    def columns(which, head):
        begin = which * width + head * HEAD_SIZE
        return slice(begin, begin + HEAD_SIZE)

    for head in range(heads):
        q_t[span[head], :] = packed[:, columns(0, head)].T
        k_t[span[head], :] = packed[:, columns(1, head)].T
        v_t[span[head], :] = packed[:, columns(2, head)].T
        g_t[span[head], :] = packed[:, columns(3, head)].T
    dv[...] = jnp.zeros_like(dv)

    def block(index, _):
        row0 = pl.multiple_of(index * TILE, TILE)
        q_rows = pl.ds(row0, TILE)
        position = row0 + lax.broadcasted_iota(jnp.int32, (1, TILE), 1)
        begin = jnp.zeros((1, TILE), jnp.int32)
        first = jnp.int32(0)
        end = jnp.int32(0)
        for doc in range(NDOC):
            end = end + meta[doc]
            begin = jnp.where(position >= end, end, begin)
            first = jnp.where(row0 >= end, end, first)
        tiles = index - lax.div(first, TILE) + 1

        def body(count):
            key0 = pl.multiple_of((index + 1 - count) * TILE, TILE)
            k_rows = pl.ds(key0, count * TILE)
            key_index = lax.broadcasted_iota(jnp.int32, (count * TILE, TILE), 0)
            in_document = key_index >= begin - key0
            causal = lax.broadcasted_iota(jnp.int32, (TILE, TILE), 0) <= (
                lax.broadcasted_iota(jnp.int32, (TILE, TILE), 1)
            )
            held = []
            for head in range(heads):
                scores = dot(packed[k_rows, columns(1, head)], q_t[span[head], q_rows])
                prob_grad = dot(packed[k_rows, columns(2, head)], g_t[span[head], q_rows])
                scores = jnp.where(in_document, scores, NEG_FILL)
                last = jnp.where(causal, scores[(count - 1) * TILE :], NEG_FILL)
                if count > 1:
                    scores = jnp.concatenate([scores[: (count - 1) * TILE], last], axis=0)
                else:
                    scores = last
                maximum = jnp.max(scores, axis=0, keepdims=True)
                powers = jnp.exp2((scores - maximum) * (SCALING * LOG2_E))
                inverse = 1.0 / jnp.sum(powers, axis=0, keepdims=True)
                held.append((prob_grad, powers.astype(jnp.bfloat16), inverse))
            for head in range(heads):
                prob_grad, rounded, inverse = held[head]
                result = (dot(v_t[span[head], k_rows], rounded) * inverse).astype(jnp.bfloat16)
                g_wide = g_t[span[head], q_rows].astype(jnp.float32)
                row_dot = jnp.sum(g_wide * result.astype(jnp.float32), axis=0, keepdims=True)
                score_grad = rounded * (prob_grad - row_dot).astype(jnp.bfloat16)
                query_grad = dot(k_t[span[head], k_rows], score_grad) * (inverse * SCALING)
                dq_t[span[head], q_rows] = query_grad.astype(jnp.bfloat16)
                out[q_rows, span[head]] = result.T
                g_scaled = (g_wide * inverse).astype(jnp.bfloat16).T
                dv[head, k_rows, :] += dot(rounded, g_scaled)

        for count in range(1, min(MAX_TILES, blocks) + 1):
            pl.when(tiles == count)(functools.partial(body, count))
        return 0

    lax.fori_loop(0, blocks, block, 0)
    for head in range(heads):
        dv_t[span[head], :] = dv[head].astype(jnp.bfloat16).T

    for part, (grads, weight) in enumerate(((dq_t, wq_up), (dv_t, wv_up))):
        returned[part * RANK : (part + 1) * RANK, :] = (
            ADAPTER_SCALE * dot(weight[...], grads[...])
        ).astype(jnp.bfloat16)
    low[...] = packed[:, 4 * width :]
    rows = backs[0].shape[2]
    for step in range(len(backs)):
        target = lax.rem(chip + step, len(backs))
        for holder in range(2):
            begin = pl.multiple_of((target * 2 + holder) * rows, rows)
            backs[step][holder] = returned[:, pl.ds(begin, rows)]
            outs[step][holder] = out[pl.ds(begin, rows), :]


def attention(meta, packed, wq_up, wv_up, seq_size):
    length = packed.shape[0]
    width = (packed.shape[1] - 2 * RANK) // 4
    rows = length // seq_size
    heads = width // HEAD_SIZE
    chips = seq_size // 2
    wide_t = pltpu.VMEM((width, length), jnp.bfloat16)
    back = jax.ShapeDtypeStruct((2, 2 * RANK, rows), jnp.bfloat16)
    grad_t = jax.ShapeDtypeStruct((width, length), jnp.bfloat16)
    return pl.pallas_call(
        attention_kernel,
        in_specs=[SMEM, VMEM, VMEM, VMEM],
        out_specs=[VMEM] * (3 + 2 * chips),
        scratch_shapes=[
            wide_t,
            wide_t,
            wide_t,
            wide_t,
            pltpu.VMEM((heads, length, HEAD_SIZE), jnp.float32),
            pltpu.VMEM((2 * RANK, length), jnp.bfloat16),
            pltpu.VMEM((length, width), jnp.bfloat16),
        ],
        out_shape=[jax.ShapeDtypeStruct((2, rows, width), jnp.bfloat16)] * chips
        + [back] * chips
        + [grad_t, grad_t, jax.ShapeDtypeStruct((length, 2 * RANK), jnp.bfloat16)],
        compiler_params=pltpu.CompilerParams(vmem_limit_bytes=40 << 20),
        cost_estimate=pl.CostEstimate(
            flops=8 << 30, bytes_accessed=16 << 20, transcendentals=4 << 20
        ),
        name="attention",
    )(meta, packed, wq_up, wv_up)


def up_kernel(where, low, dq_t, dv_t, up):
    width = dq_t.shape[0]
    lane = lax.broadcasted_iota(jnp.int32, (width, up.shape[1]), 1)
    source = lax.broadcasted_iota(jnp.int32, (width, up.shape[1]), 0)
    mine = (source == (lane // 128) * UP_COLS + lane % UP_COLS) & (
        (lane % 128) // UP_COLS == where[0]
    )
    mine = jnp.where(mine, 1.0, 0.0).astype(jnp.bfloat16)
    for part, grads in enumerate((dq_t, dv_t)):
        share = (dot(grads[...], low[...]) * ADAPTER_SCALE).T[part * RANK : (part + 1) * RANK, :]
        up[part * RANK : (part + 1) * RANK, :] = dot(share.astype(jnp.bfloat16), mine).astype(
            jnp.bfloat16
        )


def up_gradient(where, low, dq_t, dv_t):
    width = dq_t.shape[0]
    return pl.pallas_call(
        up_kernel,
        in_specs=[SMEM] + [VMEM] * 3,
        out_specs=VMEM,
        out_shape=jax.ShapeDtypeStruct((2 * RANK, width // UP_COLS * 128), jnp.bfloat16),
        compiler_params=pltpu.CompilerParams(vmem_limit_bytes=16 << 20),
        name="up_gradient",
    )(where, low, dq_t, dv_t)


def pick_kernel(where, part_0, part_1, part_2, part_3, out):
    core = where[1]
    for step, part in enumerate((part_0, part_1, part_2, part_3)):
        out[step] = part[1 - core]


def pick(where, parts):
    return pl.pallas_call(
        pick_kernel,
        in_specs=[SMEM] + [VMEM] * len(parts),
        out_specs=VMEM,
        out_shape=jax.ShapeDtypeStruct((len(parts),) + parts[0].shape[1:], parts[0].dtype),
        compiler_params=pltpu.CompilerParams(vmem_limit_bytes=SMALL_VMEM),
        name="pick",
    )(where, *parts)


def arrive_kernel(where, part_0, part_1, part_2, part_3, other, out):
    chip, core = where[0], where[1]
    parts = (part_0, part_1, part_2, part_3)
    width = part_0.shape[2]
    for step in range(len(parts)):
        origin = lax.rem(chip + len(parts) - step, len(parts))
        here = pl.multiple_of((origin * 2 + core) * width, width)
        there = pl.multiple_of((origin * 2 + 1 - core) * width, width)
        out[0, :, pl.ds(here, width)] = parts[step][core]
        out[0, :, pl.ds(there, width)] = other[step]


def arrive(where, parts, other):
    _, rows, width = parts[0].shape
    return pl.pallas_call(
        arrive_kernel,
        in_specs=[SMEM] + [VMEM] * (len(parts) + 1),
        out_specs=VMEM,
        out_shape=jax.ShapeDtypeStruct((1, rows, 2 * len(parts) * width), parts[0].dtype),
        compiler_params=pltpu.CompilerParams(vmem_limit_bytes=SMALL_VMEM),
        name="arrive",
    )(where, *parts, other)


def down_kernel(core, *refs):
    *parts, hidden, hidden_other, up, out, back = refs

    @pl.when(pl.program_id(0) == 0)
    def _():
        total = parts[0][...].astype(jnp.float32)
        for part in parts[1:]:
            total += part[...].astype(jnp.float32)
        back[...] = total.astype(jnp.bfloat16)

    grad = dot(back[core[0]], hidden[...]) + dot(back[1 - core[0]], hidden_other[...])
    grad = grad.astype(out.dtype)
    for row in range(out.shape[0]):
        across = slice(row * SHARE_ROWS, (row + 1) * SHARE_ROWS)
        for column in range(out.shape[1]):
            out[row, column, :, :DOWN_COLS] = grad[
                across, column * DOWN_COLS : (column + 1) * DOWN_COLS
            ]
            out[row, column, :, DOWN_COLS:] = up[across, column * 128 : (column + 1) * 128]


def down_gradient(core, parts, hidden, hidden_other, up):
    rows, half = hidden_other.shape
    steps = 2
    step = half // steps
    columns = half // DOWN_COLS
    across = 2 * RANK // SHARE_ROWS
    shape = parts[0].shape
    return pl.pallas_call(
        down_kernel,
        grid_spec=pltpu.PrefetchScalarGridSpec(
            num_scalar_prefetch=1,
            grid=(steps,),
            in_specs=[pl.BlockSpec(shape, lambda i, core: (0, 0, 0))] * len(parts)
            + [
                pl.BlockSpec((rows, step), lambda i, core: (0, core[0] * steps + i)),
                pl.BlockSpec((rows, step), lambda i, core: (0, i)),
                pl.BlockSpec((2 * RANK, columns // steps * 128), lambda i, core: (0, i)),
            ],
            out_specs=pl.BlockSpec(
                (across, columns // steps, SHARE_ROWS, DOWN_COLS + 128),
                lambda i, core: (0, i, 0, 0),
            ),
            scratch_shapes=[pltpu.VMEM(shape, jnp.bfloat16)],
        ),
        out_shape=jax.ShapeDtypeStruct(
            (across, columns, SHARE_ROWS, DOWN_COLS + 128), jnp.bfloat16
        ),
        compiler_params=pltpu.CompilerParams(vmem_limit_bytes=24 << 20),
        name="down_gradient",
    )(core, *parts, hidden, hidden_other, up)


def share_kernel(parts, *refs):
    out = refs[-1]
    total = parts[0].astype(jnp.float32)
    for part in range(1, parts.shape[0]):
        total += parts[part].astype(jnp.float32)
    total = total.astype(out.dtype)
    for part in range(out.shape[0]):
        out[part] = total


def sum_share(parts, after):
    return pl.pallas_call(
        share_kernel,
        in_specs=[VMEM] + [VMEM] * len(after),
        out_specs=VMEM,
        out_shape=jax.ShapeDtypeStruct(parts.shape, parts.dtype),
        compiler_params=pltpu.CompilerParams(vmem_limit_bytes=SMALL_VMEM),
        name="sum_share",
    )(parts, *after)


def place_kernel(which, shares, *refs):
    *outs, downs, ups, wide, sems = refs[-8:]
    which = which[0]
    half = shares.shape[0] // 2
    columns = shares.shape[1]
    copies = []

    def send(source, target, begin, size):
        begin = pl.multiple_of(begin, size)
        copies.append(
            pltpu.make_async_copy(source, target.at[:, pl.ds(begin, size)], sems.at[len(copies)])
        )
        copies[-1].start()

    for part in range(2):
        for row in range(half):
            across = slice(row * SHARE_ROWS, (row + 1) * SHARE_ROWS)
            for column in range(columns):
                share = shares[part * half + row, column]
                downs[part, across, column * DOWN_COLS : (column + 1) * DOWN_COLS] = share[
                    :, :DOWN_COLS
                ].astype(jnp.float32)
                wide[
                    part * RANK + row * SHARE_ROWS : part * RANK + (row + 1) * SHARE_ROWS,
                    column * 128 : (column + 1) * 128,
                ] = share[:, DOWN_COLS:]
        width = columns * DOWN_COLS
        send(downs.at[part], outs[2 * part], which * width, width)
    width = columns * UP_COLS
    source = lax.broadcasted_iota(jnp.int32, (columns * 128, width), 0)
    lane = lax.broadcasted_iota(jnp.int32, (columns * 128, width), 1)
    lane = (lane // UP_COLS) * 128 + lane % UP_COLS
    for chip in range(128 // UP_COLS):
        chosen = jnp.where(source == lane + chip * UP_COLS, 1.0, 0.0).astype(jnp.bfloat16)
        ups[chip] = dot(wide[...], chosen)
        for part in range(2):
            send(
                ups.at[chip, part * RANK : (part + 1) * RANK, :],
                outs[2 * part + 1],
                (2 * chip + which) * width,
                width,
            )
    for copy in copies:
        copy.wait()


def place(which, shares, model, width, earlier=(), after=()):
    shapes = [(RANK, model), (RANK, width), (RANK, model), (RANK, width)]
    columns = shares.shape[1]
    chips = 128 // UP_COLS
    return pl.pallas_call(
        place_kernel,
        in_specs=[SMEM, VMEM] + [ANY] * len(earlier) + [VMEM] * len(after),
        out_specs=[ANY] * 4,
        out_shape=[jax.ShapeDtypeStruct(shape, jnp.float32) for shape in shapes],
        scratch_shapes=[
            pltpu.VMEM((2, RANK, columns * DOWN_COLS), jnp.float32),
            pltpu.VMEM((chips, 2 * RANK, columns * UP_COLS), jnp.float32),
            pltpu.VMEM((2 * RANK, columns * 128), jnp.bfloat16),
            pltpu.SemaphoreType.DMA((2 + 2 * chips,)),
        ],
        input_output_aliases={2 + index: index for index in range(len(earlier))},
        compiler_params=pltpu.CompilerParams(vmem_limit_bytes=16 << 20),
        name="place",
    )(which[None], shares, *earlier, *after)


def swap(x, axes):
    return lax.all_to_all(x, axes, 0, 0, tiled=True)


def to_other_core(x):
    return lax.ppermute(x, "core", [(0, 1), (1, 0)])


def per_device(
    sizes,
    hidden,
    frozen_queries,
    frozen_keys,
    frozen_values,
    document_length_list,
    query_down_weight,
    query_up_weight,
    value_down_weight,
    value_up_weight,
    output_gradient,
):
    dp_size, seq_size = sizes
    chips = seq_size // 2
    rows, model = hidden.shape[1:]
    half = model // 2
    chip = lax.axis_index("y").astype(jnp.int32)
    core = lax.axis_index("core").astype(jnp.int32)
    where = jnp.stack([chip, core])

    def to_chip(x, step):
        return lax.ppermute(x, "y", [(c, (c + step) % chips) for c in range(chips)])

    packed = pack(
        hidden[0],
        query_down_weight.T,
        value_down_weight.T,
        frozen_queries[0],
        frozen_keys[0],
        frozen_values[0],
        output_gradient[0],
        query_up_weight,
        value_up_weight,
        seq_size,
    )
    received = swap(packed, SEQ).reshape(seq_size * rows, packed.shape[2])
    hidden_other = to_other_core(
        lax.dynamic_slice(hidden[0], (0, (1 - core) * half), (rows, half))
    )
    width = frozen_queries.shape[2] // seq_size
    own_columns = (0, (chip * 2 + core) * width)
    wq_up = lax.dynamic_slice(query_up_weight, own_columns, (RANK, width))
    wv_up = lax.dynamic_slice(value_up_weight, own_columns, (RANK, width))
    meta = jnp.concatenate([document_length_list[0], where])
    *outs, dq_t, dv_t, low = attention(meta, received, wq_up, wv_up, seq_size)
    parts, backs = outs[:chips], outs[chips:]

    backs = [backs[0]] + [to_chip(backs[step], step) for step in range(1, chips)]
    backs_other = [to_other_core(back) for back in backs]
    parts = [parts[0]] + [to_chip(parts[step], step) for step in range(1, chips)]
    up = up_gradient(where, low, dq_t, dv_t)
    down = down_gradient(core[None], backs + backs_other, hidden[0], hidden_other, up)

    shares = swap(down.reshape((-1,) + down.shape[2:]), PLANE)
    shares = swap(sum_share(shares, after=[parts[1], parts[3]]), PLANE).reshape(down.shape)
    attended = arrive(where, parts, to_other_core(pick(where, parts)))
    shares_other = to_other_core(shares)
    grads = place(core, shares, model, seq_size * width, after=[parts[2]])
    grad_a_q, up_q, grad_a_v, up_v = place(
        1 - core, shares_other, model, seq_size * width, earlier=grads
    )
    return attended, grad_a_q.T, up_q, grad_a_v.T, up_v


def solution(mesh):
    dp_size, seq_size = mesh.shape["dp"], mesh.shape["seq"]
    fine = Mesh(mesh.devices.reshape(4, 4, 4, 2), ALL)
    rows = P(DP, SEQ, None)
    in_specs = (rows, rows, rows, rows, P(DP, None), P(), P(), P(), P(), rows)
    out_specs = (rows, P(), P(), P(), P())
    return jax.shard_map(
        functools.partial(per_device, (dp_size, seq_size)),
        mesh=fine,
        in_specs=in_specs,
        out_specs=out_specs,
        check_vma=False,
    )
```

```python
import functools

import jax
import jax.numpy as jnp
from jax import lax
from jax.experimental import pallas as pl
from jax.experimental.pallas import tpu as pltpu
from jax.sharding import Mesh
from jax.sharding import PartitionSpec as P

HEAD_COUNT = 16
HEAD_SIZE = 128
RANK = 64
NDOC = 8
TILE = 256
MAX_TILES = 5
ADAPTER_SCALE = 2.0
NEG_FILL = -1e30
SCALING = HEAD_SIZE ** (-0.5)
LOG2_E = 1.4426950408889634

SHARE_ROWS = 16
DOWN_COLS = 256
UP_COLS = 32

DP = ("x", "z")
SEQ = ("y", "core")
PLANE = ("x", "z", "y")
ALL = ("x", "z", "y", "core")
NT = (((1,), (1,)), ((), ()))


def dot(a, b):
    return jnp.dot(a, b, preferred_element_type=jnp.float32)


def dot_nt(a, b):
    return lax.dot_general(a, b, NT, preferred_element_type=jnp.float32)


HIDDEN_PARTS = 4
PACK_VMEM = 56 << 20
SMALL_VMEM = 8 << 20
VMEM = pl.BlockSpec(memory_space=pltpu.VMEM)
SMEM = pl.BlockSpec(memory_space=pltpu.SMEM)
ANY = pl.BlockSpec(memory_space=pl.ANY)


def pack_kernel(
    hidden, wq_down, wv_down, fq, fk, fv, grad, wq_up, wv_up, out,
    hidden_v, wq_down_v, wv_down_v, fq_v, fv_v, wq_up_v, wv_up_v, out_v, low,
    down_sems, hidden_sems, row_sems, through_sems, out_sems,
):
    devices, rows, packed = out.shape
    width = (packed - 2 * RANK) // 4
    model = hidden.shape[1]
    step = model // HIDDEN_PARTS

    def part(index):
        return pl.ds(index * step, step)

    def columns(index):
        return pl.ds(index * width, width)

    downs = [
        pltpu.make_async_copy(wq_down, wq_down_v, down_sems.at[0]),
        pltpu.make_async_copy(wv_down, wv_down_v, down_sems.at[1]),
    ]
    hiddens = [
        pltpu.make_async_copy(
            hidden.at[:, part(index)], hidden_v.at[:, part(index)], hidden_sems.at[index]
        )
        for index in range(HIDDEN_PARTS)
    ]
    whole = [
        pltpu.make_async_copy(wq_up, wq_up_v, row_sems.at[0]),
        pltpu.make_async_copy(fq, fq_v, row_sems.at[1]),
        pltpu.make_async_copy(wv_up, wv_up_v, row_sems.at[2]),
        pltpu.make_async_copy(fv, fv_v, row_sems.at[3]),
    ]
    through = []
    for device in range(devices):
        for which, source in ((1, fk), (3, grad)):
            through.append(
                pltpu.make_async_copy(
                    source.at[:, columns(device)],
                    out_v.at[device, :, columns(which)],
                    through_sems.at[len(through)],
                )
            )
    for copy in downs + hiddens + whole + through:
        copy.start()

    for copy in downs:
        copy.wait()
    low_q = jnp.zeros((rows, RANK), jnp.float32)
    low_v = jnp.zeros((rows, RANK), jnp.float32)
    for index in range(HIDDEN_PARTS):
        hiddens[index].wait()
        low_q += dot_nt(hidden_v[:, part(index)], wq_down_v[:, part(index)])
        low_v += dot_nt(hidden_v[:, part(index)], wv_down_v[:, part(index)])
    low[:, :RANK] = low_q.astype(jnp.bfloat16)
    low[:, RANK:] = low_v.astype(jnp.bfloat16)

    for copy in whole:
        copy.wait()
    outs = []
    for device in range(devices):
        at = slice(device * width, (device + 1) * width)
        for which, (frozen, weight, begin) in enumerate(
            ((fq_v, wq_up_v, 0), (fv_v, wv_up_v, RANK))
        ):
            added = ADAPTER_SCALE * dot(low[:, begin : begin + RANK], weight[:, at])
            out_v[device, :, 2 * which * width : (2 * which + 1) * width] = (
                frozen[:, at].astype(jnp.float32) + added
            ).astype(jnp.bfloat16)
        out_v[device, :, 4 * width :] = low[...]
        through[2 * device].wait()
        through[2 * device + 1].wait()
        outs.append(pltpu.make_async_copy(out_v.at[device], out.at[device], out_sems.at[device]))
        outs[-1].start()
    for copy in outs:
        copy.wait()


def pack(hidden, wq_down_t, wv_down_t, fq, fk, fv, grad, wq_up, wv_up, seq_size):
    rows, model = hidden.shape
    columns = fq.shape[1]
    width = columns // seq_size
    bf16 = jnp.bfloat16
    return pl.pallas_call(
        pack_kernel,
        in_specs=[ANY] * 9,
        out_specs=ANY,
        out_shape=jax.ShapeDtypeStruct((seq_size, rows, 4 * width + 2 * RANK), bf16),
        scratch_shapes=[
            pltpu.VMEM((rows, model), bf16),
            pltpu.VMEM((RANK, model), bf16),
            pltpu.VMEM((RANK, model), bf16),
            pltpu.VMEM((rows, columns), bf16),
            pltpu.VMEM((rows, columns), bf16),
            pltpu.VMEM((RANK, columns), bf16),
            pltpu.VMEM((RANK, columns), bf16),
            pltpu.VMEM((seq_size, rows, 4 * width + 2 * RANK), bf16),
            pltpu.VMEM((rows, 2 * RANK), bf16),
            pltpu.SemaphoreType.DMA((2,)),
            pltpu.SemaphoreType.DMA((HIDDEN_PARTS,)),
            pltpu.SemaphoreType.DMA((4,)),
            pltpu.SemaphoreType.DMA((2 * seq_size,)),
            pltpu.SemaphoreType.DMA((seq_size,)),
        ],
        compiler_params=pltpu.CompilerParams(vmem_limit_bytes=PACK_VMEM),
        name="pack",
    )(hidden, wq_down_t, wv_down_t, fq, fk, fv, grad, wq_up, wv_up)


def attention_kernel(
    meta, packed, wq_up, wv_up, *refs
):
    *outs, dq_t, dv_t, low, q_t, k_t, v_t, g_t, dv, returned, out = refs[1:]
    outs, backs = outs[: len(outs) // 2], outs[len(outs) // 2 :]
    length = packed.shape[0]
    heads = out.shape[1] // HEAD_SIZE
    width = heads * HEAD_SIZE
    blocks = length // TILE
    chip = meta[NDOC]
    span = [slice(head * HEAD_SIZE, (head + 1) * HEAD_SIZE) for head in range(heads)]

    def columns(which, head):
        begin = which * width + head * HEAD_SIZE
        return slice(begin, begin + HEAD_SIZE)

    for head in range(heads):
        q_t[span[head], :] = packed[:, columns(0, head)].T
        k_t[span[head], :] = packed[:, columns(1, head)].T
        v_t[span[head], :] = packed[:, columns(2, head)].T
        g_t[span[head], :] = packed[:, columns(3, head)].T
    dv[...] = jnp.zeros_like(dv)

    def block(index, _):
        row0 = pl.multiple_of(index * TILE, TILE)
        q_rows = pl.ds(row0, TILE)
        position = row0 + lax.broadcasted_iota(jnp.int32, (1, TILE), 1)
        begin = jnp.zeros((1, TILE), jnp.int32)
        first = jnp.int32(0)
        end = jnp.int32(0)
        for doc in range(NDOC):
            end = end + meta[doc]
            begin = jnp.where(position >= end, end, begin)
            first = jnp.where(row0 >= end, end, first)
        tiles = index - lax.div(first, TILE) + 1

        def body(count):
            key0 = pl.multiple_of((index + 1 - count) * TILE, TILE)
            k_rows = pl.ds(key0, count * TILE)
            key_index = lax.broadcasted_iota(jnp.int32, (count * TILE, TILE), 0)
            in_document = key_index >= begin - key0
            causal = lax.broadcasted_iota(jnp.int32, (TILE, TILE), 0) <= (
                lax.broadcasted_iota(jnp.int32, (TILE, TILE), 1)
            )
            held = []
            for head in range(heads):
                scores = dot(packed[k_rows, columns(1, head)], q_t[span[head], q_rows])
                prob_grad = dot(packed[k_rows, columns(2, head)], g_t[span[head], q_rows])
                scores = jnp.where(in_document, scores, NEG_FILL)
                last = jnp.where(causal, scores[(count - 1) * TILE :], NEG_FILL)
                if count > 1:
                    scores = jnp.concatenate([scores[: (count - 1) * TILE], last], axis=0)
                else:
                    scores = last
                maximum = jnp.max(scores, axis=0, keepdims=True)
                powers = jnp.exp2((scores - maximum) * (SCALING * LOG2_E))
                inverse = 1.0 / jnp.sum(powers, axis=0, keepdims=True)
                held.append((prob_grad, powers.astype(jnp.bfloat16), inverse))
            for head in range(heads):
                prob_grad, rounded, inverse = held[head]
                result = (dot(v_t[span[head], k_rows], rounded) * inverse).astype(jnp.bfloat16)
                g_wide = g_t[span[head], q_rows].astype(jnp.float32)
                row_dot = jnp.sum(g_wide * result.astype(jnp.float32), axis=0, keepdims=True)
                score_grad = rounded * (prob_grad - row_dot).astype(jnp.bfloat16)
                query_grad = dot(k_t[span[head], k_rows], score_grad) * (inverse * SCALING)
                dq_t[span[head], q_rows] = query_grad.astype(jnp.bfloat16)
                out[q_rows, span[head]] = result.T
                g_scaled = (g_wide * inverse).astype(jnp.bfloat16).T
                dv[head, k_rows, :] += dot(rounded, g_scaled)

        for count in range(1, min(MAX_TILES, blocks) + 1):
            pl.when(tiles == count)(functools.partial(body, count))
        return 0

    lax.fori_loop(0, blocks, block, 0)
    for head in range(heads):
        dv_t[span[head], :] = dv[head].astype(jnp.bfloat16).T

    for part, (grads, weight) in enumerate(((dq_t, wq_up), (dv_t, wv_up))):
        returned[part * RANK : (part + 1) * RANK, :] = (
            ADAPTER_SCALE * dot(weight[...], grads[...])
        ).astype(jnp.bfloat16)
    low[...] = packed[:, 4 * width :]
    rows = backs[0].shape[2]
    for step in range(len(backs)):
        target = lax.rem(chip + step, len(backs))
        for holder in range(2):
            begin = pl.multiple_of((target * 2 + holder) * rows, rows)
            backs[step][holder] = returned[:, pl.ds(begin, rows)]
            outs[step][holder] = out[pl.ds(begin, rows), :]


def attention(meta, packed, wq_up, wv_up, seq_size, after):
    length = packed.shape[0]
    width = (packed.shape[1] - 2 * RANK) // 4
    rows = length // seq_size
    heads = width // HEAD_SIZE
    chips = seq_size // 2
    wide_t = pltpu.VMEM((width, length), jnp.bfloat16)
    back = jax.ShapeDtypeStruct((2, 2 * RANK, rows), jnp.bfloat16)
    grad_t = jax.ShapeDtypeStruct((width, length), jnp.bfloat16)
    return pl.pallas_call(
        attention_kernel,
        in_specs=[SMEM, VMEM, VMEM, VMEM, VMEM],
        out_specs=[VMEM] * (3 + 2 * chips),
        scratch_shapes=[
            wide_t,
            wide_t,
            wide_t,
            wide_t,
            pltpu.VMEM((heads, length, HEAD_SIZE), jnp.float32),
            pltpu.VMEM((2 * RANK, length), jnp.bfloat16),
            pltpu.VMEM((length, width), jnp.bfloat16),
        ],
        out_shape=[jax.ShapeDtypeStruct((2, rows, width), jnp.bfloat16)] * chips
        + [back] * chips
        + [grad_t, grad_t, jax.ShapeDtypeStruct((length, 2 * RANK), jnp.bfloat16)],
        compiler_params=pltpu.CompilerParams(vmem_limit_bytes=40 << 20),
        cost_estimate=pl.CostEstimate(
            flops=8 << 30, bytes_accessed=16 << 20, transcendentals=4 << 20
        ),
        name="attention",
    )(meta, packed, wq_up, wv_up, after)


def up_kernel(where, low, dq_t, dv_t, *refs):
    up = refs[len(refs) // 2]
    width = dq_t.shape[0]
    lane = lax.broadcasted_iota(jnp.int32, (width, up.shape[1]), 1)
    source = lax.broadcasted_iota(jnp.int32, (width, up.shape[1]), 0)
    mine = (source == (lane // 128) * UP_COLS + lane % UP_COLS) & (
        (lane % 128) // UP_COLS == where[0]
    )
    mine = jnp.where(mine, 1.0, 0.0).astype(jnp.bfloat16)
    for part, grads in enumerate((dq_t, dv_t)):
        share = (dot(grads[...], low[...]) * ADAPTER_SCALE).T[part * RANK : (part + 1) * RANK, :]
        up[part * RANK : (part + 1) * RANK, :] = dot(share.astype(jnp.bfloat16), mine).astype(
            jnp.bfloat16
        )


def up_gradient(where, low, dq_t, dv_t, held):
    width = dq_t.shape[0]
    return pl.pallas_call(
        up_kernel,
        in_specs=[SMEM] + [VMEM] * (3 + len(held)),
        out_specs=[VMEM] * (1 + len(held)),
        out_shape=[jax.ShapeDtypeStruct((2 * RANK, width // UP_COLS * 128), jnp.bfloat16)]
        + [jax.ShapeDtypeStruct(part.shape, part.dtype) for part in held],
        input_output_aliases={4 + index: 1 + index for index in range(len(held))},
        compiler_params=pltpu.CompilerParams(vmem_limit_bytes=16 << 20),
        name="up_gradient",
    )(where, low, dq_t, dv_t, *held)


def pick_kernel(where, part_0, part_1, part_2, part_3, out):
    core = where[1]
    for step, part in enumerate((part_0, part_1, part_2, part_3)):
        out[step] = part[1 - core]


def pick(where, parts):
    return pl.pallas_call(
        pick_kernel,
        in_specs=[SMEM] + [VMEM] * len(parts),
        out_specs=VMEM,
        out_shape=jax.ShapeDtypeStruct((len(parts),) + parts[0].shape[1:], parts[0].dtype),
        compiler_params=pltpu.CompilerParams(vmem_limit_bytes=SMALL_VMEM),
        name="pick",
    )(where, *parts)


def arrive_kernel(where, part_0, part_1, part_2, part_3, other, out):
    chip, core = where[0], where[1]
    parts = (part_0, part_1, part_2, part_3)
    width = part_0.shape[2]
    for step in range(len(parts)):
        origin = lax.rem(chip + len(parts) - step, len(parts))
        here = pl.multiple_of((origin * 2 + core) * width, width)
        there = pl.multiple_of((origin * 2 + 1 - core) * width, width)
        out[0, :, pl.ds(here, width)] = parts[step][core]
        out[0, :, pl.ds(there, width)] = other[step]


def arrive(where, parts, other):
    _, rows, width = parts[0].shape
    return pl.pallas_call(
        arrive_kernel,
        in_specs=[SMEM] + [VMEM] * (len(parts) + 1),
        out_specs=VMEM,
        out_shape=jax.ShapeDtypeStruct((1, rows, 2 * len(parts) * width), parts[0].dtype),
        compiler_params=pltpu.CompilerParams(vmem_limit_bytes=SMALL_VMEM),
        name="arrive",
    )(where, *parts, other)


def down_kernel(core, *refs):
    parts, (hidden, hidden_other, up) = refs[:8], refs[8:11]
    out, back = refs[-2:]

    @pl.when(pl.program_id(0) == 0)
    def _():
        total = parts[0][...].astype(jnp.float32)
        for part in parts[1:]:
            total += part[...].astype(jnp.float32)
        back[...] = total.astype(jnp.bfloat16)

    grad = dot(back[core[0]], hidden[...]) + dot(back[1 - core[0]], hidden_other[...])
    grad = grad.astype(out.dtype)
    for row in range(out.shape[0]):
        across = slice(row * SHARE_ROWS, (row + 1) * SHARE_ROWS)
        for column in range(out.shape[1]):
            out[row, column, :, :DOWN_COLS] = grad[
                across, column * DOWN_COLS : (column + 1) * DOWN_COLS
            ]
            out[row, column, :, DOWN_COLS:] = up[across, column * 128 : (column + 1) * 128]


def down_gradient(core, parts, hidden, hidden_other, up, after):
    rows, half = hidden_other.shape
    steps = 2
    step = half // steps
    columns = half // DOWN_COLS
    across = 2 * RANK // SHARE_ROWS
    shape = parts[0].shape
    return pl.pallas_call(
        down_kernel,
        grid_spec=pltpu.PrefetchScalarGridSpec(
            num_scalar_prefetch=1,
            grid=(steps,),
            in_specs=[pl.BlockSpec(shape, lambda i, core: (0, 0, 0))] * len(parts)
            + [
                pl.BlockSpec((rows, step), lambda i, core: (0, core[0] * steps + i)),
                pl.BlockSpec((rows, step), lambda i, core: (0, i)),
                pl.BlockSpec((2 * RANK, columns // steps * 128), lambda i, core: (0, i)),
            ]
            + [VMEM] * len(after),
            out_specs=pl.BlockSpec(
                (across, columns // steps, SHARE_ROWS, DOWN_COLS + 128),
                lambda i, core: (0, i, 0, 0),
            ),
            scratch_shapes=[pltpu.VMEM(shape, jnp.bfloat16)],
        ),
        out_shape=jax.ShapeDtypeStruct(
            (across, columns, SHARE_ROWS, DOWN_COLS + 128), jnp.bfloat16
        ),
        compiler_params=pltpu.CompilerParams(vmem_limit_bytes=24 << 20),
        name="down_gradient",
    )(core, *parts, hidden, hidden_other, up, *after)


def share_kernel(parts, *refs):
    out = refs[-1]
    total = parts[0].astype(jnp.float32)
    for part in range(1, parts.shape[0]):
        total += parts[part].astype(jnp.float32)
    total = total.astype(out.dtype)
    for part in range(out.shape[0]):
        out[part] = total


def sum_share(parts, after):
    return pl.pallas_call(
        share_kernel,
        in_specs=[VMEM] + [VMEM] * len(after),
        out_specs=VMEM,
        out_shape=jax.ShapeDtypeStruct(parts.shape, parts.dtype),
        compiler_params=pltpu.CompilerParams(vmem_limit_bytes=SMALL_VMEM),
        name="sum_share",
    )(parts, *after)


def place_kernel(which, shares, *refs):
    *outs, downs, ups, wide, sems = refs[-8:]
    which = which[0]
    half = shares.shape[0] // 2
    columns = shares.shape[1]
    copies = []

    def send(source, target, begin, size):
        begin = pl.multiple_of(begin, size)
        copies.append(
            pltpu.make_async_copy(source, target.at[:, pl.ds(begin, size)], sems.at[len(copies)])
        )
        copies[-1].start()

    for part in range(2):
        for row in range(half):
            across = slice(row * SHARE_ROWS, (row + 1) * SHARE_ROWS)
            for column in range(columns):
                share = shares[part * half + row, column]
                downs[part, across, column * DOWN_COLS : (column + 1) * DOWN_COLS] = share[
                    :, :DOWN_COLS
                ].astype(jnp.float32)
                wide[
                    part * RANK + row * SHARE_ROWS : part * RANK + (row + 1) * SHARE_ROWS,
                    column * 128 : (column + 1) * 128,
                ] = share[:, DOWN_COLS:]
        width = columns * DOWN_COLS
        send(downs.at[part], outs[2 * part], which * width, width)
    width = columns * UP_COLS
    source = lax.broadcasted_iota(jnp.int32, (columns * 128, width), 0)
    lane = lax.broadcasted_iota(jnp.int32, (columns * 128, width), 1)
    lane = (lane // UP_COLS) * 128 + lane % UP_COLS
    for chip in range(128 // UP_COLS):
        chosen = jnp.where(source == lane + chip * UP_COLS, 1.0, 0.0).astype(jnp.bfloat16)
        ups[chip] = dot(wide[...], chosen)
        for part in range(2):
            send(
                ups.at[chip, part * RANK : (part + 1) * RANK, :],
                outs[2 * part + 1],
                (2 * chip + which) * width,
                width,
            )
    for copy in copies:
        copy.wait()


def place(which, shares, model, width, earlier=()):
    shapes = [(RANK, model), (RANK, width), (RANK, model), (RANK, width)]
    columns = shares.shape[1]
    chips = 128 // UP_COLS
    return pl.pallas_call(
        place_kernel,
        in_specs=[SMEM, VMEM] + [ANY] * len(earlier),
        out_specs=[ANY] * 4,
        out_shape=[jax.ShapeDtypeStruct(shape, jnp.float32) for shape in shapes],
        scratch_shapes=[
            pltpu.VMEM((2, RANK, columns * DOWN_COLS), jnp.float32),
            pltpu.VMEM((chips, 2 * RANK, columns * UP_COLS), jnp.float32),
            pltpu.VMEM((2 * RANK, columns * 128), jnp.bfloat16),
            pltpu.SemaphoreType.DMA((2 + 2 * chips,)),
        ],
        input_output_aliases={2 + index: index for index in range(len(earlier))},
        compiler_params=pltpu.CompilerParams(vmem_limit_bytes=16 << 20),
        name="place",
    )(which[None], shares, *earlier)


def swap(x, axes):
    return lax.all_to_all(x, axes, 0, 0, tiled=True)


def to_other_core(x):
    return lax.ppermute(x, "core", [(0, 1), (1, 0)])


def per_device(
    sizes,
    hidden,
    frozen_queries,
    frozen_keys,
    frozen_values,
    document_length_list,
    query_down_weight,
    query_up_weight,
    value_down_weight,
    value_up_weight,
    output_gradient,
):
    dp_size, seq_size = sizes
    chips = seq_size // 2
    rows, model = hidden.shape[1:]
    half = model // 2
    chip = lax.axis_index("y").astype(jnp.int32)
    core = lax.axis_index("core").astype(jnp.int32)
    where = jnp.stack([chip, core])

    def to_chip(x, step):
        return lax.ppermute(x, "y", [(c, (c + step) % chips) for c in range(chips)])

    packed = pack(
        hidden[0],
        query_down_weight.T,
        value_down_weight.T,
        frozen_queries[0],
        frozen_keys[0],
        frozen_values[0],
        output_gradient[0],
        query_up_weight,
        value_up_weight,
        seq_size,
    )
    received = swap(packed, SEQ).reshape(seq_size * rows, packed.shape[2])
    hidden_other = to_other_core(
        lax.dynamic_slice(hidden[0], (0, (1 - core) * half), (rows, half))
    )
    width = frozen_queries.shape[2] // seq_size
    own_columns = (0, (chip * 2 + core) * width)
    wq_up = lax.dynamic_slice(query_up_weight, own_columns, (RANK, width))
    wv_up = lax.dynamic_slice(value_up_weight, own_columns, (RANK, width))
    meta = jnp.concatenate([document_length_list[0], where])
    *outs, dq_t, dv_t, low = attention(
        meta, received, wq_up, wv_up, seq_size, after=hidden_other
    )
    parts, backs = outs[:chips], outs[chips:]

    backs = [backs[0]] + [to_chip(backs[step], step) for step in range(1, chips)]
    backs_other = [to_other_core(back) for back in backs]
    up, *held = up_gradient(where, low, dq_t, dv_t, parts[1:])
    parts = [parts[0]] + [to_chip(held[step - 1], step) for step in range(1, chips)]
    down = down_gradient(
        core[None],
        backs + backs_other,
        hidden[0],
        hidden_other,
        up,
        after=[parts[1], parts[3]],
    )

    shares = swap(down.reshape((-1,) + down.shape[2:]), PLANE)
    shares = swap(sum_share(shares, after=[parts[2]]), PLANE).reshape(down.shape)
    attended = arrive(where, parts, to_other_core(pick(where, parts)))
    shares_other = to_other_core(shares)
    grads = place(core, shares, model, seq_size * width)
    grad_a_q, up_q, grad_a_v, up_v = place(
        1 - core, shares_other, model, seq_size * width, earlier=grads
    )
    return attended, grad_a_q.T, up_q, grad_a_v.T, up_v


def solution(mesh):
    dp_size, seq_size = mesh.shape["dp"], mesh.shape["seq"]
    fine = Mesh(mesh.devices.reshape(4, 4, 4, 2), ALL)
    rows = P(DP, SEQ, None)
    in_specs = (rows, rows, rows, rows, P(DP, None), P(), P(), P(), P(), rows)
    out_specs = (rows, P(), P(), P(), P())
    return jax.shard_map(
        functools.partial(per_device, (dp_size, seq_size)),
        mesh=fine,
        in_specs=in_specs,
        out_specs=out_specs,
        check_vma=False,
    )
```

```python
import functools

import jax
import jax.numpy as jnp
from jax import lax
from jax.experimental import pallas as pl
from jax.experimental.pallas import tpu as pltpu
from jax.sharding import Mesh
from jax.sharding import PartitionSpec as P

HEAD_COUNT = 16
HEAD_SIZE = 128
RANK = 64
NDOC = 8
TILE = 256
MAX_TILES = 5
ADAPTER_SCALE = 2.0
NEG_FILL = -1e30
SCALING = HEAD_SIZE ** (-0.5)
LOG2_E = 1.4426950408889634

SHARE_ROWS = 16
DOWN_COLS = 1024
UP_COLS = 128

DP = ("x", "z")
SEQ = ("y", "core")
ALL = ("x", "z", "y", "core")
NT = (((1,), (1,)), ((), ()))


def dot(a, b):
    return jnp.dot(a, b, preferred_element_type=jnp.float32)


def dot_nt(a, b):
    return lax.dot_general(a, b, NT, preferred_element_type=jnp.float32)


HIDDEN_PARTS = 4
PACK_VMEM = 56 << 20
SMALL_VMEM = 8 << 20
VMEM = pl.BlockSpec(memory_space=pltpu.VMEM)
SMEM = pl.BlockSpec(memory_space=pltpu.SMEM)
ANY = pl.BlockSpec(memory_space=pl.ANY)


def pack_kernel(
    hidden, wq_down, wv_down, fq, fk, fv, grad, wq_up, wv_up, out,
    hidden_v, wq_down_v, wv_down_v, fq_v, fv_v, wq_up_v, wv_up_v, out_v, low,
    down_sems, hidden_sems, row_sems, through_sems, out_sems,
):
    devices, rows, packed = out.shape
    width = (packed - 2 * RANK) // 4
    model = hidden.shape[1]
    step = model // HIDDEN_PARTS

    def part(index):
        return pl.ds(index * step, step)

    def columns(index):
        return pl.ds(index * width, width)

    downs = [
        pltpu.make_async_copy(wq_down, wq_down_v, down_sems.at[0]),
        pltpu.make_async_copy(wv_down, wv_down_v, down_sems.at[1]),
    ]
    hiddens = [
        pltpu.make_async_copy(
            hidden.at[:, part(index)], hidden_v.at[:, part(index)], hidden_sems.at[index]
        )
        for index in range(HIDDEN_PARTS)
    ]
    whole = [
        pltpu.make_async_copy(wq_up, wq_up_v, row_sems.at[0]),
        pltpu.make_async_copy(fq, fq_v, row_sems.at[1]),
        pltpu.make_async_copy(wv_up, wv_up_v, row_sems.at[2]),
        pltpu.make_async_copy(fv, fv_v, row_sems.at[3]),
    ]
    through = []
    for device in range(devices):
        for which, source in ((1, fk), (3, grad)):
            through.append(
                pltpu.make_async_copy(
                    source.at[:, columns(device)],
                    out_v.at[device, :, columns(which)],
                    through_sems.at[len(through)],
                )
            )
    for copy in downs + hiddens + whole + through:
        copy.start()

    for copy in downs:
        copy.wait()
    low_q = jnp.zeros((rows, RANK), jnp.float32)
    low_v = jnp.zeros((rows, RANK), jnp.float32)
    for index in range(HIDDEN_PARTS):
        hiddens[index].wait()
        low_q += dot_nt(hidden_v[:, part(index)], wq_down_v[:, part(index)])
        low_v += dot_nt(hidden_v[:, part(index)], wv_down_v[:, part(index)])
    low[:, :RANK] = low_q.astype(jnp.bfloat16)
    low[:, RANK:] = low_v.astype(jnp.bfloat16)

    for copy in whole:
        copy.wait()
    outs = []
    for device in range(devices):
        at = slice(device * width, (device + 1) * width)
        for which, (frozen, weight, begin) in enumerate(
            ((fq_v, wq_up_v, 0), (fv_v, wv_up_v, RANK))
        ):
            added = ADAPTER_SCALE * dot(low[:, begin : begin + RANK], weight[:, at])
            out_v[device, :, 2 * which * width : (2 * which + 1) * width] = (
                frozen[:, at].astype(jnp.float32) + added
            ).astype(jnp.bfloat16)
        out_v[device, :, 4 * width :] = low[...]
        through[2 * device].wait()
        through[2 * device + 1].wait()
        outs.append(pltpu.make_async_copy(out_v.at[device], out.at[device], out_sems.at[device]))
        outs[-1].start()
    for copy in outs:
        copy.wait()


def pack(hidden, wq_down_t, wv_down_t, fq, fk, fv, grad, wq_up, wv_up, seq_size):
    rows, model = hidden.shape
    columns = fq.shape[1]
    width = columns // seq_size
    bf16 = jnp.bfloat16
    return pl.pallas_call(
        pack_kernel,
        in_specs=[ANY] * 9,
        out_specs=ANY,
        out_shape=jax.ShapeDtypeStruct((seq_size, rows, 4 * width + 2 * RANK), bf16),
        scratch_shapes=[
            pltpu.VMEM((rows, model), bf16),
            pltpu.VMEM((RANK, model), bf16),
            pltpu.VMEM((RANK, model), bf16),
            pltpu.VMEM((rows, columns), bf16),
            pltpu.VMEM((rows, columns), bf16),
            pltpu.VMEM((RANK, columns), bf16),
            pltpu.VMEM((RANK, columns), bf16),
            pltpu.VMEM((seq_size, rows, 4 * width + 2 * RANK), bf16),
            pltpu.VMEM((rows, 2 * RANK), bf16),
            pltpu.SemaphoreType.DMA((2,)),
            pltpu.SemaphoreType.DMA((HIDDEN_PARTS,)),
            pltpu.SemaphoreType.DMA((4,)),
            pltpu.SemaphoreType.DMA((2 * seq_size,)),
            pltpu.SemaphoreType.DMA((seq_size,)),
        ],
        compiler_params=pltpu.CompilerParams(vmem_limit_bytes=PACK_VMEM),
        name="pack",
    )(hidden, wq_down_t, wv_down_t, fq, fk, fv, grad, wq_up, wv_up)


def attention_kernel(
    meta, packed, wq_up, wv_up, *refs
):
    *outs, dq_t, dv_t, low, q_t, k_t, v_t, g_t, dv, returned, out = refs
    outs, backs = outs[: len(outs) // 2], outs[len(outs) // 2 :]
    length = packed.shape[0]
    heads = out.shape[1] // HEAD_SIZE
    width = heads * HEAD_SIZE
    blocks = length // TILE
    chip = meta[NDOC]
    span = [slice(head * HEAD_SIZE, (head + 1) * HEAD_SIZE) for head in range(heads)]

    def columns(which, head):
        begin = which * width + head * HEAD_SIZE
        return slice(begin, begin + HEAD_SIZE)

    for head in range(heads):
        q_t[span[head], :] = packed[:, columns(0, head)].T
        k_t[span[head], :] = packed[:, columns(1, head)].T
        v_t[span[head], :] = packed[:, columns(2, head)].T
        g_t[span[head], :] = packed[:, columns(3, head)].T
    dv[...] = jnp.zeros_like(dv)

    def block(index, _):
        row0 = pl.multiple_of(index * TILE, TILE)
        q_rows = pl.ds(row0, TILE)
        position = row0 + lax.broadcasted_iota(jnp.int32, (1, TILE), 1)
        begin = jnp.zeros((1, TILE), jnp.int32)
        first = jnp.int32(0)
        end = jnp.int32(0)
        for doc in range(NDOC):
            end = end + meta[doc]
            begin = jnp.where(position >= end, end, begin)
            first = jnp.where(row0 >= end, end, first)
        tiles = index - lax.div(first, TILE) + 1

        def body(count):
            key0 = pl.multiple_of((index + 1 - count) * TILE, TILE)
            k_rows = pl.ds(key0, count * TILE)
            key_index = lax.broadcasted_iota(jnp.int32, (count * TILE, TILE), 0)
            in_document = key_index >= begin - key0
            causal = lax.broadcasted_iota(jnp.int32, (TILE, TILE), 0) <= (
                lax.broadcasted_iota(jnp.int32, (TILE, TILE), 1)
            )
            held = []
            for head in range(heads):
                scores = dot(packed[k_rows, columns(1, head)], q_t[span[head], q_rows])
                prob_grad = dot(packed[k_rows, columns(2, head)], g_t[span[head], q_rows])
                scores = jnp.where(in_document, scores, NEG_FILL)
                last = jnp.where(causal, scores[(count - 1) * TILE :], NEG_FILL)
                if count > 1:
                    scores = jnp.concatenate([scores[: (count - 1) * TILE], last], axis=0)
                else:
                    scores = last
                maximum = jnp.max(scores, axis=0, keepdims=True)
                powers = jnp.exp2((scores - maximum) * (SCALING * LOG2_E))
                inverse = 1.0 / jnp.sum(powers, axis=0, keepdims=True)
                held.append((prob_grad, powers.astype(jnp.bfloat16), inverse))
            for head in range(heads):
                prob_grad, rounded, inverse = held[head]
                result = (dot(v_t[span[head], k_rows], rounded) * inverse).astype(jnp.bfloat16)
                g_wide = g_t[span[head], q_rows].astype(jnp.float32)
                row_dot = jnp.sum(g_wide * result.astype(jnp.float32), axis=0, keepdims=True)
                score_grad = rounded * (prob_grad - row_dot).astype(jnp.bfloat16)
                query_grad = dot(k_t[span[head], k_rows], score_grad) * (inverse * SCALING)
                dq_t[span[head], q_rows] = query_grad.astype(jnp.bfloat16)
                out[q_rows, span[head]] = result.T
                g_scaled = (g_wide * inverse).astype(jnp.bfloat16).T
                dv[head, k_rows, :] += dot(rounded, g_scaled)

        for count in range(1, min(MAX_TILES, blocks) + 1):
            pl.when(tiles == count)(functools.partial(body, count))
        return 0

    lax.fori_loop(0, blocks, block, 0)
    for head in range(heads):
        dv_t[span[head], :] = dv[head].astype(jnp.bfloat16).T

    for part, (grads, weight) in enumerate(((dq_t, wq_up), (dv_t, wv_up))):
        returned[part * RANK : (part + 1) * RANK, :] = (
            ADAPTER_SCALE * dot(weight[...], grads[...])
        ).astype(jnp.bfloat16)
    low[...] = packed[:, 4 * width :]
    rows = backs[0].shape[2]
    for step in range(len(backs)):
        target = lax.rem(chip + step, len(backs))
        for holder in range(2):
            begin = pl.multiple_of((target * 2 + holder) * rows, rows)
            backs[step][holder] = returned[:, pl.ds(begin, rows)]
            outs[step][holder] = out[pl.ds(begin, rows), :]


def attention(meta, packed, wq_up, wv_up, seq_size):
    length = packed.shape[0]
    width = (packed.shape[1] - 2 * RANK) // 4
    rows = length // seq_size
    heads = width // HEAD_SIZE
    chips = seq_size // 2
    wide_t = pltpu.VMEM((width, length), jnp.bfloat16)
    back = jax.ShapeDtypeStruct((2, 2 * RANK, rows), jnp.bfloat16)
    grad_t = jax.ShapeDtypeStruct((width, length), jnp.bfloat16)
    return pl.pallas_call(
        attention_kernel,
        in_specs=[SMEM, VMEM, VMEM, VMEM],
        out_specs=[VMEM] * (3 + 2 * chips),
        scratch_shapes=[
            wide_t,
            wide_t,
            wide_t,
            wide_t,
            pltpu.VMEM((heads, length, HEAD_SIZE), jnp.float32),
            pltpu.VMEM((2 * RANK, length), jnp.bfloat16),
            pltpu.VMEM((length, width), jnp.bfloat16),
        ],
        out_shape=[jax.ShapeDtypeStruct((2, rows, width), jnp.bfloat16)] * chips
        + [back] * chips
        + [grad_t, grad_t, jax.ShapeDtypeStruct((length, 2 * RANK), jnp.bfloat16)],
        compiler_params=pltpu.CompilerParams(vmem_limit_bytes=40 << 20),
        cost_estimate=pl.CostEstimate(
            flops=8 << 30, bytes_accessed=16 << 20, transcendentals=4 << 20
        ),
        name="attention",
    )(meta, packed, wq_up, wv_up)


def up_kernel(low, dq_t, dv_t, up):
    for part, grads in enumerate((dq_t, dv_t)):
        share = (dot(grads[...], low[...]) * ADAPTER_SCALE).T[part * RANK : (part + 1) * RANK, :]
        up[part * RANK : (part + 1) * RANK, :] = share.astype(jnp.bfloat16)


def up_gradient(low, dq_t, dv_t):
    return pl.pallas_call(
        up_kernel,
        in_specs=[VMEM] * 3,
        out_specs=VMEM,
        out_shape=jax.ShapeDtypeStruct((2 * RANK, dq_t.shape[0]), jnp.bfloat16),
        compiler_params=pltpu.CompilerParams(vmem_limit_bytes=16 << 20),
        name="up_gradient",
    )(low, dq_t, dv_t)


def pick_kernel(where, part_0, part_1, part_2, part_3, out):
    core = where[1]
    for step, part in enumerate((part_0, part_1, part_2, part_3)):
        out[step] = part[1 - core]


def pick(where, parts):
    return pl.pallas_call(
        pick_kernel,
        in_specs=[SMEM] + [VMEM] * len(parts),
        out_specs=VMEM,
        out_shape=jax.ShapeDtypeStruct((len(parts),) + parts[0].shape[1:], parts[0].dtype),
        compiler_params=pltpu.CompilerParams(vmem_limit_bytes=SMALL_VMEM),
        name="pick",
    )(where, *parts)


def arrive_kernel(where, part_0, part_1, part_2, part_3, other, out):
    chip, core = where[0], where[1]
    parts = (part_0, part_1, part_2, part_3)
    width = part_0.shape[2]
    for step in range(len(parts)):
        origin = lax.rem(chip + len(parts) - step, len(parts))
        here = pl.multiple_of((origin * 2 + core) * width, width)
        there = pl.multiple_of((origin * 2 + 1 - core) * width, width)
        out[0, :, pl.ds(here, width)] = parts[step][core]
        out[0, :, pl.ds(there, width)] = other[step]


def arrive(where, parts, other):
    _, rows, width = parts[0].shape
    return pl.pallas_call(
        arrive_kernel,
        in_specs=[SMEM] + [VMEM] * (len(parts) + 1),
        out_specs=VMEM,
        out_shape=jax.ShapeDtypeStruct((1, rows, 2 * len(parts) * width), parts[0].dtype),
        compiler_params=pltpu.CompilerParams(vmem_limit_bytes=SMALL_VMEM),
        name="arrive",
    )(where, *parts, other)


def down_kernel(core, *refs):
    *parts, hidden, hidden_other, up, out, back = refs

    @pl.when(pl.program_id(0) == 0)
    def _():
        total = parts[0][...].astype(jnp.float32)
        for part in parts[1:]:
            total += part[...].astype(jnp.float32)
        back[...] = total.astype(jnp.bfloat16)

    grad = dot(back[core[0]], hidden[...]) + dot(back[1 - core[0]], hidden_other[...])
    grad = grad.astype(out.dtype)
    for row in range(out.shape[0]):
        across = slice(row * SHARE_ROWS, (row + 1) * SHARE_ROWS)
        out[row, 0, :, :DOWN_COLS] = grad[across, :]
        out[row, 0, :, DOWN_COLS:] = up[across, :]


def down_gradient(core, parts, hidden, hidden_other, up):
    rows, half = hidden_other.shape
    steps = half // DOWN_COLS
    across = 2 * RANK // SHARE_ROWS
    shape = parts[0].shape
    return pl.pallas_call(
        down_kernel,
        grid_spec=pltpu.PrefetchScalarGridSpec(
            num_scalar_prefetch=1,
            grid=(steps,),
            in_specs=[pl.BlockSpec(shape, lambda i, core: (0, 0, 0))] * len(parts)
            + [
                pl.BlockSpec((rows, DOWN_COLS), lambda i, core: (0, core[0] * steps + i)),
                pl.BlockSpec((rows, DOWN_COLS), lambda i, core: (0, i)),
                pl.BlockSpec((2 * RANK, UP_COLS), lambda i, core: (0, i)),
            ],
            out_specs=pl.BlockSpec(
                (across, 1, SHARE_ROWS, DOWN_COLS + UP_COLS), lambda i, core: (0, i, 0, 0)
            ),
            scratch_shapes=[pltpu.VMEM(shape, jnp.bfloat16)],
        ),
        out_shape=jax.ShapeDtypeStruct(
            (across, steps, SHARE_ROWS, DOWN_COLS + UP_COLS), jnp.bfloat16
        ),
        compiler_params=pltpu.CompilerParams(vmem_limit_bytes=24 << 20),
        name="down_gradient",
    )(core, *parts, hidden, hidden_other, up)


def share_kernel(parts, *refs):
    out = refs[-1]
    total = parts[0].astype(jnp.float32)
    for part in range(1, parts.shape[0]):
        total += parts[part].astype(jnp.float32)
    out[...] = total.astype(out.dtype)


def sum_share(parts, after):
    return pl.pallas_call(
        share_kernel,
        in_specs=[VMEM] + [VMEM] * len(after),
        out_specs=VMEM,
        out_shape=jax.ShapeDtypeStruct(parts.shape[1:], parts.dtype),
        compiler_params=pltpu.CompilerParams(vmem_limit_bytes=SMALL_VMEM),
        name="sum_share",
    )(parts, *after)


def chips_kernel(where, *refs):
    *parts, _, out = refs
    chip = where[0]
    total = parts[0][:, :DOWN_COLS].astype(jnp.float32)
    for part in parts[1:]:
        total += part[:, :DOWN_COLS].astype(jnp.float32)
    total = total.astype(out.dtype)
    for device in range(out.shape[0]):
        out[device, :, :DOWN_COLS] = total
    for step, part in enumerate(parts):
        origin = lax.rem(chip + len(parts) - step, len(parts))
        begin = pl.multiple_of(DOWN_COLS + origin * UP_COLS, UP_COLS)
        for device in range(out.shape[0]):
            out[device, :, pl.ds(begin, UP_COLS)] = part[:, DOWN_COLS:]


def sum_chips(where, parts, devices, after):
    shape = (devices, SHARE_ROWS, DOWN_COLS + len(parts) * UP_COLS)
    return pl.pallas_call(
        chips_kernel,
        in_specs=[SMEM] + [VMEM] * (len(parts) + 1),
        out_specs=VMEM,
        out_shape=jax.ShapeDtypeStruct(shape, parts[0].dtype),
        compiler_params=pltpu.CompilerParams(vmem_limit_bytes=SMALL_VMEM),
        name="sum_chips",
    )(where, *parts, after)


def place_kernel(which, shares, *refs):
    *outs, downs, ups, sems = refs[-7:]
    which = which[0]
    half = shares.shape[0] // 2
    columns = shares.shape[1]
    copies = []

    def send(source, target, begin, size):
        begin = pl.multiple_of(begin, size)
        copies.append(
            pltpu.make_async_copy(source, target.at[:, pl.ds(begin, size)], sems.at[len(copies)])
        )
        copies[-1].start()

    chips, _, width = ups.shape
    for row in range(2 * half):
        part, across = row // half, slice(row % half * SHARE_ROWS, (row % half + 1) * SHARE_ROWS)
        for column in range(columns):
            share = shares[row, column]
            downs[part, across, column * DOWN_COLS : (column + 1) * DOWN_COLS] = share[
                :, :DOWN_COLS
            ].astype(jnp.float32)
            for chip in range(chips):
                begin = DOWN_COLS + chip * UP_COLS
                ups[
                    chip,
                    row * SHARE_ROWS : (row + 1) * SHARE_ROWS,
                    column * UP_COLS : (column + 1) * UP_COLS,
                ] = share[:, begin : begin + UP_COLS].astype(jnp.float32)
        if row % half == half - 1:
            send(downs.at[part], outs[2 * part], which * downs.shape[2], downs.shape[2])
            for chip in range(chips):
                send(
                    ups.at[chip, part * RANK : (part + 1) * RANK, :],
                    outs[2 * part + 1],
                    (2 * chip + which) * width,
                    width,
                )
    for copy in copies:
        copy.wait()


def place(which, shares, model, width, earlier=()):
    shapes = [(RANK, model), (RANK, width), (RANK, model), (RANK, width)]
    columns = shares.shape[1]
    chips = (shares.shape[3] - DOWN_COLS) // UP_COLS
    return pl.pallas_call(
        place_kernel,
        in_specs=[SMEM, VMEM] + [ANY] * len(earlier),
        out_specs=[ANY] * 4,
        out_shape=[jax.ShapeDtypeStruct(shape, jnp.float32) for shape in shapes],
        scratch_shapes=[
            pltpu.VMEM((2, RANK, columns * DOWN_COLS), jnp.float32),
            pltpu.VMEM((chips, 2 * RANK, columns * UP_COLS), jnp.float32),
            pltpu.SemaphoreType.DMA((2 + 2 * chips,)),
        ],
        input_output_aliases={2 + index: index for index in range(len(earlier))},
        compiler_params=pltpu.CompilerParams(vmem_limit_bytes=16 << 20),
        name="place",
    )(which[None], shares, *earlier)


def swap(x, axes):
    return lax.all_to_all(x, axes, 0, 0, tiled=True)


def to_other_core(x):
    return lax.ppermute(x, "core", [(0, 1), (1, 0)])


def per_device(
    sizes,
    hidden,
    frozen_queries,
    frozen_keys,
    frozen_values,
    document_length_list,
    query_down_weight,
    query_up_weight,
    value_down_weight,
    value_up_weight,
    output_gradient,
):
    dp_size, seq_size = sizes
    chips = seq_size // 2
    rows, model = hidden.shape[1:]
    half = model // 2
    chip = lax.axis_index("y").astype(jnp.int32)
    core = lax.axis_index("core").astype(jnp.int32)
    where = jnp.stack([chip, core])

    def to_chip(x, step):
        return lax.ppermute(x, "y", [(c, (c + step) % chips) for c in range(chips)])

    packed = pack(
        hidden[0],
        query_down_weight.T,
        value_down_weight.T,
        frozen_queries[0],
        frozen_keys[0],
        frozen_values[0],
        output_gradient[0],
        query_up_weight,
        value_up_weight,
        seq_size,
    )
    received = swap(packed, SEQ).reshape(seq_size * rows, packed.shape[2])
    hidden_other = to_other_core(
        lax.dynamic_slice(hidden[0], (0, (1 - core) * half), (rows, half))
    )
    width = frozen_queries.shape[2] // seq_size
    own_columns = (0, (chip * 2 + core) * width)
    wq_up = lax.dynamic_slice(query_up_weight, own_columns, (RANK, width))
    wv_up = lax.dynamic_slice(value_up_weight, own_columns, (RANK, width))
    meta = jnp.concatenate([document_length_list[0], where])
    *outs, dq_t, dv_t, low = attention(meta, received, wq_up, wv_up, seq_size)
    parts, backs = outs[:chips], outs[chips:]

    backs = [backs[0]] + [to_chip(backs[step], step) for step in range(1, chips)]
    backs_other = [to_other_core(back) for back in backs]
    parts = [parts[0]] + [to_chip(parts[step], step) for step in range(1, chips)]
    up = up_gradient(low, dq_t, dv_t)
    down = down_gradient(core[None], backs + backs_other, hidden[0], hidden_other, up)

    other = to_other_core(pick(where, parts))
    attended = arrive(where, parts, other)

    shares = swap(down.reshape((-1,) + down.shape[2:]), DP)
    share = sum_share(shares, after=parts[1:])
    share = [share] + [to_chip(share, step) for step in range(1, chips)]
    shares = swap(sum_chips(where, share, shares.shape[0], after=other), DP)
    shares = shares.reshape(down.shape[:2] + shares.shape[1:])
    shares_other = to_other_core(shares)
    grads = place(core, shares, model, seq_size * width)
    grad_a_q, up_q, grad_a_v, up_v = place(
        1 - core, shares_other, model, seq_size * width, earlier=grads
    )
    return attended, grad_a_q.T, up_q, grad_a_v.T, up_v


def solution(mesh):
    dp_size, seq_size = mesh.shape["dp"], mesh.shape["seq"]
    fine = Mesh(mesh.devices.reshape(4, 4, 4, 2), ALL)
    rows = P(DP, SEQ, None)
    in_specs = (rows, rows, rows, rows, P(DP, None), P(), P(), P(), P(), rows)
    out_specs = (rows, P(), P(), P(), P())
    return jax.shard_map(
        functools.partial(per_device, (dp_size, seq_size)),
        mesh=fine,
        in_specs=in_specs,
        out_specs=out_specs,
        check_vma=False,
    )
```

```python
import functools

import jax
import jax.numpy as jnp
from jax import lax
from jax.experimental import pallas as pl
from jax.experimental.pallas import tpu as pltpu
from jax.sharding import Mesh
from jax.sharding import PartitionSpec as P

HEAD_COUNT = 16
HEAD_SIZE = 128
RANK = 64
NDOC = 8
TILE = 256
MAX_TILES = 5
ADAPTER_SCALE = 2.0
NEG_FILL = -1e30
SCALING = HEAD_SIZE ** (-0.5)
LOG2_E = 1.4426950408889634

SHARE_ROWS = 16
DOWN_COLS = 1024
UP_COLS = 128

DP = ("x", "z")
SEQ = ("y", "core")
ALL = ("x", "z", "y", "core")
NT = (((1,), (1,)), ((), ()))


def dot(a, b):
    return jnp.dot(a, b, preferred_element_type=jnp.float32)


def dot_nt(a, b):
    return lax.dot_general(a, b, NT, preferred_element_type=jnp.float32)


HIDDEN_PARTS = 4
PACK_VMEM = 56 << 20
SMALL_VMEM = 8 << 20
VMEM = pl.BlockSpec(memory_space=pltpu.VMEM)
SMEM = pl.BlockSpec(memory_space=pltpu.SMEM)
ANY = pl.BlockSpec(memory_space=pl.ANY)


def pack_kernel(
    hidden, wq_down, wv_down, fq, fk, fv, grad, wq_up, wv_up, out,
    hidden_v, down_v, fq_v, fv_v, wq_up_v, wv_up_v, out_v, low,
    down_sems, hidden_sems, row_sems, through_sems, out_sems,
):
    devices, rows, packed = out.shape
    width = (packed - 2 * RANK) // 4
    model = hidden.shape[1]
    step = model // HIDDEN_PARTS

    def part(index):
        return pl.ds(index * step, step)

    def columns(index):
        return pl.ds(index * width, width)

    downs = [
        pltpu.make_async_copy(wq_down, down_v.at[pl.ds(0, RANK)], down_sems.at[0]),
        pltpu.make_async_copy(wv_down, down_v.at[pl.ds(RANK, RANK)], down_sems.at[1]),
    ]
    hiddens = [
        pltpu.make_async_copy(
            hidden.at[:, part(index)], hidden_v.at[:, part(index)], hidden_sems.at[index]
        )
        for index in range(HIDDEN_PARTS)
    ]
    through = [
        pltpu.make_async_copy(
            source.at[:, columns(device)],
            out_v.at[device, :, columns(which)],
            through_sems.at[which - 2, device],
        )
        for device in range(devices)
        for which, source in ((2, fk), (3, grad))
    ]
    whole = [
        pltpu.make_async_copy(wq_up, wq_up_v, row_sems.at[0]),
        pltpu.make_async_copy(fq, fq_v, row_sems.at[1]),
        pltpu.make_async_copy(wv_up, wv_up_v, row_sems.at[2]),
        pltpu.make_async_copy(fv, fv_v, row_sems.at[3]),
    ]
    for copy in downs + hiddens + through + whole:
        copy.start()

    def leave(device, begin, size, number):
        at = (device, slice(None), pl.ds(begin, size))
        copy = pltpu.make_async_copy(out_v.at[at], out.at[at], out_sems.at[number, device])
        copy.start()
        return copy

    for copy in downs:
        copy.wait()
    total = jnp.zeros((rows, 2 * RANK), jnp.float32)
    for index in range(HIDDEN_PARTS):
        hiddens[index].wait()
        total += dot_nt(hidden_v[:, part(index)], down_v[:, part(index)])
    low[...] = total.astype(jnp.bfloat16)
    outs = []
    for device in range(devices):
        through[2 * device].wait()
        through[2 * device + 1].wait()
        out_v[device, :, 4 * width :] = low[...]
        outs.append(leave(device, 2 * width, 2 * width + 2 * RANK, 0))
    for copy in whole:
        copy.wait()
    for device in range(devices):
        at = slice(device * width, (device + 1) * width)
        for which, (frozen, weight) in enumerate(((fq_v, wq_up_v), (fv_v, wv_up_v))):
            added = ADAPTER_SCALE * dot(low[:, which * RANK : (which + 1) * RANK], weight[:, at])
            out_v[device, :, which * width : (which + 1) * width] = (
                frozen[:, at].astype(jnp.float32) + added
            ).astype(jnp.bfloat16)
        outs.append(leave(device, 0, 2 * width, 1))
    for copy in outs:
        copy.wait()


def pack(hidden, wq_down_t, wv_down_t, fq, fk, fv, grad, wq_up, wv_up, seq_size):
    rows, model = hidden.shape
    columns = fq.shape[1]
    width = columns // seq_size
    bf16 = jnp.bfloat16
    return pl.pallas_call(
        pack_kernel,
        in_specs=[ANY] * 9,
        out_specs=ANY,
        out_shape=jax.ShapeDtypeStruct((seq_size, rows, 4 * width + 2 * RANK), bf16),
        scratch_shapes=[
            pltpu.VMEM((rows, model), bf16),
            pltpu.VMEM((2 * RANK, model), bf16),
            pltpu.VMEM((rows, columns), bf16),
            pltpu.VMEM((rows, columns), bf16),
            pltpu.VMEM((RANK, columns), bf16),
            pltpu.VMEM((RANK, columns), bf16),
            pltpu.VMEM((seq_size, rows, 4 * width + 2 * RANK), bf16),
            pltpu.VMEM((rows, 2 * RANK), bf16),
            pltpu.SemaphoreType.DMA((2,)),
            pltpu.SemaphoreType.DMA((HIDDEN_PARTS,)),
            pltpu.SemaphoreType.DMA((4,)),
            pltpu.SemaphoreType.DMA((2, seq_size)),
            pltpu.SemaphoreType.DMA((2, seq_size)),
        ],
        compiler_params=pltpu.CompilerParams(vmem_limit_bytes=PACK_VMEM),
        name="pack",
    )(hidden, wq_down_t, wv_down_t, fq, fk, fv, grad, wq_up, wv_up)


def attention_kernel(
    meta, packed, wq_up, wv_up, *refs
):
    *outs, dq_t, dv_t, low, q_t, k_t, v_t, g_t, dv, returned, out = refs[1:]
    outs, backs = outs[: len(outs) // 2], outs[len(outs) // 2 :]
    length = packed.shape[0]
    heads = out.shape[1] // HEAD_SIZE
    width = heads * HEAD_SIZE
    blocks = length // TILE
    chip = meta[NDOC]
    span = [slice(head * HEAD_SIZE, (head + 1) * HEAD_SIZE) for head in range(heads)]

    def columns(which, head):
        begin = which * width + head * HEAD_SIZE
        return slice(begin, begin + HEAD_SIZE)

    for head in range(heads):
        q_t[span[head], :] = packed[:, columns(0, head)].T
        v_t[span[head], :] = packed[:, columns(1, head)].T
        k_t[span[head], :] = packed[:, columns(2, head)].T
        g_t[span[head], :] = packed[:, columns(3, head)].T
    dv[...] = jnp.zeros_like(dv)

    def block(index, _):
        row0 = pl.multiple_of(index * TILE, TILE)
        q_rows = pl.ds(row0, TILE)
        position = row0 + lax.broadcasted_iota(jnp.int32, (1, TILE), 1)
        begin = jnp.zeros((1, TILE), jnp.int32)
        first = jnp.int32(0)
        end = jnp.int32(0)
        for doc in range(NDOC):
            end = end + meta[doc]
            begin = jnp.where(position >= end, end, begin)
            first = jnp.where(row0 >= end, end, first)
        tiles = index - lax.div(first, TILE) + 1

        def body(count):
            key0 = pl.multiple_of((index + 1 - count) * TILE, TILE)
            k_rows = pl.ds(key0, count * TILE)
            key_index = lax.broadcasted_iota(jnp.int32, (count * TILE, TILE), 0)
            in_document = key_index >= begin - key0
            causal = lax.broadcasted_iota(jnp.int32, (TILE, TILE), 0) <= (
                lax.broadcasted_iota(jnp.int32, (TILE, TILE), 1)
            )
            held = []
            for head in range(heads):
                scores = dot(packed[k_rows, columns(2, head)], q_t[span[head], q_rows])
                prob_grad = dot(packed[k_rows, columns(1, head)], g_t[span[head], q_rows])
                scores = jnp.where(in_document, scores, NEG_FILL)
                last = jnp.where(causal, scores[(count - 1) * TILE :], NEG_FILL)
                if count > 1:
                    scores = jnp.concatenate([scores[: (count - 1) * TILE], last], axis=0)
                else:
                    scores = last
                maximum = jnp.max(scores, axis=0, keepdims=True)
                powers = jnp.exp2((scores - maximum) * (SCALING * LOG2_E))
                inverse = 1.0 / jnp.sum(powers, axis=0, keepdims=True)
                held.append((prob_grad, powers.astype(jnp.bfloat16), inverse))
            for head in range(heads):
                prob_grad, rounded, inverse = held[head]
                result = (dot(v_t[span[head], k_rows], rounded) * inverse).astype(jnp.bfloat16)
                g_wide = g_t[span[head], q_rows].astype(jnp.float32)
                row_dot = jnp.sum(g_wide * result.astype(jnp.float32), axis=0, keepdims=True)
                score_grad = rounded * (prob_grad - row_dot).astype(jnp.bfloat16)
                query_grad = dot(k_t[span[head], k_rows], score_grad) * (inverse * SCALING)
                dq_t[span[head], q_rows] = query_grad.astype(jnp.bfloat16)
                out[q_rows, span[head]] = result.T
                g_scaled = (g_wide * inverse).astype(jnp.bfloat16).T
                dv[head, k_rows, :] += dot(rounded, g_scaled)

        for count in range(1, min(MAX_TILES, blocks) + 1):
            pl.when(tiles == count)(functools.partial(body, count))
        return 0

    lax.fori_loop(0, blocks, block, 0)
    for head in range(heads):
        dv_t[span[head], :] = dv[head].astype(jnp.bfloat16).T

    for part, (grads, weight) in enumerate(((dq_t, wq_up), (dv_t, wv_up))):
        returned[part * RANK : (part + 1) * RANK, :] = (
            ADAPTER_SCALE * dot(weight[...], grads[...])
        ).astype(jnp.bfloat16)
    low[...] = packed[:, 4 * width :]
    rows = backs[0].shape[2]
    for step in range(len(backs)):
        target = lax.rem(chip + step, len(backs))
        for holder in range(2):
            begin = pl.multiple_of((target * 2 + holder) * rows, rows)
            backs[step][holder] = returned[:, pl.ds(begin, rows)]
            outs[step][holder] = out[pl.ds(begin, rows), :]


def attention(meta, packed, wq_up, wv_up, seq_size, after):
    length = packed.shape[0]
    width = (packed.shape[1] - 2 * RANK) // 4
    rows = length // seq_size
    heads = width // HEAD_SIZE
    chips = seq_size // 2
    wide_t = pltpu.VMEM((width, length), jnp.bfloat16)
    back = jax.ShapeDtypeStruct((2, 2 * RANK, rows), jnp.bfloat16)
    grad_t = jax.ShapeDtypeStruct((width, length), jnp.bfloat16)
    return pl.pallas_call(
        attention_kernel,
        in_specs=[SMEM, VMEM, VMEM, VMEM, VMEM],
        out_specs=[VMEM] * (3 + 2 * chips),
        scratch_shapes=[
            wide_t,
            wide_t,
            wide_t,
            wide_t,
            pltpu.VMEM((heads, length, HEAD_SIZE), jnp.float32),
            pltpu.VMEM((2 * RANK, length), jnp.bfloat16),
            pltpu.VMEM((length, width), jnp.bfloat16),
        ],
        out_shape=[jax.ShapeDtypeStruct((2, rows, width), jnp.bfloat16)] * chips
        + [back] * chips
        + [grad_t, grad_t, jax.ShapeDtypeStruct((length, 2 * RANK), jnp.bfloat16)],
        compiler_params=pltpu.CompilerParams(vmem_limit_bytes=32 << 20),
        cost_estimate=pl.CostEstimate(
            flops=8 << 30, bytes_accessed=16 << 20, transcendentals=4 << 20
        ),
        name="attention",
    )(meta, packed, wq_up, wv_up, after)


def up_kernel(low, dq_t, dv_t, up):
    for part, grads in enumerate((dq_t, dv_t)):
        share = (dot(grads[...], low[...]) * ADAPTER_SCALE).T[part * RANK : (part + 1) * RANK, :]
        up[part * RANK : (part + 1) * RANK, :] = share.astype(jnp.bfloat16)


def up_gradient(low, dq_t, dv_t):
    return pl.pallas_call(
        up_kernel,
        in_specs=[VMEM] * 3,
        out_specs=VMEM,
        out_shape=jax.ShapeDtypeStruct((2 * RANK, dq_t.shape[0]), jnp.bfloat16),
        compiler_params=pltpu.CompilerParams(vmem_limit_bytes=16 << 20),
        name="up_gradient",
    )(low, dq_t, dv_t)


def pick_kernel(where, part_0, part_1, part_2, part_3, out):
    core = where[1]
    for step, part in enumerate((part_0, part_1, part_2, part_3)):
        out[step] = part[1 - core]


def pick(where, parts):
    return pl.pallas_call(
        pick_kernel,
        in_specs=[SMEM] + [VMEM] * len(parts),
        out_specs=VMEM,
        out_shape=jax.ShapeDtypeStruct((len(parts),) + parts[0].shape[1:], parts[0].dtype),
        compiler_params=pltpu.CompilerParams(vmem_limit_bytes=SMALL_VMEM),
        name="pick",
    )(where, *parts)


def arrive_kernel(where, part_0, part_1, part_2, part_3, other, out, done):
    chip, core = where[0], where[1]
    parts = (part_0, part_1, part_2, part_3)
    width = part_0.shape[2]
    for step in range(len(parts)):
        origin = lax.rem(chip + len(parts) - step, len(parts))
        here = pl.multiple_of((origin * 2 + core) * width, width)
        there = pl.multiple_of((origin * 2 + 1 - core) * width, width)
        out[0, :, pl.ds(here, width)] = parts[step][core]
        out[0, :, pl.ds(there, width)] = other[step]
    done[...] = jnp.zeros_like(done)


def arrive(where, parts, other):
    _, rows, width = parts[0].shape
    return pl.pallas_call(
        arrive_kernel,
        in_specs=[SMEM] + [VMEM] * (len(parts) + 1),
        out_specs=[VMEM] * 2,
        out_shape=[
            jax.ShapeDtypeStruct((1, rows, 2 * len(parts) * width), parts[0].dtype),
            jax.ShapeDtypeStruct((8, 128), jnp.float32),
        ],
        compiler_params=pltpu.CompilerParams(vmem_limit_bytes=SMALL_VMEM),
        name="arrive",
    )(where, *parts, other)


def halves_kernel(core, hidden, other, out):
    rows, half = other.shape
    out[:rows] = hidden[:, pl.ds(pl.multiple_of(core[0] * half, half), half)]
    out[rows:] = other[...]


def halves(core, hidden, other):
    rows, half = other.shape
    return pl.pallas_call(
        halves_kernel,
        in_specs=[SMEM, VMEM, VMEM],
        out_specs=VMEM,
        out_shape=jax.ShapeDtypeStruct((2 * rows, half), hidden.dtype),
        compiler_params=pltpu.CompilerParams(vmem_limit_bytes=SMALL_VMEM),
        name="halves",
    )(core, hidden, other)


def down_kernel(core, *refs):
    *parts, hidden, up, out, back = refs
    rows = parts[0].shape[2]

    @pl.when(pl.program_id(0) == 0)
    def _():
        total = parts[0][...].astype(jnp.float32)
        for part in parts[1:]:
            total += part[...].astype(jnp.float32)
        back[...] = total.astype(jnp.bfloat16)

    grad = dot(back[core[0]], hidden[:rows]) + dot(back[1 - core[0]], hidden[rows:])
    grad = grad.astype(out.dtype)
    for row in range(out.shape[0]):
        across = slice(row * SHARE_ROWS, (row + 1) * SHARE_ROWS)
        out[row, 0, :, :DOWN_COLS] = grad[across, :]
        out[row, 0, :, DOWN_COLS:] = up[across, :]


def down_gradient(core, parts, hidden, up):
    rows, half = hidden.shape
    steps = half // DOWN_COLS
    across = 2 * RANK // SHARE_ROWS
    shape = parts[0].shape
    return pl.pallas_call(
        down_kernel,
        grid_spec=pltpu.PrefetchScalarGridSpec(
            num_scalar_prefetch=1,
            grid=(steps,),
            in_specs=[pl.BlockSpec(shape, lambda i, core: (0, 0, 0))] * len(parts)
            + [
                pl.BlockSpec((rows, DOWN_COLS), lambda i, core: (0, i)),
                pl.BlockSpec((2 * RANK, UP_COLS), lambda i, core: (0, i)),
            ],
            out_specs=pl.BlockSpec(
                (across, 1, SHARE_ROWS, DOWN_COLS + UP_COLS), lambda i, core: (0, i, 0, 0)
            ),
            scratch_shapes=[pltpu.VMEM(shape, jnp.bfloat16)],
        ),
        out_shape=jax.ShapeDtypeStruct(
            (across, steps, SHARE_ROWS, DOWN_COLS + UP_COLS), jnp.bfloat16
        ),
        compiler_params=pltpu.CompilerParams(vmem_limit_bytes=24 << 20),
        name="down_gradient",
    )(core, *parts, hidden, up)


def share_kernel(parts, *refs):
    out = refs[-1]
    total = parts[0].astype(jnp.float32)
    for part in range(1, parts.shape[0]):
        total += parts[part].astype(jnp.float32)
    out[...] = total.astype(out.dtype)


def sum_share(parts, after):
    return pl.pallas_call(
        share_kernel,
        in_specs=[VMEM] + [VMEM] * len(after),
        out_specs=VMEM,
        out_shape=jax.ShapeDtypeStruct(parts.shape[1:], parts.dtype),
        compiler_params=pltpu.CompilerParams(vmem_limit_bytes=SMALL_VMEM),
        name="sum_share",
    )(parts, *after)


def chips_kernel(where, *refs):
    *parts, out = refs
    chip = where[0]
    total = parts[0][:, :DOWN_COLS].astype(jnp.float32)
    for part in parts[1:]:
        total += part[:, :DOWN_COLS].astype(jnp.float32)
    total = total.astype(out.dtype)
    for device in range(out.shape[0]):
        out[device, :, :DOWN_COLS] = total
    for step, part in enumerate(parts):
        origin = lax.rem(chip + len(parts) - step, len(parts))
        begin = pl.multiple_of(DOWN_COLS + origin * UP_COLS, UP_COLS)
        for device in range(out.shape[0]):
            out[device, :, pl.ds(begin, UP_COLS)] = part[:, DOWN_COLS:]


def sum_chips(where, parts, devices):
    shape = (devices, SHARE_ROWS, DOWN_COLS + len(parts) * UP_COLS)
    return pl.pallas_call(
        chips_kernel,
        in_specs=[SMEM] + [VMEM] * len(parts),
        out_specs=VMEM,
        out_shape=jax.ShapeDtypeStruct(shape, parts[0].dtype),
        compiler_params=pltpu.CompilerParams(vmem_limit_bytes=SMALL_VMEM),
        name="sum_chips",
    )(where, *parts)


def place_kernel(which, shares, *refs):
    *outs, downs, ups, sems = refs[-7:]
    which = which[0]
    half = shares.shape[0] // 2
    columns = shares.shape[1]
    copies = []

    def send(source, target, begin, size):
        begin = pl.multiple_of(begin, size)
        copies.append(
            pltpu.make_async_copy(source, target.at[:, pl.ds(begin, size)], sems.at[len(copies)])
        )
        copies[-1].start()

    chips, _, width = ups.shape
    for row in range(2 * half):
        part, across = row // half, slice(row % half * SHARE_ROWS, (row % half + 1) * SHARE_ROWS)
        for column in range(columns):
            share = shares[row, column]
            downs[part, across, column * DOWN_COLS : (column + 1) * DOWN_COLS] = share[
                :, :DOWN_COLS
            ].astype(jnp.float32)
            for chip in range(chips):
                begin = DOWN_COLS + chip * UP_COLS
                ups[
                    chip,
                    row * SHARE_ROWS : (row + 1) * SHARE_ROWS,
                    column * UP_COLS : (column + 1) * UP_COLS,
                ] = share[:, begin : begin + UP_COLS].astype(jnp.float32)
        if row % half == half - 1:
            send(downs.at[part], outs[2 * part], which * downs.shape[2], downs.shape[2])
            for chip in range(chips):
                send(
                    ups.at[chip, part * RANK : (part + 1) * RANK, :],
                    outs[2 * part + 1],
                    (2 * chip + which) * width,
                    width,
                )
    for copy in copies:
        copy.wait()


def place(which, shares, model, width, earlier=()):
    shapes = [(RANK, model), (RANK, width), (RANK, model), (RANK, width)]
    columns = shares.shape[1]
    chips = (shares.shape[3] - DOWN_COLS) // UP_COLS
    return pl.pallas_call(
        place_kernel,
        in_specs=[SMEM, VMEM] + [ANY] * len(earlier),
        out_specs=[ANY] * 4,
        out_shape=[jax.ShapeDtypeStruct(shape, jnp.float32) for shape in shapes],
        scratch_shapes=[
            pltpu.VMEM((2, RANK, columns * DOWN_COLS), jnp.float32),
            pltpu.VMEM((chips, 2 * RANK, columns * UP_COLS), jnp.float32),
            pltpu.SemaphoreType.DMA((2 + 2 * chips,)),
        ],
        input_output_aliases={2 + index: index for index in range(len(earlier))},
        compiler_params=pltpu.CompilerParams(vmem_limit_bytes=16 << 20),
        name="place",
    )(which[None], shares, *earlier)


def swap(x, axes):
    return lax.all_to_all(x, axes, 0, 0, tiled=True)


def to_other_core(x):
    return lax.ppermute(x, "core", [(0, 1), (1, 0)])


def per_device(
    sizes,
    hidden,
    frozen_queries,
    frozen_keys,
    frozen_values,
    document_length_list,
    query_down_weight,
    query_up_weight,
    value_down_weight,
    value_up_weight,
    output_gradient,
):
    dp_size, seq_size = sizes
    chips = seq_size // 2
    rows, model = hidden.shape[1:]
    half = model // 2
    chip = lax.axis_index("y").astype(jnp.int32)
    core = lax.axis_index("core").astype(jnp.int32)
    where = jnp.stack([chip, core])

    def to_chip(x, step):
        return lax.ppermute(x, "y", [(c, (c + step) % chips) for c in range(chips)])

    packed = pack(
        hidden[0],
        query_down_weight.T,
        value_down_weight.T,
        frozen_queries[0],
        frozen_keys[0],
        frozen_values[0],
        output_gradient[0],
        query_up_weight,
        value_up_weight,
        seq_size,
    )
    received = swap(packed, SEQ).reshape(seq_size * rows, packed.shape[2])
    hidden_other = to_other_core(
        lax.dynamic_slice(hidden[0], (0, (1 - core) * half), (rows, half))
    )
    hidden_half = halves(core[None], hidden[0], hidden_other)
    width = frozen_queries.shape[2] // seq_size
    own_columns = (0, (chip * 2 + core) * width)
    wq_up = lax.dynamic_slice(query_up_weight, own_columns, (RANK, width))
    wv_up = lax.dynamic_slice(value_up_weight, own_columns, (RANK, width))
    meta = jnp.concatenate([document_length_list[0], where])
    *outs, dq_t, dv_t, low = attention(
        meta, received, wq_up, wv_up, seq_size, after=hidden_half
    )
    parts, backs = outs[:chips], outs[chips:]

    backs = [backs[0]] + [to_chip(backs[step], step) for step in range(1, chips)]
    backs_other = [to_other_core(back) for back in backs]
    parts = [parts[0]] + [to_chip(parts[step], step) for step in range(1, chips)]
    up = up_gradient(low, dq_t, dv_t)
    down = down_gradient(core[None], backs + backs_other, hidden_half, up)

    other = to_other_core(pick(where, parts))
    attended, attended_done = arrive(where, parts, other)

    shares = swap(down.reshape((-1,) + down.shape[2:]), DP)
    share = sum_share(shares, after=[attended_done])
    share = [share] + [to_chip(share, step) for step in range(1, chips)]
    shares = swap(sum_chips(where, share, shares.shape[0]), DP)
    shares = shares.reshape(down.shape[:2] + shares.shape[1:])
    shares_other = to_other_core(shares)
    grads = place(core, shares, model, seq_size * width)
    grad_a_q, up_q, grad_a_v, up_v = place(
        1 - core, shares_other, model, seq_size * width, earlier=grads
    )
    return attended, grad_a_q.T, up_q, grad_a_v.T, up_v


def solution(mesh):
    dp_size, seq_size = mesh.shape["dp"], mesh.shape["seq"]
    fine = Mesh(mesh.devices.reshape(4, 4, 4, 2), ALL)
    rows = P(DP, SEQ, None)
    in_specs = (rows, rows, rows, rows, P(DP, None), P(), P(), P(), P(), rows)
    out_specs = (rows, P(), P(), P(), P())
    return jax.shard_map(
        functools.partial(per_device, (dp_size, seq_size)),
        mesh=fine,
        in_specs=in_specs,
        out_specs=out_specs,
        check_vma=False,
    )
```

```python
import functools

import jax
import jax.numpy as jnp
from jax import lax
from jax.experimental import pallas as pl
from jax.experimental.pallas import tpu as pltpu
from jax.sharding import Mesh
from jax.sharding import PartitionSpec as P

HEAD_COUNT = 16
HEAD_SIZE = 128
RANK = 64
NDOC = 8
TILE = 256
MAX_TILES = 5
ADAPTER_SCALE = 2.0
NEG_FILL = -1e30
SCALING = HEAD_SIZE ** (-0.5)
LOG2_E = 1.4426950408889634

SHARE_ROWS = 16
DOWN_COLS = 1024
UP_COLS = 128

DP = ("x", "z")
SEQ = ("y", "core")
ALL = ("x", "z", "y", "core")
NT = (((1,), (1,)), ((), ()))


def dot(a, b):
    return jnp.dot(a, b, preferred_element_type=jnp.float32)


def dot_nt(a, b):
    return lax.dot_general(a, b, NT, preferred_element_type=jnp.float32)


HIDDEN_PARTS = 4
PACK_VMEM = 56 << 20
SMALL_VMEM = 8 << 20
VMEM = pl.BlockSpec(memory_space=pltpu.VMEM)
SMEM = pl.BlockSpec(memory_space=pltpu.SMEM)
ANY = pl.BlockSpec(memory_space=pl.ANY)
DONE = jax.ShapeDtypeStruct((8, 128), jnp.float32)


def pack_kernel(
    hidden, wq_down, wv_down, fq, fk, fv, grad, wq_up, wv_up, out,
    hidden_v, down_v, fq_v, fv_v, wq_up_v, wv_up_v, out_v, low,
    down_sems, hidden_sems, row_sems, through_sems, out_sems,
):
    devices, rows, packed = out.shape
    width = (packed - 2 * RANK) // 4
    model = hidden.shape[1]
    step = model // HIDDEN_PARTS

    def part(index):
        return pl.ds(index * step, step)

    def columns(index):
        return pl.ds(index * width, width)

    downs = [
        pltpu.make_async_copy(wq_down, down_v.at[pl.ds(0, RANK)], down_sems.at[0]),
        pltpu.make_async_copy(wv_down, down_v.at[pl.ds(RANK, RANK)], down_sems.at[1]),
    ]
    hiddens = [
        pltpu.make_async_copy(
            hidden.at[:, part(index)], hidden_v.at[:, part(index)], hidden_sems.at[index]
        )
        for index in range(HIDDEN_PARTS)
    ]
    through = [
        pltpu.make_async_copy(
            source.at[:, columns(device)],
            out_v.at[device, :, columns(which)],
            through_sems.at[which - 2, device],
        )
        for device in range(devices)
        for which, source in ((2, fk), (3, grad))
    ]
    whole = [
        pltpu.make_async_copy(wq_up, wq_up_v, row_sems.at[0]),
        pltpu.make_async_copy(fq, fq_v, row_sems.at[1]),
        pltpu.make_async_copy(wv_up, wv_up_v, row_sems.at[2]),
        pltpu.make_async_copy(fv, fv_v, row_sems.at[3]),
    ]
    for copy in downs + hiddens + through + whole:
        copy.start()

    def leave(device, begin, size, number):
        at = (device, slice(None), pl.ds(begin, size))
        copy = pltpu.make_async_copy(out_v.at[at], out.at[at], out_sems.at[number, device])
        copy.start()
        return copy

    for copy in downs:
        copy.wait()
    total = jnp.zeros((rows, 2 * RANK), jnp.float32)
    for index in range(HIDDEN_PARTS):
        hiddens[index].wait()
        total += dot_nt(hidden_v[:, part(index)], down_v[:, part(index)])
    low[...] = total.astype(jnp.bfloat16)
    outs = []
    for device in range(devices):
        through[2 * device].wait()
        through[2 * device + 1].wait()
        out_v[device, :, 4 * width :] = low[...]
        outs.append(leave(device, 2 * width, 2 * width + 2 * RANK, 0))
    for copy in whole:
        copy.wait()
    for device in range(devices):
        at = slice(device * width, (device + 1) * width)
        for which, (frozen, weight) in enumerate(((fq_v, wq_up_v), (fv_v, wv_up_v))):
            added = ADAPTER_SCALE * dot(low[:, which * RANK : (which + 1) * RANK], weight[:, at])
            out_v[device, :, which * width : (which + 1) * width] = (
                frozen[:, at].astype(jnp.float32) + added
            ).astype(jnp.bfloat16)
        outs.append(leave(device, 0, 2 * width, 1))
    for copy in outs:
        copy.wait()


def pack(hidden, wq_down_t, wv_down_t, fq, fk, fv, grad, wq_up, wv_up, seq_size):
    rows, model = hidden.shape
    columns = fq.shape[1]
    width = columns // seq_size
    bf16 = jnp.bfloat16
    return pl.pallas_call(
        pack_kernel,
        in_specs=[ANY] * 9,
        out_specs=ANY,
        out_shape=jax.ShapeDtypeStruct((seq_size, rows, 4 * width + 2 * RANK), bf16),
        scratch_shapes=[
            pltpu.VMEM((rows, model), bf16),
            pltpu.VMEM((2 * RANK, model), bf16),
            pltpu.VMEM((rows, columns), bf16),
            pltpu.VMEM((rows, columns), bf16),
            pltpu.VMEM((RANK, columns), bf16),
            pltpu.VMEM((RANK, columns), bf16),
            pltpu.VMEM((seq_size, rows, 4 * width + 2 * RANK), bf16),
            pltpu.VMEM((rows, 2 * RANK), bf16),
            pltpu.SemaphoreType.DMA((2,)),
            pltpu.SemaphoreType.DMA((HIDDEN_PARTS,)),
            pltpu.SemaphoreType.DMA((4,)),
            pltpu.SemaphoreType.DMA((2, seq_size)),
            pltpu.SemaphoreType.DMA((2, seq_size)),
        ],
        compiler_params=pltpu.CompilerParams(vmem_limit_bytes=PACK_VMEM),
        name="pack",
    )(hidden, wq_down_t, wv_down_t, fq, fk, fv, grad, wq_up, wv_up)


def attention_kernel(
    meta, packed, wq_up, wv_up, *refs
):
    *outs, dq_t, dv_t, low, q_t, k_t, v_t, g_t, dv, returned, out = refs[1:]
    outs, backs = outs[: len(outs) // 2], outs[len(outs) // 2 :]
    length = packed.shape[0]
    heads = out.shape[1] // HEAD_SIZE
    width = heads * HEAD_SIZE
    blocks = length // TILE
    chip = meta[NDOC]
    span = [slice(head * HEAD_SIZE, (head + 1) * HEAD_SIZE) for head in range(heads)]

    def columns(which, head):
        begin = which * width + head * HEAD_SIZE
        return slice(begin, begin + HEAD_SIZE)

    for head in range(heads):
        q_t[span[head], :] = packed[:, columns(0, head)].T
        v_t[span[head], :] = packed[:, columns(1, head)].T
        k_t[span[head], :] = packed[:, columns(2, head)].T
        g_t[span[head], :] = packed[:, columns(3, head)].T
    dv[...] = jnp.zeros_like(dv)

    def block(index, _):
        row0 = pl.multiple_of(index * TILE, TILE)
        q_rows = pl.ds(row0, TILE)
        position = row0 + lax.broadcasted_iota(jnp.int32, (1, TILE), 1)
        begin = jnp.zeros((1, TILE), jnp.int32)
        first = jnp.int32(0)
        end = jnp.int32(0)
        for doc in range(NDOC):
            end = end + meta[doc]
            begin = jnp.where(position >= end, end, begin)
            first = jnp.where(row0 >= end, end, first)
        tiles = index - lax.div(first, TILE) + 1

        def body(count):
            key0 = pl.multiple_of((index + 1 - count) * TILE, TILE)
            k_rows = pl.ds(key0, count * TILE)
            key_index = lax.broadcasted_iota(jnp.int32, (count * TILE, TILE), 0)
            in_document = key_index >= begin - key0
            causal = lax.broadcasted_iota(jnp.int32, (TILE, TILE), 0) <= (
                lax.broadcasted_iota(jnp.int32, (TILE, TILE), 1)
            )
            held = []
            for head in range(heads):
                scores = dot(packed[k_rows, columns(2, head)], q_t[span[head], q_rows])
                prob_grad = dot(packed[k_rows, columns(1, head)], g_t[span[head], q_rows])
                scores = jnp.where(in_document, scores, NEG_FILL)
                last = jnp.where(causal, scores[(count - 1) * TILE :], NEG_FILL)
                if count > 1:
                    scores = jnp.concatenate([scores[: (count - 1) * TILE], last], axis=0)
                else:
                    scores = last
                maximum = jnp.max(scores, axis=0, keepdims=True)
                powers = jnp.exp2((scores - maximum) * (SCALING * LOG2_E))
                inverse = 1.0 / jnp.sum(powers, axis=0, keepdims=True)
                held.append((prob_grad, powers.astype(jnp.bfloat16), inverse))
            for head in range(heads):
                prob_grad, rounded, inverse = held[head]
                result = (dot(v_t[span[head], k_rows], rounded) * inverse).astype(jnp.bfloat16)
                g_wide = g_t[span[head], q_rows].astype(jnp.float32)
                row_dot = jnp.sum(g_wide * result.astype(jnp.float32), axis=0, keepdims=True)
                score_grad = rounded * (prob_grad - row_dot).astype(jnp.bfloat16)
                query_grad = dot(k_t[span[head], k_rows], score_grad) * (inverse * SCALING)
                dq_t[span[head], q_rows] = query_grad.astype(jnp.bfloat16)
                out[q_rows, span[head]] = result.T
                g_scaled = (g_wide * inverse).astype(jnp.bfloat16).T
                dv[head, k_rows, :] += dot(rounded, g_scaled)

        for count in range(1, min(MAX_TILES, blocks) + 1):
            pl.when(tiles == count)(functools.partial(body, count))
        return 0

    lax.fori_loop(0, blocks, block, 0)
    for head in range(heads):
        dv_t[span[head], :] = dv[head].astype(jnp.bfloat16).T

    for part, (grads, weight) in enumerate(((dq_t, wq_up), (dv_t, wv_up))):
        returned[part * RANK : (part + 1) * RANK, :] = (
            ADAPTER_SCALE * dot(weight[...], grads[...])
        ).astype(jnp.bfloat16)
    low[...] = packed[:, 4 * width :]
    rows = backs[0].shape[2]
    for step in range(len(backs)):
        target = lax.rem(chip + step, len(backs))
        for holder in range(2):
            begin = pl.multiple_of((target * 2 + holder) * rows, rows)
            backs[step][holder] = returned[:, pl.ds(begin, rows)]
            outs[step][holder] = out[pl.ds(begin, rows), :]


def attention(meta, packed, wq_up, wv_up, seq_size, after):
    length = packed.shape[0]
    width = (packed.shape[1] - 2 * RANK) // 4
    rows = length // seq_size
    heads = width // HEAD_SIZE
    chips = seq_size // 2
    wide_t = pltpu.VMEM((width, length), jnp.bfloat16)
    back = jax.ShapeDtypeStruct((2, 2 * RANK, rows), jnp.bfloat16)
    grad_t = jax.ShapeDtypeStruct((width, length), jnp.bfloat16)
    return pl.pallas_call(
        attention_kernel,
        in_specs=[SMEM, VMEM, VMEM, VMEM, VMEM],
        out_specs=[VMEM] * (3 + 2 * chips),
        scratch_shapes=[
            wide_t,
            wide_t,
            wide_t,
            wide_t,
            pltpu.VMEM((heads, length, HEAD_SIZE), jnp.float32),
            pltpu.VMEM((2 * RANK, length), jnp.bfloat16),
            pltpu.VMEM((length, width), jnp.bfloat16),
        ],
        out_shape=[jax.ShapeDtypeStruct((2, rows, width), jnp.bfloat16)] * chips
        + [back] * chips
        + [grad_t, grad_t, jax.ShapeDtypeStruct((length, 2 * RANK), jnp.bfloat16)],
        compiler_params=pltpu.CompilerParams(vmem_limit_bytes=32 << 20),
        cost_estimate=pl.CostEstimate(
            flops=8 << 30, bytes_accessed=16 << 20, transcendentals=4 << 20
        ),
        name="attention",
    )(meta, packed, wq_up, wv_up, after)


def up_kernel(low, dq_t, dv_t, up):
    for part, grads in enumerate((dq_t, dv_t)):
        share = (dot(grads[...], low[...]) * ADAPTER_SCALE).T[part * RANK : (part + 1) * RANK, :]
        up[part * RANK : (part + 1) * RANK, :] = share.astype(jnp.bfloat16)


def up_gradient(low, dq_t, dv_t):
    return pl.pallas_call(
        up_kernel,
        in_specs=[VMEM] * 3,
        out_specs=VMEM,
        out_shape=jax.ShapeDtypeStruct((2 * RANK, dq_t.shape[0]), jnp.bfloat16),
        compiler_params=pltpu.CompilerParams(vmem_limit_bytes=16 << 20),
        name="up_gradient",
    )(low, dq_t, dv_t)


def pick_kernel(where, part_0, part_1, part_2, part_3, out):
    core = where[1]
    for step, part in enumerate((part_0, part_1, part_2, part_3)):
        out[step] = part[1 - core]


def pick(where, parts):
    return pl.pallas_call(
        pick_kernel,
        in_specs=[SMEM] + [VMEM] * len(parts),
        out_specs=VMEM,
        out_shape=jax.ShapeDtypeStruct((len(parts),) + parts[0].shape[1:], parts[0].dtype),
        compiler_params=pltpu.CompilerParams(vmem_limit_bytes=SMALL_VMEM),
        name="pick",
    )(where, *parts)


def arrive_kernel(where, part_0, part_1, part_2, part_3, other, out, done):
    chip, core = where[0], where[1]
    parts = (part_0, part_1, part_2, part_3)
    width = part_0.shape[2]
    for step in range(len(parts)):
        origin = lax.rem(chip + len(parts) - step, len(parts))
        here = pl.multiple_of((origin * 2 + core) * width, width)
        there = pl.multiple_of((origin * 2 + 1 - core) * width, width)
        out[0, :, pl.ds(here, width)] = parts[step][core]
        out[0, :, pl.ds(there, width)] = other[step]
    done[...] = jnp.zeros_like(done)


def arrive(where, parts, other):
    _, rows, width = parts[0].shape
    return pl.pallas_call(
        arrive_kernel,
        in_specs=[SMEM] + [VMEM] * (len(parts) + 1),
        out_specs=[VMEM] * 2,
        out_shape=[
            jax.ShapeDtypeStruct((1, rows, 2 * len(parts) * width), parts[0].dtype),
            DONE,
        ],
        compiler_params=pltpu.CompilerParams(vmem_limit_bytes=SMALL_VMEM),
        name="arrive",
    )(where, *parts, other)


def backs_kernel(part_0, part_1, part_2, part_3, out):
    total = part_0[...].astype(jnp.float32)
    for part in (part_1, part_2, part_3):
        total += part[...].astype(jnp.float32)
    out[...] = total.astype(out.dtype)


def sum_backs(parts):
    return pl.pallas_call(
        backs_kernel,
        in_specs=[VMEM] * len(parts),
        out_specs=VMEM,
        out_shape=jax.ShapeDtypeStruct(parts[0].shape, parts[0].dtype),
        compiler_params=pltpu.CompilerParams(vmem_limit_bytes=SMALL_VMEM),
        name="sum_backs",
    )(*parts)


def halves_kernel(core, hidden, other, out, done):
    rows, half = other.shape
    out[:rows] = hidden[:, pl.ds(pl.multiple_of(core[0] * half, half), half)]
    out[rows:] = other[...]
    done[...] = jnp.zeros_like(done)


def halves(core, hidden, other):
    rows, half = other.shape
    return pl.pallas_call(
        halves_kernel,
        in_specs=[SMEM, VMEM, VMEM],
        out_specs=[VMEM] * 2,
        out_shape=[jax.ShapeDtypeStruct((2 * rows, half), hidden.dtype), DONE],
        compiler_params=pltpu.CompilerParams(vmem_limit_bytes=SMALL_VMEM),
        name="halves",
    )(core, hidden, other)


def down_kernel(core, *refs):
    *parts, hidden, up, out, back = refs
    rows = parts[0].shape[2]

    @pl.when(pl.program_id(0) == 0)
    def _():
        total = parts[0][...].astype(jnp.float32)
        for part in parts[1:]:
            total += part[...].astype(jnp.float32)
        back[...] = total.astype(jnp.bfloat16)

    grad = dot(back[core[0]], hidden[:rows]) + dot(back[1 - core[0]], hidden[rows:])
    grad = grad.astype(out.dtype)
    for row in range(out.shape[0]):
        across = slice(row * SHARE_ROWS, (row + 1) * SHARE_ROWS)
        out[row, 0, :, :DOWN_COLS] = grad[across, :]
        out[row, 0, :, DOWN_COLS:] = up[across, :]


def down_gradient(core, parts, hidden, up):
    rows, half = hidden.shape
    steps = half // DOWN_COLS
    across = 2 * RANK // SHARE_ROWS
    shape = parts[0].shape
    return pl.pallas_call(
        down_kernel,
        grid_spec=pltpu.PrefetchScalarGridSpec(
            num_scalar_prefetch=1,
            grid=(steps,),
            in_specs=[pl.BlockSpec(shape, lambda i, core: (0, 0, 0))] * len(parts)
            + [
                pl.BlockSpec((rows, DOWN_COLS), lambda i, core: (0, i)),
                pl.BlockSpec((2 * RANK, UP_COLS), lambda i, core: (0, i)),
            ],
            out_specs=pl.BlockSpec(
                (across, 1, SHARE_ROWS, DOWN_COLS + UP_COLS), lambda i, core: (0, i, 0, 0)
            ),
            scratch_shapes=[pltpu.VMEM(shape, jnp.bfloat16)],
        ),
        out_shape=jax.ShapeDtypeStruct(
            (across, steps, SHARE_ROWS, DOWN_COLS + UP_COLS), jnp.bfloat16
        ),
        compiler_params=pltpu.CompilerParams(vmem_limit_bytes=24 << 20),
        name="down_gradient",
    )(core, *parts, hidden, up)


def share_kernel(parts, *refs):
    out = refs[-1]
    total = parts[0].astype(jnp.float32)
    for part in range(1, parts.shape[0]):
        total += parts[part].astype(jnp.float32)
    out[...] = total.astype(out.dtype)


def sum_share(parts, after):
    return pl.pallas_call(
        share_kernel,
        in_specs=[VMEM] + [VMEM] * len(after),
        out_specs=VMEM,
        out_shape=jax.ShapeDtypeStruct(parts.shape[1:], parts.dtype),
        compiler_params=pltpu.CompilerParams(vmem_limit_bytes=SMALL_VMEM),
        name="sum_share",
    )(parts, *after)


def chips_kernel(where, *refs):
    *parts, out = refs
    chip = where[0]
    total = parts[0][:, :DOWN_COLS].astype(jnp.float32)
    for part in parts[1:]:
        total += part[:, :DOWN_COLS].astype(jnp.float32)
    total = total.astype(out.dtype)
    for device in range(out.shape[0]):
        out[device, :, :DOWN_COLS] = total
    for step, part in enumerate(parts):
        origin = lax.rem(chip + len(parts) - step, len(parts))
        begin = pl.multiple_of(DOWN_COLS + origin * UP_COLS, UP_COLS)
        for device in range(out.shape[0]):
            out[device, :, pl.ds(begin, UP_COLS)] = part[:, DOWN_COLS:]


def sum_chips(where, parts, devices):
    shape = (devices, SHARE_ROWS, DOWN_COLS + len(parts) * UP_COLS)
    return pl.pallas_call(
        chips_kernel,
        in_specs=[SMEM] + [VMEM] * len(parts),
        out_specs=VMEM,
        out_shape=jax.ShapeDtypeStruct(shape, parts[0].dtype),
        compiler_params=pltpu.CompilerParams(vmem_limit_bytes=SMALL_VMEM),
        name="sum_chips",
    )(where, *parts)


def place_kernel(which, shares, *refs):
    *outs, downs, ups, sems = refs[-7:]
    which = which[0]
    half = shares.shape[0] // 2
    columns = shares.shape[1]
    copies = []

    def send(source, target, begin, size):
        begin = pl.multiple_of(begin, size)
        copies.append(
            pltpu.make_async_copy(source, target.at[:, pl.ds(begin, size)], sems.at[len(copies)])
        )
        copies[-1].start()

    chips, _, width = ups.shape
    for row in range(2 * half):
        part, across = row // half, slice(row % half * SHARE_ROWS, (row % half + 1) * SHARE_ROWS)
        for column in range(columns):
            share = shares[row, column]
            downs[part, across, column * DOWN_COLS : (column + 1) * DOWN_COLS] = share[
                :, :DOWN_COLS
            ].astype(jnp.float32)
            for chip in range(chips):
                begin = DOWN_COLS + chip * UP_COLS
                ups[
                    chip,
                    row * SHARE_ROWS : (row + 1) * SHARE_ROWS,
                    column * UP_COLS : (column + 1) * UP_COLS,
                ] = share[:, begin : begin + UP_COLS].astype(jnp.float32)
        if row % half == half - 1:
            send(downs.at[part], outs[2 * part], which * downs.shape[2], downs.shape[2])
            for chip in range(chips):
                send(
                    ups.at[chip, part * RANK : (part + 1) * RANK, :],
                    outs[2 * part + 1],
                    (2 * chip + which) * width,
                    width,
                )
    for copy in copies:
        copy.wait()


def place(which, shares, model, width, earlier=()):
    shapes = [(RANK, model), (RANK, width), (RANK, model), (RANK, width)]
    columns = shares.shape[1]
    chips = (shares.shape[3] - DOWN_COLS) // UP_COLS
    return pl.pallas_call(
        place_kernel,
        in_specs=[SMEM, VMEM] + [ANY] * len(earlier),
        out_specs=[ANY] * 4,
        out_shape=[jax.ShapeDtypeStruct(shape, jnp.float32) for shape in shapes],
        scratch_shapes=[
            pltpu.VMEM((2, RANK, columns * DOWN_COLS), jnp.float32),
            pltpu.VMEM((chips, 2 * RANK, columns * UP_COLS), jnp.float32),
            pltpu.SemaphoreType.DMA((2 + 2 * chips,)),
        ],
        input_output_aliases={2 + index: index for index in range(len(earlier))},
        compiler_params=pltpu.CompilerParams(vmem_limit_bytes=16 << 20),
        name="place",
    )(which[None], shares, *earlier)


def swap(x, axes):
    return lax.all_to_all(x, axes, 0, 0, tiled=True)


def to_other_core(x):
    return lax.ppermute(x, "core", [(0, 1), (1, 0)])


def per_device(
    sizes,
    hidden,
    frozen_queries,
    frozen_keys,
    frozen_values,
    document_length_list,
    query_down_weight,
    query_up_weight,
    value_down_weight,
    value_up_weight,
    output_gradient,
):
    dp_size, seq_size = sizes
    chips = seq_size // 2
    rows, model = hidden.shape[1:]
    half = model // 2
    chip = lax.axis_index("y").astype(jnp.int32)
    core = lax.axis_index("core").astype(jnp.int32)
    where = jnp.stack([chip, core])

    def to_chip(x, step):
        return lax.ppermute(x, "y", [(c, (c + step) % chips) for c in range(chips)])

    packed = pack(
        hidden[0],
        query_down_weight.T,
        value_down_weight.T,
        frozen_queries[0],
        frozen_keys[0],
        frozen_values[0],
        output_gradient[0],
        query_up_weight,
        value_up_weight,
        seq_size,
    )
    received = swap(packed, SEQ).reshape(seq_size * rows, packed.shape[2])
    hidden_other = to_other_core(
        lax.dynamic_slice(hidden[0], (0, (1 - core) * half), (rows, half))
    )
    hidden_half, halves_done = halves(core[None], hidden[0], hidden_other)
    width = frozen_queries.shape[2] // seq_size
    own_columns = (0, (chip * 2 + core) * width)
    wq_up = lax.dynamic_slice(query_up_weight, own_columns, (RANK, width))
    wv_up = lax.dynamic_slice(value_up_weight, own_columns, (RANK, width))
    meta = jnp.concatenate([document_length_list[0], where])
    *outs, dq_t, dv_t, low = attention(
        meta, received, wq_up, wv_up, seq_size, after=halves_done
    )
    parts, backs = outs[:chips], outs[chips:]

    backs = [backs[0]] + [to_chip(backs[step], step) for step in range(1, chips)]
    back = sum_backs(backs)
    back_other = to_other_core(back)
    parts = [parts[0]] + [to_chip(parts[step], step) for step in range(1, chips)]
    up = up_gradient(low, dq_t, dv_t)
    down = down_gradient(core[None], [back, back_other], hidden_half, up)

    other = to_other_core(pick(where, parts))
    attended, attended_done = arrive(where, parts, other)

    shares = swap(down.reshape((-1,) + down.shape[2:]), DP)
    share = sum_share(shares, after=[attended_done])
    share = [share] + [to_chip(share, step) for step in range(1, chips)]
    shares = swap(sum_chips(where, share, shares.shape[0]), DP)
    shares = shares.reshape(down.shape[:2] + shares.shape[1:])
    shares_other = to_other_core(shares)
    grads = place(core, shares, model, seq_size * width)
    grad_a_q, up_q, grad_a_v, up_v = place(
        1 - core, shares_other, model, seq_size * width, earlier=grads
    )
    return attended, grad_a_q.T, up_q, grad_a_v.T, up_v


def solution(mesh):
    dp_size, seq_size = mesh.shape["dp"], mesh.shape["seq"]
    fine = Mesh(mesh.devices.reshape(4, 4, 4, 2), ALL)
    rows = P(DP, SEQ, None)
    in_specs = (rows, rows, rows, rows, P(DP, None), P(), P(), P(), P(), rows)
    out_specs = (rows, P(), P(), P(), P())
    return jax.shard_map(
        functools.partial(per_device, (dp_size, seq_size)),
        mesh=fine,
        in_specs=in_specs,
        out_specs=out_specs,
        check_vma=False,
    )
```

```python
import functools

import jax
import jax.numpy as jnp
from jax import lax
from jax.experimental import pallas as pl
from jax.experimental.pallas import tpu as pltpu
from jax.sharding import Mesh
from jax.sharding import PartitionSpec as P

HEAD_COUNT = 16
HEAD_SIZE = 128
RANK = 64
NDOC = 8
TILE = 256
MAX_TILES = 5
ADAPTER_SCALE = 2.0
NEG_FILL = -1e30
SCALING = HEAD_SIZE ** (-0.5)
LOG2_E = 1.4426950408889634

SHARE_ROWS = 16
DOWN_COLS = 1024
UP_COLS = 128

DP = ("x", "z")
SEQ = ("y", "core")
ALL = ("x", "z", "y", "core")
NT = (((1,), (1,)), ((), ()))


def dot(a, b):
    return jnp.dot(a, b, preferred_element_type=jnp.float32)


def dot_nt(a, b):
    return lax.dot_general(a, b, NT, preferred_element_type=jnp.float32)


LOW_ROWS = 16

HIDDEN_PARTS = 4
PACK_VMEM = 56 << 20
SMALL_VMEM = 8 << 20
VMEM = pl.BlockSpec(memory_space=pltpu.VMEM)
SMEM = pl.BlockSpec(memory_space=pltpu.SMEM)
ANY = pl.BlockSpec(memory_space=pl.ANY)
DONE = jax.ShapeDtypeStruct((8, 128), jnp.float32)


def pack_kernel(
    hidden, wq_down, wv_down, fq, fk, fv, grad, wq_up, wv_up, out,
    hidden_v, down_v, fq_v, fv_v, wq_up_v, wv_up_v, out_v, low,
    down_sems, hidden_sems, row_sems, through_sems, out_sems,
):
    devices, _, packed = out.shape
    width = packed // 4
    rows, model = hidden.shape
    step = model // HIDDEN_PARTS

    def part(index):
        return pl.ds(index * step, step)

    def columns(index):
        return pl.ds(index * width, width)

    downs = [
        pltpu.make_async_copy(wq_down, down_v.at[pl.ds(0, RANK)], down_sems.at[0]),
        pltpu.make_async_copy(wv_down, down_v.at[pl.ds(RANK, RANK)], down_sems.at[1]),
    ]
    hiddens = [
        pltpu.make_async_copy(
            hidden.at[:, part(index)], hidden_v.at[:, part(index)], hidden_sems.at[index]
        )
        for index in range(HIDDEN_PARTS)
    ]
    through = [
        pltpu.make_async_copy(
            source.at[:, columns(device)],
            out_v.at[device, pl.ds(0, rows), columns(which)],
            through_sems.at[which - 2, device],
        )
        for device in range(devices)
        for which, source in ((2, fk), (3, grad))
    ]
    whole = [
        pltpu.make_async_copy(wq_up, wq_up_v, row_sems.at[0]),
        pltpu.make_async_copy(fq, fq_v, row_sems.at[1]),
        pltpu.make_async_copy(wv_up, wv_up_v, row_sems.at[2]),
        pltpu.make_async_copy(fv, fv_v, row_sems.at[3]),
    ]
    for copy in downs + hiddens + through + whole:
        copy.start()

    def leave(device, begin, size, number):
        at = (device, slice(None), pl.ds(begin, size))
        copy = pltpu.make_async_copy(out_v.at[at], out.at[at], out_sems.at[number, device])
        copy.start()
        return copy

    for copy in downs:
        copy.wait()
    total = jnp.zeros((rows, 2 * RANK), jnp.float32)
    for index in range(HIDDEN_PARTS):
        hiddens[index].wait()
        total += dot_nt(hidden_v[:, part(index)], down_v[:, part(index)])
    low[...] = total.astype(jnp.bfloat16)
    upper, lower = total[: rows // 2], total[rows // 2 :]
    left = lax.broadcasted_iota(jnp.int32, upper.shape, 1) < RANK
    sides = (
        jnp.where(left, upper, pltpu.roll(lower, RANK, 1)).astype(jnp.bfloat16),
        jnp.where(left, pltpu.roll(upper, RANK, 1), lower).astype(jnp.bfloat16),
    )
    outs = []
    for device in range(devices):
        for piece in range(rows // 2 // LOW_ROWS):
            out_v[device, rows:, piece * 2 * RANK : (piece + 1) * 2 * RANK] = sides[device % 2][
                piece * LOW_ROWS : (piece + 1) * LOW_ROWS
            ]
        through[2 * device].wait()
        through[2 * device + 1].wait()
        outs.append(leave(device, 2 * width, 2 * width, 0))
    for copy in whole:
        copy.wait()
    for device in range(devices):
        at = slice(device * width, (device + 1) * width)
        for which, (frozen, weight) in enumerate(((fq_v, wq_up_v), (fv_v, wv_up_v))):
            added = ADAPTER_SCALE * dot(low[:, which * RANK : (which + 1) * RANK], weight[:, at])
            out_v[device, :rows, which * width : (which + 1) * width] = (
                frozen[:, at].astype(jnp.float32) + added
            ).astype(jnp.bfloat16)
        outs.append(leave(device, 0, 2 * width, 1))
    for copy in outs:
        copy.wait()


def pack(hidden, wq_down_t, wv_down_t, fq, fk, fv, grad, wq_up, wv_up, seq_size):
    rows, model = hidden.shape
    columns = fq.shape[1]
    width = columns // seq_size
    bf16 = jnp.bfloat16
    return pl.pallas_call(
        pack_kernel,
        in_specs=[ANY] * 9,
        out_specs=ANY,
        out_shape=jax.ShapeDtypeStruct((seq_size, rows + LOW_ROWS, 4 * width), bf16),
        scratch_shapes=[
            pltpu.VMEM((rows, model), bf16),
            pltpu.VMEM((2 * RANK, model), bf16),
            pltpu.VMEM((rows, columns), bf16),
            pltpu.VMEM((rows, columns), bf16),
            pltpu.VMEM((RANK, columns), bf16),
            pltpu.VMEM((RANK, columns), bf16),
            pltpu.VMEM((seq_size, rows + LOW_ROWS, 4 * width), bf16),
            pltpu.VMEM((rows, 2 * RANK), bf16),
            pltpu.SemaphoreType.DMA((2,)),
            pltpu.SemaphoreType.DMA((HIDDEN_PARTS,)),
            pltpu.SemaphoreType.DMA((4,)),
            pltpu.SemaphoreType.DMA((2, seq_size)),
            pltpu.SemaphoreType.DMA((2, seq_size)),
        ],
        compiler_params=pltpu.CompilerParams(vmem_limit_bytes=PACK_VMEM),
        name="pack",
    )(hidden, wq_down_t, wv_down_t, fq, fk, fv, grad, wq_up, wv_up)


def attention_kernel(
    meta, packed, wq_up, wv_up, *refs
):
    *outs, dq_t, dv_t, low, q_t, k_t, v_t, g_t, dv, returned, out = refs[1:]
    outs, backs = outs[: len(outs) // 2], outs[len(outs) // 2 :]
    length = out.shape[0]
    heads = out.shape[1] // HEAD_SIZE
    width = heads * HEAD_SIZE
    blocks = length // TILE
    chip = meta[NDOC]
    span = [slice(head * HEAD_SIZE, (head + 1) * HEAD_SIZE) for head in range(heads)]

    def columns(which, head):
        begin = which * width + head * HEAD_SIZE
        return slice(begin, begin + HEAD_SIZE)

    def tiles_of(first, count, which, head):
        rows = packed[pl.ds(first, count), :TILE, columns(which, head)]
        return rows.reshape(count * TILE, HEAD_SIZE)

    for head in range(heads):
        q_t[span[head], :] = tiles_of(0, blocks, 0, head).T
        v_t[span[head], :] = tiles_of(0, blocks, 1, head).T
        k_t[span[head], :] = tiles_of(0, blocks, 2, head).T
        g_t[span[head], :] = tiles_of(0, blocks, 3, head).T
    dv[...] = jnp.zeros_like(dv)

    def block(index, _):
        row0 = pl.multiple_of(index * TILE, TILE)
        q_rows = pl.ds(row0, TILE)
        position = row0 + lax.broadcasted_iota(jnp.int32, (1, TILE), 1)
        begin = jnp.zeros((1, TILE), jnp.int32)
        first = jnp.int32(0)
        end = jnp.int32(0)
        for doc in range(NDOC):
            end = end + meta[doc]
            begin = jnp.where(position >= end, end, begin)
            first = jnp.where(row0 >= end, end, first)
        tiles = index - lax.div(first, TILE) + 1

        def body(count):
            tile0 = index + 1 - count
            key0 = pl.multiple_of(tile0 * TILE, TILE)
            k_rows = pl.ds(key0, count * TILE)
            key_index = lax.broadcasted_iota(jnp.int32, (count * TILE, TILE), 0)
            in_document = key_index >= begin - key0
            causal = lax.broadcasted_iota(jnp.int32, (TILE, TILE), 0) <= (
                lax.broadcasted_iota(jnp.int32, (TILE, TILE), 1)
            )
            held = []
            for head in range(heads):
                scores = dot(tiles_of(tile0, count, 2, head), q_t[span[head], q_rows])
                prob_grad = dot(tiles_of(tile0, count, 1, head), g_t[span[head], q_rows])
                scores = jnp.where(in_document, scores, NEG_FILL)
                last = jnp.where(causal, scores[(count - 1) * TILE :], NEG_FILL)
                if count > 1:
                    scores = jnp.concatenate([scores[: (count - 1) * TILE], last], axis=0)
                else:
                    scores = last
                maximum = jnp.max(scores, axis=0, keepdims=True)
                powers = jnp.exp2((scores - maximum) * (SCALING * LOG2_E))
                inverse = 1.0 / jnp.sum(powers, axis=0, keepdims=True)
                held.append((prob_grad, powers.astype(jnp.bfloat16), inverse))
            for head in range(heads):
                prob_grad, rounded, inverse = held[head]
                powers = rounded.astype(jnp.float32)
                result = (dot(v_t[span[head], k_rows], rounded) * inverse).astype(jnp.bfloat16)
                row_dot = jnp.sum(powers * prob_grad, axis=0, keepdims=True) * inverse
                g_wide = g_t[span[head], q_rows].astype(jnp.float32)
                score_grad = rounded * (prob_grad - row_dot).astype(jnp.bfloat16)
                query_grad = dot(k_t[span[head], k_rows], score_grad) * (inverse * SCALING)
                dq_t[span[head], q_rows] = query_grad.astype(jnp.bfloat16)
                out[q_rows, span[head]] = result.T
                g_scaled = (g_wide * inverse).astype(jnp.bfloat16).T
                dv[head, k_rows, :] += dot(rounded, g_scaled)

        for count in range(1, min(MAX_TILES, blocks) + 1):
            pl.when(tiles == count)(functools.partial(body, count))
        return 0

    lax.fori_loop(0, blocks, block, 0)
    for head in range(heads):
        dv_t[span[head], :] = dv[head].astype(jnp.bfloat16).T

    for part, (grads, weight) in enumerate(((dq_t, wq_up), (dv_t, wv_up))):
        returned[part * RANK : (part + 1) * RANK, :] = (
            ADAPTER_SCALE * dot(weight[...], grads[...])
        ).astype(jnp.bfloat16)
    for piece in range(low.shape[1] // LOW_ROWS):
        low[:, piece * LOW_ROWS : (piece + 1) * LOW_ROWS, :] = packed[
            :, TILE:, piece * 2 * RANK : (piece + 1) * 2 * RANK
        ]
    rows = backs[0].shape[2]
    for step in range(len(backs)):
        target = lax.rem(chip + step, len(backs))
        for holder in range(2):
            begin = pl.multiple_of((target * 2 + holder) * rows, rows)
            backs[step][holder] = returned[:, pl.ds(begin, rows)]
            outs[step][holder] = out[pl.ds(begin, rows), :]


def attention(meta, packed, wq_up, wv_up, seq_size, after):
    rows = packed.shape[1] - LOW_ROWS
    length = seq_size * rows
    width = packed.shape[2] // 4
    heads = width // HEAD_SIZE
    chips = seq_size // 2
    wide_t = pltpu.VMEM((width, length), jnp.bfloat16)
    back = jax.ShapeDtypeStruct((2, 2 * RANK, rows), jnp.bfloat16)
    grad_t = jax.ShapeDtypeStruct((width, length), jnp.bfloat16)
    return pl.pallas_call(
        attention_kernel,
        in_specs=[SMEM, VMEM, VMEM, VMEM, VMEM],
        out_specs=[VMEM] * (3 + 2 * chips),
        scratch_shapes=[
            wide_t,
            wide_t,
            wide_t,
            wide_t,
            pltpu.VMEM((heads, length, HEAD_SIZE), jnp.float32),
            pltpu.VMEM((2 * RANK, length), jnp.bfloat16),
            pltpu.VMEM((length, width), jnp.bfloat16),
        ],
        out_shape=[jax.ShapeDtypeStruct((2, rows, width), jnp.bfloat16)] * chips
        + [back] * chips
        + [grad_t, grad_t]
        + [jax.ShapeDtypeStruct((seq_size, rows // 2, 2 * RANK), jnp.bfloat16)],
        compiler_params=pltpu.CompilerParams(vmem_limit_bytes=32 << 20),
        cost_estimate=pl.CostEstimate(
            flops=8 << 30, bytes_accessed=16 << 20, transcendentals=4 << 20
        ),
        name="attention",
    )(meta, packed, wq_up, wv_up, after)


def up_kernel(where, low, low_other, dq_t, dv_t, up, lows):
    lows[where[1]] = low[...]
    lows[1 - where[1]] = low_other[...]
    devices, half, _ = low.shape
    for part, grads in enumerate((dq_t, dv_t)):
        upper = lower = jnp.zeros((grads.shape[0], 2 * RANK), jnp.float32)
        for device in range(devices):
            begin = 2 * device * half
            upper += dot(grads[:, begin : begin + half], lows[part, device])
            lower += dot(grads[:, begin + half : begin + 2 * half], lows[part, device])
        share = ADAPTER_SCALE * (upper.T[:RANK] + lower.T[RANK:])
        up[part * RANK : (part + 1) * RANK, :] = share.astype(jnp.bfloat16)


def up_gradient(where, low, low_other, dq_t, dv_t):
    return pl.pallas_call(
        up_kernel,
        in_specs=[SMEM] + [VMEM] * 4,
        out_specs=VMEM,
        out_shape=jax.ShapeDtypeStruct((2 * RANK, dq_t.shape[0]), jnp.bfloat16),
        scratch_shapes=[pltpu.VMEM((2,) + low.shape, jnp.bfloat16)],
        compiler_params=pltpu.CompilerParams(vmem_limit_bytes=16 << 20),
        name="up_gradient",
    )(where, low, low_other, dq_t, dv_t)


def pick_kernel(where, part_0, part_1, part_2, part_3, out):
    core = where[1]
    for step, part in enumerate((part_0, part_1, part_2, part_3)):
        out[step] = part[1 - core]


def pick(where, parts):
    return pl.pallas_call(
        pick_kernel,
        in_specs=[SMEM] + [VMEM] * len(parts),
        out_specs=VMEM,
        out_shape=jax.ShapeDtypeStruct((len(parts),) + parts[0].shape[1:], parts[0].dtype),
        compiler_params=pltpu.CompilerParams(vmem_limit_bytes=SMALL_VMEM),
        name="pick",
    )(where, *parts)


def arrive_kernel(where, part_0, part_1, part_2, part_3, other, out, done):
    chip, core = where[0], where[1]
    parts = (part_0, part_1, part_2, part_3)
    width = part_0.shape[2]
    for step in range(len(parts)):
        origin = lax.rem(chip + len(parts) - step, len(parts))
        here = pl.multiple_of((origin * 2 + core) * width, width)
        there = pl.multiple_of((origin * 2 + 1 - core) * width, width)
        out[0, :, pl.ds(here, width)] = parts[step][core]
        out[0, :, pl.ds(there, width)] = other[step]
    done[...] = jnp.zeros_like(done)


def arrive(where, parts, other):
    _, rows, width = parts[0].shape
    return pl.pallas_call(
        arrive_kernel,
        in_specs=[SMEM] + [VMEM] * (len(parts) + 1),
        out_specs=[VMEM] * 2,
        out_shape=[
            jax.ShapeDtypeStruct((1, rows, 2 * len(parts) * width), parts[0].dtype),
            DONE,
        ],
        compiler_params=pltpu.CompilerParams(vmem_limit_bytes=SMALL_VMEM),
        name="arrive",
    )(where, *parts, other)


def backs_kernel(part_0, part_1, part_2, part_3, *refs):
    out = refs[len(refs) // 2]
    total = part_0[...].astype(jnp.float32)
    for part in (part_1, part_2, part_3):
        total += part[...].astype(jnp.float32)
    out[...] = total.astype(out.dtype)


def sum_backs(parts, held):
    count = len(parts)
    return pl.pallas_call(
        backs_kernel,
        in_specs=[VMEM] * (count + len(held)),
        out_specs=[VMEM] * (1 + len(held)),
        out_shape=[
            jax.ShapeDtypeStruct(part.shape, part.dtype) for part in [parts[0]] + list(held)
        ],
        input_output_aliases={count + index: 1 + index for index in range(len(held))},
        compiler_params=pltpu.CompilerParams(vmem_limit_bytes=SMALL_VMEM),
        name="sum_backs",
    )(*parts, *held)


def halves_kernel(core, hidden, other, out, done):
    rows, half = other.shape
    out[:rows] = hidden[:, pl.ds(pl.multiple_of(core[0] * half, half), half)]
    out[rows:] = other[...]
    done[...] = jnp.zeros_like(done)


def halves(core, hidden, other):
    rows, half = other.shape
    return pl.pallas_call(
        halves_kernel,
        in_specs=[SMEM, VMEM, VMEM],
        out_specs=[VMEM] * 2,
        out_shape=[jax.ShapeDtypeStruct((2 * rows, half), hidden.dtype), DONE],
        compiler_params=pltpu.CompilerParams(vmem_limit_bytes=SMALL_VMEM),
        name="halves",
    )(core, hidden, other)


def down_kernel(core, *refs):
    *parts, hidden, up, out, back = refs
    rows = parts[0].shape[2]

    @pl.when(pl.program_id(0) == 0)
    def _():
        total = parts[0][...].astype(jnp.float32)
        for part in parts[1:]:
            total += part[...].astype(jnp.float32)
        back[...] = total.astype(jnp.bfloat16)

    grad = dot(back[core[0]], hidden[:rows]) + dot(back[1 - core[0]], hidden[rows:])
    grad = grad.astype(out.dtype)
    for row in range(out.shape[0]):
        across = slice(row * SHARE_ROWS, (row + 1) * SHARE_ROWS)
        out[row, 0, :, :DOWN_COLS] = grad[across, :]
        out[row, 0, :, DOWN_COLS:] = up[across, :]


def down_gradient(core, parts, hidden, up):
    rows, half = hidden.shape
    steps = half // DOWN_COLS
    across = 2 * RANK // SHARE_ROWS
    shape = parts[0].shape
    return pl.pallas_call(
        down_kernel,
        grid_spec=pltpu.PrefetchScalarGridSpec(
            num_scalar_prefetch=1,
            grid=(steps,),
            in_specs=[pl.BlockSpec(shape, lambda i, core: (0, 0, 0))] * len(parts)
            + [
                pl.BlockSpec((rows, DOWN_COLS), lambda i, core: (0, i)),
                pl.BlockSpec((2 * RANK, UP_COLS), lambda i, core: (0, i)),
            ],
            out_specs=pl.BlockSpec(
                (across, 1, SHARE_ROWS, DOWN_COLS + UP_COLS), lambda i, core: (0, i, 0, 0)
            ),
            scratch_shapes=[pltpu.VMEM(shape, jnp.bfloat16)],
        ),
        out_shape=jax.ShapeDtypeStruct(
            (across, steps, SHARE_ROWS, DOWN_COLS + UP_COLS), jnp.bfloat16
        ),
        compiler_params=pltpu.CompilerParams(vmem_limit_bytes=24 << 20),
        name="down_gradient",
    )(core, *parts, hidden, up)


def share_kernel(parts, *refs):
    out = refs[-1]
    total = parts[0].astype(jnp.float32)
    for part in range(1, parts.shape[0]):
        total += parts[part].astype(jnp.float32)
    out[...] = total.astype(out.dtype)


def sum_share(parts, after):
    return pl.pallas_call(
        share_kernel,
        in_specs=[VMEM] + [VMEM] * len(after),
        out_specs=VMEM,
        out_shape=jax.ShapeDtypeStruct(parts.shape[1:], parts.dtype),
        compiler_params=pltpu.CompilerParams(vmem_limit_bytes=SMALL_VMEM),
        name="sum_share",
    )(parts, *after)


def chips_kernel(where, *refs):
    *parts, out = refs
    chip = where[0]
    total = parts[0][:, :DOWN_COLS].astype(jnp.float32)
    for part in parts[1:]:
        total += part[:, :DOWN_COLS].astype(jnp.float32)
    total = total.astype(out.dtype)
    for device in range(out.shape[0]):
        out[device, :, :DOWN_COLS] = total
    for step, part in enumerate(parts):
        origin = lax.rem(chip + len(parts) - step, len(parts))
        begin = pl.multiple_of(DOWN_COLS + origin * UP_COLS, UP_COLS)
        for device in range(out.shape[0]):
            out[device, :, pl.ds(begin, UP_COLS)] = part[:, DOWN_COLS:]


def sum_chips(where, parts, devices):
    shape = (devices, SHARE_ROWS, DOWN_COLS + len(parts) * UP_COLS)
    return pl.pallas_call(
        chips_kernel,
        in_specs=[SMEM] + [VMEM] * len(parts),
        out_specs=VMEM,
        out_shape=jax.ShapeDtypeStruct(shape, parts[0].dtype),
        compiler_params=pltpu.CompilerParams(vmem_limit_bytes=SMALL_VMEM),
        name="sum_chips",
    )(where, *parts)


def place_kernel(which, shares, *refs):
    *outs, downs, ups, sems = refs[-7:]
    which = which[0]
    half = shares.shape[0] // 2
    columns = shares.shape[1]
    copies = []

    def send(source, target, begin, size):
        begin = pl.multiple_of(begin, size)
        copies.append(
            pltpu.make_async_copy(source, target.at[:, pl.ds(begin, size)], sems.at[len(copies)])
        )
        copies[-1].start()

    chips, _, width = ups.shape
    for row in range(2 * half):
        part, across = row // half, slice(row % half * SHARE_ROWS, (row % half + 1) * SHARE_ROWS)
        for column in range(columns):
            share = shares[row, column]
            downs[part, across, column * DOWN_COLS : (column + 1) * DOWN_COLS] = share[
                :, :DOWN_COLS
            ].astype(jnp.float32)
            for chip in range(chips):
                begin = DOWN_COLS + chip * UP_COLS
                ups[
                    chip,
                    row * SHARE_ROWS : (row + 1) * SHARE_ROWS,
                    column * UP_COLS : (column + 1) * UP_COLS,
                ] = share[:, begin : begin + UP_COLS].astype(jnp.float32)
        if row % half == half - 1:
            send(downs.at[part], outs[2 * part], which * downs.shape[2], downs.shape[2])
            for chip in range(chips):
                send(
                    ups.at[chip, part * RANK : (part + 1) * RANK, :],
                    outs[2 * part + 1],
                    (2 * chip + which) * width,
                    width,
                )
    for copy in copies:
        copy.wait()


def place(which, shares, model, width, earlier=()):
    shapes = [(RANK, model), (RANK, width), (RANK, model), (RANK, width)]
    columns = shares.shape[1]
    chips = (shares.shape[3] - DOWN_COLS) // UP_COLS
    return pl.pallas_call(
        place_kernel,
        in_specs=[SMEM, VMEM] + [ANY] * len(earlier),
        out_specs=[ANY] * 4,
        out_shape=[jax.ShapeDtypeStruct(shape, jnp.float32) for shape in shapes],
        scratch_shapes=[
            pltpu.VMEM((2, RANK, columns * DOWN_COLS), jnp.float32),
            pltpu.VMEM((chips, 2 * RANK, columns * UP_COLS), jnp.float32),
            pltpu.SemaphoreType.DMA((2 + 2 * chips,)),
        ],
        input_output_aliases={2 + index: index for index in range(len(earlier))},
        compiler_params=pltpu.CompilerParams(vmem_limit_bytes=16 << 20),
        name="place",
    )(which[None], shares, *earlier)


def swap(x, axes):
    return lax.all_to_all(x, axes, 0, 0, tiled=True)


def to_other_core(x):
    return lax.ppermute(x, "core", [(0, 1), (1, 0)])


def per_device(
    sizes,
    hidden,
    frozen_queries,
    frozen_keys,
    frozen_values,
    document_length_list,
    query_down_weight,
    query_up_weight,
    value_down_weight,
    value_up_weight,
    output_gradient,
):
    dp_size, seq_size = sizes
    chips = seq_size // 2
    rows, model = hidden.shape[1:]
    half = model // 2
    chip = lax.axis_index("y").astype(jnp.int32)
    core = lax.axis_index("core").astype(jnp.int32)
    where = jnp.stack([chip, core])

    def to_chip(x, step):
        return lax.ppermute(x, "y", [(c, (c + step) % chips) for c in range(chips)])

    packed = pack(
        hidden[0],
        query_down_weight.T,
        value_down_weight.T,
        frozen_queries[0],
        frozen_keys[0],
        frozen_values[0],
        output_gradient[0],
        query_up_weight,
        value_up_weight,
        seq_size,
    )
    received = swap(packed, SEQ)
    hidden_other = to_other_core(
        lax.dynamic_slice(hidden[0], (0, (1 - core) * half), (rows, half))
    )
    hidden_half, halves_done = halves(core[None], hidden[0], hidden_other)
    width = frozen_queries.shape[2] // seq_size
    own_columns = (0, (chip * 2 + core) * width)
    wq_up = lax.dynamic_slice(query_up_weight, own_columns, (RANK, width))
    wv_up = lax.dynamic_slice(value_up_weight, own_columns, (RANK, width))
    meta = jnp.concatenate([document_length_list[0], where])
    *outs, dq_t, dv_t, low = attention(
        meta, received, wq_up, wv_up, seq_size, after=halves_done
    )
    parts, backs = outs[:chips], outs[chips:]

    backs = [backs[0]] + [to_chip(backs[step], step) for step in range(1, chips)]
    back, *held = sum_backs(backs, parts[-2:])
    parts = parts[:-2] + held
    back_other = to_other_core(back)
    parts = [parts[0]] + [to_chip(parts[step], step) for step in range(1, chips)]
    up = up_gradient(where, low, to_other_core(low), dq_t, dv_t)
    down = down_gradient(core[None], [back, back_other], hidden_half, up)

    other = to_other_core(pick(where, parts))
    attended, attended_done = arrive(where, parts, other)

    shares = swap(down.reshape((-1,) + down.shape[2:]), DP)
    share = sum_share(shares, after=[attended_done])
    share = [share] + [to_chip(share, step) for step in range(1, chips)]
    shares = swap(sum_chips(where, share, shares.shape[0]), DP)
    shares = shares.reshape(down.shape[:2] + shares.shape[1:])
    shares_other = to_other_core(shares)
    grads = place(core, shares, model, seq_size * width)
    grad_a_q, up_q, grad_a_v, up_v = place(
        1 - core, shares_other, model, seq_size * width, earlier=grads
    )
    return attended, grad_a_q.T, up_q, grad_a_v.T, up_v


def solution(mesh):
    dp_size, seq_size = mesh.shape["dp"], mesh.shape["seq"]
    fine = Mesh(mesh.devices.reshape(4, 4, 4, 2), ALL)
    rows = P(DP, SEQ, None)
    in_specs = (rows, rows, rows, rows, P(DP, None), P(), P(), P(), P(), rows)
    out_specs = (rows, P(), P(), P(), P())
    return jax.shard_map(
        functools.partial(per_device, (dp_size, seq_size)),
        mesh=fine,
        in_specs=in_specs,
        out_specs=out_specs,
        check_vma=False,
    )
```

```python
import functools

import jax
import jax.numpy as jnp
from jax import lax
from jax.experimental import pallas as pl
from jax.experimental.pallas import tpu as pltpu
from jax.sharding import Mesh
from jax.sharding import PartitionSpec as P

HEAD_COUNT = 16
HEAD_SIZE = 128
RANK = 64
NDOC = 8
TILE = 256
MAX_TILES = 5
ADAPTER_SCALE = 2.0
NEG_FILL = -1e30
SCALING = HEAD_SIZE ** (-0.5)
LOG2_E = 1.4426950408889634

SHARE_ROWS = 16
DOWN_COLS = 1024
UP_COLS = 128

DP = ("x", "z")
SEQ = ("y", "core")
ALL = ("x", "z", "y", "core")
NT = (((1,), (1,)), ((), ()))


def dot(a, b):
    return jnp.dot(a, b, preferred_element_type=jnp.float32)


def dot_nt(a, b):
    return lax.dot_general(a, b, NT, preferred_element_type=jnp.float32)


LOW_ROWS = 16

HIDDEN_PARTS = 4
PACK_VMEM = 56 << 20
SMALL_VMEM = 8 << 20
VMEM = pl.BlockSpec(memory_space=pltpu.VMEM)
SMEM = pl.BlockSpec(memory_space=pltpu.SMEM)
ANY = pl.BlockSpec(memory_space=pl.ANY)
DONE = jax.ShapeDtypeStruct((8, 128), jnp.float32)


def pack_kernel(
    core, hidden, wq_down, wv_down, fq, fk, fv, grad, wq_up, wv_up, out, other,
    hidden_v, down_v, fq_v, fv_v, wq_up_v, wv_up_v, out_v, low,
    down_sems, hidden_sems, row_sems, through_sems, out_sems, other_sem,
):
    devices, _, packed = out.shape
    width = packed // 4
    rows, model = hidden.shape
    step = model // HIDDEN_PARTS

    def part(index):
        return pl.ds(index * step, step)

    def columns(index):
        return pl.ds(index * width, width)

    downs = [
        pltpu.make_async_copy(wq_down, down_v.at[pl.ds(0, RANK)], down_sems.at[0]),
        pltpu.make_async_copy(wv_down, down_v.at[pl.ds(RANK, RANK)], down_sems.at[1]),
    ]
    hiddens = [
        pltpu.make_async_copy(
            hidden.at[:, part(index)], hidden_v.at[:, part(index)], hidden_sems.at[index]
        )
        for index in range(HIDDEN_PARTS)
    ]
    through = [
        pltpu.make_async_copy(
            source.at[:, columns(device)],
            out_v.at[device, pl.ds(0, rows), columns(which)],
            through_sems.at[which - 2, device],
        )
        for device in range(devices)
        for which, source in ((2, fk), (3, grad))
    ]
    whole = [
        pltpu.make_async_copy(wq_up, wq_up_v, row_sems.at[0]),
        pltpu.make_async_copy(fq, fq_v, row_sems.at[1]),
        pltpu.make_async_copy(wv_up, wv_up_v, row_sems.at[2]),
        pltpu.make_async_copy(fv, fv_v, row_sems.at[3]),
    ]
    for copy in downs + hiddens + through + whole:
        copy.start()

    def leave(device, begin, size, number):
        at = (device, slice(None), pl.ds(begin, size))
        copy = pltpu.make_async_copy(out_v.at[at], out.at[at], out_sems.at[number, device])
        copy.start()
        return copy

    for copy in downs:
        copy.wait()
    total = jnp.zeros((rows, 2 * RANK), jnp.float32)
    for index in range(HIDDEN_PARTS):
        hiddens[index].wait()
        total += dot_nt(hidden_v[:, part(index)], down_v[:, part(index)])
    low[...] = total.astype(jnp.bfloat16)
    half = other.shape[1]
    begin = pl.multiple_of((1 - core[0]) * half, half)
    other_copy = pltpu.make_async_copy(hidden_v.at[:, pl.ds(begin, half)], other, other_sem)
    other_copy.start()
    upper, lower = total[: rows // 2], total[rows // 2 :]
    left = lax.broadcasted_iota(jnp.int32, upper.shape, 1) < RANK
    sides = (
        jnp.where(left, upper, pltpu.roll(lower, RANK, 1)).astype(jnp.bfloat16),
        jnp.where(left, pltpu.roll(upper, RANK, 1), lower).astype(jnp.bfloat16),
    )
    outs = []
    for device in range(devices):
        for piece in range(rows // 2 // LOW_ROWS):
            out_v[device, rows:, piece * 2 * RANK : (piece + 1) * 2 * RANK] = sides[device % 2][
                piece * LOW_ROWS : (piece + 1) * LOW_ROWS
            ]
        through[2 * device].wait()
        through[2 * device + 1].wait()
        outs.append(leave(device, 2 * width, 2 * width, 0))
    for copy in whole:
        copy.wait()
    for device in range(devices):
        at = slice(device * width, (device + 1) * width)
        for which, (frozen, weight) in enumerate(((fq_v, wq_up_v), (fv_v, wv_up_v))):
            added = ADAPTER_SCALE * dot(low[:, which * RANK : (which + 1) * RANK], weight[:, at])
            out_v[device, :rows, which * width : (which + 1) * width] = (
                frozen[:, at].astype(jnp.float32) + added
            ).astype(jnp.bfloat16)
        outs.append(leave(device, 0, 2 * width, 1))
    for copy in outs:
        copy.wait()
    other_copy.wait()


def pack(core, hidden, wq_down_t, wv_down_t, fq, fk, fv, grad, wq_up, wv_up, seq_size):
    rows, model = hidden.shape
    columns = fq.shape[1]
    width = columns // seq_size
    bf16 = jnp.bfloat16
    return pl.pallas_call(
        pack_kernel,
        in_specs=[SMEM] + [ANY] * 9,
        out_specs=[ANY] * 2,
        out_shape=[
            jax.ShapeDtypeStruct((seq_size, rows + LOW_ROWS, 4 * width), bf16),
            jax.ShapeDtypeStruct((rows, model // 2), bf16),
        ],
        scratch_shapes=[
            pltpu.VMEM((rows, model), bf16),
            pltpu.VMEM((2 * RANK, model), bf16),
            pltpu.VMEM((rows, columns), bf16),
            pltpu.VMEM((rows, columns), bf16),
            pltpu.VMEM((RANK, columns), bf16),
            pltpu.VMEM((RANK, columns), bf16),
            pltpu.VMEM((seq_size, rows + LOW_ROWS, 4 * width), bf16),
            pltpu.VMEM((rows, 2 * RANK), bf16),
            pltpu.SemaphoreType.DMA((2,)),
            pltpu.SemaphoreType.DMA((HIDDEN_PARTS,)),
            pltpu.SemaphoreType.DMA((4,)),
            pltpu.SemaphoreType.DMA((2, seq_size)),
            pltpu.SemaphoreType.DMA((2, seq_size)),
            pltpu.SemaphoreType.DMA,
        ],
        compiler_params=pltpu.CompilerParams(vmem_limit_bytes=PACK_VMEM),
        name="pack",
    )(core, hidden, wq_down_t, wv_down_t, fq, fk, fv, grad, wq_up, wv_up)


def attention_kernel(
    lengths, chip, core, packed, wq_up, wv_up, *refs
):
    *outs, dq_t, dv_t, low, q_t, k_t, v_t, g_t, dv, returned, out = refs[1:]
    outs, backs = outs[: len(outs) // 2], outs[len(outs) // 2 :]
    length = out.shape[0]
    heads = out.shape[1] // HEAD_SIZE
    width = heads * HEAD_SIZE
    blocks = length // TILE
    chip, core = chip[0], core[0]
    own_columns = pl.ds(pl.multiple_of((chip * 2 + core) * width, width), width)
    span = [slice(head * HEAD_SIZE, (head + 1) * HEAD_SIZE) for head in range(heads)]

    def columns(which, head):
        begin = which * width + head * HEAD_SIZE
        return slice(begin, begin + HEAD_SIZE)

    def tiles_of(first, count, which, head):
        rows = packed[pl.ds(first, count), :TILE, columns(which, head)]
        return rows.reshape(count * TILE, HEAD_SIZE)

    for head in range(heads):
        q_t[span[head], :] = tiles_of(0, blocks, 0, head).T
        v_t[span[head], :] = tiles_of(0, blocks, 1, head).T
        k_t[span[head], :] = tiles_of(0, blocks, 2, head).T
        g_t[span[head], :] = tiles_of(0, blocks, 3, head).T
    dv[...] = jnp.zeros_like(dv)

    def block(index, _):
        row0 = pl.multiple_of(index * TILE, TILE)
        q_rows = pl.ds(row0, TILE)
        position = row0 + lax.broadcasted_iota(jnp.int32, (1, TILE), 1)
        begin = jnp.zeros((1, TILE), jnp.int32)
        first = jnp.int32(0)
        end = jnp.int32(0)
        for doc in range(NDOC):
            end = end + lengths[0, doc]
            begin = jnp.where(position >= end, end, begin)
            first = jnp.where(row0 >= end, end, first)
        tiles = index - lax.div(first, TILE) + 1

        def body(count):
            tile0 = index + 1 - count
            key0 = pl.multiple_of(tile0 * TILE, TILE)
            k_rows = pl.ds(key0, count * TILE)
            key_index = lax.broadcasted_iota(jnp.int32, (count * TILE, TILE), 0)
            in_document = key_index >= begin - key0
            causal = lax.broadcasted_iota(jnp.int32, (TILE, TILE), 0) <= (
                lax.broadcasted_iota(jnp.int32, (TILE, TILE), 1)
            )
            held = []
            for head in range(heads):
                scores = dot(tiles_of(tile0, count, 2, head), q_t[span[head], q_rows])
                prob_grad = dot(tiles_of(tile0, count, 1, head), g_t[span[head], q_rows])
                scores = jnp.where(in_document, scores, NEG_FILL)
                last = jnp.where(causal, scores[(count - 1) * TILE :], NEG_FILL)
                if count > 1:
                    scores = jnp.concatenate([scores[: (count - 1) * TILE], last], axis=0)
                else:
                    scores = last
                maximum = jnp.max(scores, axis=0, keepdims=True)
                powers = jnp.exp2((scores - maximum) * (SCALING * LOG2_E))
                inverse = 1.0 / jnp.sum(powers, axis=0, keepdims=True)
                held.append((prob_grad, powers.astype(jnp.bfloat16), inverse))
            for head in range(heads):
                prob_grad, rounded, inverse = held[head]
                powers = rounded.astype(jnp.float32)
                result = (dot(v_t[span[head], k_rows], rounded) * inverse).astype(jnp.bfloat16)
                row_dot = jnp.sum(powers * prob_grad, axis=0, keepdims=True) * inverse
                g_wide = g_t[span[head], q_rows].astype(jnp.float32)
                score_grad = rounded * (prob_grad - row_dot).astype(jnp.bfloat16)
                query_grad = dot(k_t[span[head], k_rows], score_grad) * (inverse * SCALING)
                dq_t[span[head], q_rows] = query_grad.astype(jnp.bfloat16)
                out[q_rows, span[head]] = result.T
                g_scaled = (g_wide * inverse).astype(jnp.bfloat16).T
                dv[head, k_rows, :] += dot(rounded, g_scaled)

        for count in range(1, min(MAX_TILES, blocks) + 1):
            pl.when(tiles == count)(functools.partial(body, count))
        return 0

    lax.fori_loop(0, blocks, block, 0)
    for head in range(heads):
        dv_t[span[head], :] = dv[head].astype(jnp.bfloat16).T

    for part, (grads, weight) in enumerate(((dq_t, wq_up), (dv_t, wv_up))):
        returned[part * RANK : (part + 1) * RANK, :] = (
            ADAPTER_SCALE * dot(weight[:, own_columns], grads[...])
        ).astype(jnp.bfloat16)
    for piece in range(low.shape[1] // LOW_ROWS):
        low[:, piece * LOW_ROWS : (piece + 1) * LOW_ROWS, :] = packed[
            :, TILE:, piece * 2 * RANK : (piece + 1) * 2 * RANK
        ]
    rows = backs[0].shape[2]
    for step in range(len(backs)):
        target = lax.rem(chip + step, len(backs))
        for holder in range(2):
            begin = pl.multiple_of((target * 2 + holder) * rows, rows)
            backs[step][holder] = returned[:, pl.ds(begin, rows)]
            outs[step][holder] = out[pl.ds(begin, rows), :]


def attention(lengths, chip, core, packed, wq_up, wv_up, after):
    seq_size = packed.shape[0]
    rows = packed.shape[1] - LOW_ROWS
    length = seq_size * rows
    width = packed.shape[2] // 4
    heads = width // HEAD_SIZE
    chips = seq_size // 2
    wide_t = pltpu.VMEM((width, length), jnp.bfloat16)
    back = jax.ShapeDtypeStruct((2, 2 * RANK, rows), jnp.bfloat16)
    grad_t = jax.ShapeDtypeStruct((width, length), jnp.bfloat16)
    return pl.pallas_call(
        attention_kernel,
        in_specs=[SMEM] * 3 + [VMEM] * 4,
        out_specs=[VMEM] * (3 + 2 * chips),
        scratch_shapes=[
            wide_t,
            wide_t,
            wide_t,
            wide_t,
            pltpu.VMEM((heads, length, HEAD_SIZE), jnp.float32),
            pltpu.VMEM((2 * RANK, length), jnp.bfloat16),
            pltpu.VMEM((length, width), jnp.bfloat16),
        ],
        out_shape=[jax.ShapeDtypeStruct((2, rows, width), jnp.bfloat16)] * chips
        + [back] * chips
        + [grad_t, grad_t]
        + [jax.ShapeDtypeStruct((seq_size, rows // 2, 2 * RANK), jnp.bfloat16)],
        compiler_params=pltpu.CompilerParams(vmem_limit_bytes=32 << 20),
        cost_estimate=pl.CostEstimate(
            flops=8 << 30, bytes_accessed=16 << 20, transcendentals=4 << 20
        ),
        name="attention",
    )(lengths, chip, core, packed, wq_up, wv_up, after)


def up_kernel(core, low, low_other, dq_t, dv_t, up, lows):
    lows[core[0]] = low[...]
    lows[1 - core[0]] = low_other[...]
    devices, half, _ = low.shape
    for part, grads in enumerate((dq_t, dv_t)):
        upper = lower = jnp.zeros((grads.shape[0], 2 * RANK), jnp.float32)
        for device in range(devices):
            begin = 2 * device * half
            upper += dot(grads[:, begin : begin + half], lows[part, device])
            lower += dot(grads[:, begin + half : begin + 2 * half], lows[part, device])
        share = ADAPTER_SCALE * (upper.T[:RANK] + lower.T[RANK:])
        up[part * RANK : (part + 1) * RANK, :] = share.astype(jnp.bfloat16)


def up_gradient(core, low, low_other, dq_t, dv_t):
    return pl.pallas_call(
        up_kernel,
        in_specs=[SMEM] + [VMEM] * 4,
        out_specs=VMEM,
        out_shape=jax.ShapeDtypeStruct((2 * RANK, dq_t.shape[0]), jnp.bfloat16),
        scratch_shapes=[pltpu.VMEM((2,) + low.shape, jnp.bfloat16)],
        compiler_params=pltpu.CompilerParams(vmem_limit_bytes=16 << 20),
        name="up_gradient",
    )(core, low, low_other, dq_t, dv_t)


def pick_kernel(core, part_0, part_1, part_2, part_3, out):
    core = core[0]
    for step, part in enumerate((part_0, part_1, part_2, part_3)):
        out[step] = part[1 - core]


def pick(core, parts):
    return pl.pallas_call(
        pick_kernel,
        in_specs=[SMEM] + [VMEM] * len(parts),
        out_specs=VMEM,
        out_shape=jax.ShapeDtypeStruct((len(parts),) + parts[0].shape[1:], parts[0].dtype),
        compiler_params=pltpu.CompilerParams(vmem_limit_bytes=SMALL_VMEM),
        name="pick",
    )(core, *parts)


def arrive_kernel(chip, core, part_0, part_1, part_2, part_3, other, out, done):
    chip, core = chip[0], core[0]
    parts = (part_0, part_1, part_2, part_3)
    width = part_0.shape[2]
    for step in range(len(parts)):
        origin = lax.rem(chip + len(parts) - step, len(parts))
        here = pl.multiple_of((origin * 2 + core) * width, width)
        there = pl.multiple_of((origin * 2 + 1 - core) * width, width)
        out[0, :, pl.ds(here, width)] = parts[step][core]
        out[0, :, pl.ds(there, width)] = other[step]
    done[...] = jnp.zeros_like(done)


def arrive(chip, core, parts, other):
    _, rows, width = parts[0].shape
    return pl.pallas_call(
        arrive_kernel,
        in_specs=[SMEM] * 2 + [VMEM] * (len(parts) + 1),
        out_specs=[VMEM] * 2,
        out_shape=[
            jax.ShapeDtypeStruct((1, rows, 2 * len(parts) * width), parts[0].dtype),
            DONE,
        ],
        compiler_params=pltpu.CompilerParams(vmem_limit_bytes=SMALL_VMEM),
        name="arrive",
    )(chip, core, *parts, other)


def backs_kernel(part_0, part_1, part_2, part_3, *refs):
    out = refs[len(refs) // 2]
    total = part_0[...].astype(jnp.float32)
    for part in (part_1, part_2, part_3):
        total += part[...].astype(jnp.float32)
    out[...] = total.astype(out.dtype)


def sum_backs(parts, held):
    count = len(parts)
    return pl.pallas_call(
        backs_kernel,
        in_specs=[VMEM] * (count + len(held)),
        out_specs=[VMEM] * (1 + len(held)),
        out_shape=[
            jax.ShapeDtypeStruct(part.shape, part.dtype) for part in [parts[0]] + list(held)
        ],
        input_output_aliases={count + index: 1 + index for index in range(len(held))},
        compiler_params=pltpu.CompilerParams(vmem_limit_bytes=SMALL_VMEM),
        name="sum_backs",
    )(*parts, *held)


def halves_kernel(core, hidden, other, out, done):
    rows, half = other.shape
    out[:rows] = hidden[:, pl.ds(pl.multiple_of(core[0] * half, half), half)]
    out[rows:] = other[...]
    done[...] = jnp.zeros_like(done)


def halves(core, hidden, other):
    rows, half = other.shape
    return pl.pallas_call(
        halves_kernel,
        in_specs=[SMEM, VMEM, VMEM],
        out_specs=[VMEM] * 2,
        out_shape=[jax.ShapeDtypeStruct((2 * rows, half), hidden.dtype), DONE],
        compiler_params=pltpu.CompilerParams(vmem_limit_bytes=SMALL_VMEM),
        name="halves",
    )(core, hidden, other)


def down_kernel(core, *refs):
    *parts, hidden, up, out, back = refs
    rows = parts[0].shape[2]

    @pl.when(pl.program_id(0) == 0)
    def _():
        total = parts[0][...].astype(jnp.float32)
        for part in parts[1:]:
            total += part[...].astype(jnp.float32)
        back[...] = total.astype(jnp.bfloat16)

    grad = dot(back[core[0]], hidden[:rows]) + dot(back[1 - core[0]], hidden[rows:])
    grad = grad.astype(out.dtype)
    for row in range(out.shape[0]):
        across = slice(row * SHARE_ROWS, (row + 1) * SHARE_ROWS)
        out[row, 0, :, :DOWN_COLS] = grad[across, :]
        out[row, 0, :, DOWN_COLS:] = up[across, :]


def down_gradient(core, parts, hidden, up):
    rows, half = hidden.shape
    steps = half // DOWN_COLS
    across = 2 * RANK // SHARE_ROWS
    shape = parts[0].shape
    return pl.pallas_call(
        down_kernel,
        grid_spec=pltpu.PrefetchScalarGridSpec(
            num_scalar_prefetch=1,
            grid=(steps,),
            in_specs=[pl.BlockSpec(shape, lambda i, core: (0, 0, 0))] * len(parts)
            + [
                pl.BlockSpec((rows, DOWN_COLS), lambda i, core: (0, i)),
                pl.BlockSpec((2 * RANK, UP_COLS), lambda i, core: (0, i)),
            ],
            out_specs=pl.BlockSpec(
                (across, 1, SHARE_ROWS, DOWN_COLS + UP_COLS), lambda i, core: (0, i, 0, 0)
            ),
            scratch_shapes=[pltpu.VMEM(shape, jnp.bfloat16)],
        ),
        out_shape=jax.ShapeDtypeStruct(
            (across, steps, SHARE_ROWS, DOWN_COLS + UP_COLS), jnp.bfloat16
        ),
        compiler_params=pltpu.CompilerParams(vmem_limit_bytes=24 << 20),
        name="down_gradient",
    )(core, *parts, hidden, up)


def share_kernel(parts, *refs):
    out = refs[-1]
    total = parts[0].astype(jnp.float32)
    for part in range(1, parts.shape[0]):
        total += parts[part].astype(jnp.float32)
    out[...] = total.astype(out.dtype)


def sum_share(parts, after):
    return pl.pallas_call(
        share_kernel,
        in_specs=[VMEM] + [VMEM] * len(after),
        out_specs=VMEM,
        out_shape=jax.ShapeDtypeStruct(parts.shape[1:], parts.dtype),
        compiler_params=pltpu.CompilerParams(vmem_limit_bytes=SMALL_VMEM),
        name="sum_share",
    )(parts, *after)


def chips_kernel(chip, *refs):
    *parts, out = refs
    chip = chip[0]
    total = parts[0][:, :DOWN_COLS].astype(jnp.float32)
    for part in parts[1:]:
        total += part[:, :DOWN_COLS].astype(jnp.float32)
    total = total.astype(out.dtype)
    for device in range(out.shape[0]):
        out[device, :, :DOWN_COLS] = total
    for step, part in enumerate(parts):
        origin = lax.rem(chip + len(parts) - step, len(parts))
        begin = pl.multiple_of(DOWN_COLS + origin * UP_COLS, UP_COLS)
        for device in range(out.shape[0]):
            out[device, :, pl.ds(begin, UP_COLS)] = part[:, DOWN_COLS:]


def sum_chips(chip, parts, devices):
    shape = (devices, SHARE_ROWS, DOWN_COLS + len(parts) * UP_COLS)
    return pl.pallas_call(
        chips_kernel,
        in_specs=[SMEM] + [VMEM] * len(parts),
        out_specs=VMEM,
        out_shape=jax.ShapeDtypeStruct(shape, parts[0].dtype),
        compiler_params=pltpu.CompilerParams(vmem_limit_bytes=SMALL_VMEM),
        name="sum_chips",
    )(chip, *parts)


def place_kernel(which, shares, *refs):
    *outs, downs, ups, sems = refs[-7:]
    which = which[0]
    half = shares.shape[0] // 2
    columns = shares.shape[1]
    copies = []

    def send(source, target, begin, size):
        begin = pl.multiple_of(begin, size)
        copies.append(
            pltpu.make_async_copy(source, target.at[:, pl.ds(begin, size)], sems.at[len(copies)])
        )
        copies[-1].start()

    chips, _, width = ups.shape
    for row in range(2 * half):
        part, across = row // half, slice(row % half * SHARE_ROWS, (row % half + 1) * SHARE_ROWS)
        for column in range(columns):
            share = shares[row, column]
            downs[part, across, column * DOWN_COLS : (column + 1) * DOWN_COLS] = share[
                :, :DOWN_COLS
            ].astype(jnp.float32)
            for chip in range(chips):
                begin = DOWN_COLS + chip * UP_COLS
                ups[
                    chip,
                    row * SHARE_ROWS : (row + 1) * SHARE_ROWS,
                    column * UP_COLS : (column + 1) * UP_COLS,
                ] = share[:, begin : begin + UP_COLS].astype(jnp.float32)
        if row % half == half - 1:
            send(downs.at[part], outs[2 * part], which * downs.shape[2], downs.shape[2])
            for chip in range(chips):
                send(
                    ups.at[chip, part * RANK : (part + 1) * RANK, :],
                    outs[2 * part + 1],
                    (2 * chip + which) * width,
                    width,
                )
    for copy in copies:
        copy.wait()


def place(which, shares, model, width, earlier=()):
    shapes = [(RANK, model), (RANK, width), (RANK, model), (RANK, width)]
    columns = shares.shape[1]
    chips = (shares.shape[3] - DOWN_COLS) // UP_COLS
    return pl.pallas_call(
        place_kernel,
        in_specs=[SMEM, VMEM] + [ANY] * len(earlier),
        out_specs=[ANY] * 4,
        out_shape=[jax.ShapeDtypeStruct(shape, jnp.float32) for shape in shapes],
        scratch_shapes=[
            pltpu.VMEM((2, RANK, columns * DOWN_COLS), jnp.float32),
            pltpu.VMEM((chips, 2 * RANK, columns * UP_COLS), jnp.float32),
            pltpu.SemaphoreType.DMA((2 + 2 * chips,)),
        ],
        input_output_aliases={2 + index: index for index in range(len(earlier))},
        compiler_params=pltpu.CompilerParams(vmem_limit_bytes=16 << 20),
        name="place",
    )(which, shares, *earlier)


def swap(x, axes):
    return lax.all_to_all(x, axes, 0, 0, tiled=True)


def to_other_core(x):
    return lax.ppermute(x, "core", [(0, 1), (1, 0)])


def per_device(
    sizes,
    hidden,
    frozen_queries,
    frozen_keys,
    frozen_values,
    document_length_list,
    query_down_weight,
    query_up_weight,
    value_down_weight,
    value_up_weight,
    output_gradient,
):
    dp_size, seq_size = sizes
    chips = seq_size // 2
    rows, model = hidden.shape[1:]
    half = model // 2
    chip = lax.axis_index("y").astype(jnp.int32)[None]
    core = lax.axis_index("core").astype(jnp.int32)[None]
    width = frozen_queries.shape[2] // seq_size

    def to_chip(x, step):
        return lax.ppermute(x, "y", [(c, (c + step) % chips) for c in range(chips)])

    packed, hidden_leaving = pack(
        core,
        hidden[0],
        query_down_weight.T,
        value_down_weight.T,
        frozen_queries[0],
        frozen_keys[0],
        frozen_values[0],
        output_gradient[0],
        query_up_weight,
        value_up_weight,
        seq_size,
    )
    received = swap(packed, SEQ)
    hidden_other = to_other_core(hidden_leaving)
    hidden_half, halves_done = halves(core, hidden[0], hidden_other)
    *outs, dq_t, dv_t, low = attention(
        document_length_list,
        chip,
        core,
        received,
        query_up_weight,
        value_up_weight,
        after=halves_done,
    )
    parts, backs = outs[:chips], outs[chips:]

    backs = [backs[0]] + [to_chip(backs[step], step) for step in range(1, chips)]
    back, *held = sum_backs(backs, parts[-2:])
    parts = parts[:-2] + held
    back_other = to_other_core(back)
    parts = [parts[0]] + [to_chip(parts[step], step) for step in range(1, chips)]
    up = up_gradient(core, low, to_other_core(low), dq_t, dv_t)
    down = down_gradient(core, [back, back_other], hidden_half, up)

    other = to_other_core(pick(core, parts))
    attended, attended_done = arrive(chip, core, parts, other)

    shares = swap(down.reshape((-1,) + down.shape[2:]), DP)
    share = sum_share(shares, after=[attended_done])
    share = [share] + [to_chip(share, step) for step in range(1, chips)]
    shares = swap(sum_chips(chip, share, shares.shape[0]), DP)
    shares = shares.reshape(down.shape[:2] + shares.shape[1:])
    shares_other = to_other_core(shares)
    grads = place(core, shares, model, seq_size * width)
    grad_a_q, up_q, grad_a_v, up_v = place(
        1 - core, shares_other, model, seq_size * width, earlier=grads
    )
    return attended, grad_a_q.T, up_q, grad_a_v.T, up_v


def solution(mesh):
    dp_size, seq_size = mesh.shape["dp"], mesh.shape["seq"]
    fine = Mesh(mesh.devices.reshape(4, 4, 4, 2), ALL)
    rows = P(DP, SEQ, None)
    in_specs = (rows, rows, rows, rows, P(DP, None), P(), P(), P(), P(), rows)
    out_specs = (rows, P(), P(), P(), P())
    return jax.shard_map(
        functools.partial(per_device, (dp_size, seq_size)),
        mesh=fine,
        in_specs=in_specs,
        out_specs=out_specs,
        check_vma=False,
    )
```

```python
import functools

import jax
import jax.numpy as jnp
from jax import lax
from jax.experimental import pallas as pl
from jax.experimental.pallas import tpu as pltpu
from jax.sharding import Mesh
from jax.sharding import PartitionSpec as P

HEAD_COUNT = 16
HEAD_SIZE = 128
RANK = 64
NDOC = 8
TILE = 256
MAX_TILES = 5
ADAPTER_SCALE = 2.0
NEG_FILL = -1e30
SCALING = HEAD_SIZE ** (-0.5)
LOG2_E = 1.4426950408889634

SHARE_ROWS = 16
DOWN_COLS = 1024
UP_COLS = 128

DP = ("x", "z")
SEQ = ("y", "core")
ALL = ("x", "z", "y", "core")
NT = (((1,), (1,)), ((), ()))


def dot(a, b):
    return jnp.dot(a, b, preferred_element_type=jnp.float32)


def dot_nt(a, b):
    return lax.dot_general(a, b, NT, preferred_element_type=jnp.float32)


LOW_ROWS = 16

HIDDEN_PARTS = 4
PACK_VMEM = 56 << 20
SMALL_VMEM = 8 << 20
VMEM = pl.BlockSpec(memory_space=pltpu.VMEM)
SMEM = pl.BlockSpec(memory_space=pltpu.SMEM)
ANY = pl.BlockSpec(memory_space=pl.ANY)
DONE = jax.ShapeDtypeStruct((8, 128), jnp.float32)


def pack_kernel(
    core, hidden, wq_down, wv_down, fq, fk, fv, grad, wq_up, wv_up, out, other,
    hidden_v, down_v, fq_v, fv_v, wq_up_v, wv_up_v, out_v, low,
    down_sems, hidden_sems, row_sems, through_sems, out_sems, other_sem,
):
    devices, _, packed = out.shape
    width = packed // 4
    rows, model = hidden.shape
    step = model // HIDDEN_PARTS

    def part(index):
        return pl.ds(index * step, step)

    def columns(index):
        return pl.ds(index * width, width)

    downs = [
        pltpu.make_async_copy(wq_down, down_v.at[pl.ds(0, RANK)], down_sems.at[0]),
        pltpu.make_async_copy(wv_down, down_v.at[pl.ds(RANK, RANK)], down_sems.at[1]),
    ]
    hiddens = [
        pltpu.make_async_copy(
            hidden.at[:, part(index)], hidden_v.at[:, part(index)], hidden_sems.at[index]
        )
        for index in range(HIDDEN_PARTS)
    ]
    through = [
        pltpu.make_async_copy(
            source.at[:, columns(device)],
            out_v.at[device, pl.ds(0, rows), columns(which)],
            through_sems.at[which - 2, device],
        )
        for device in range(devices)
        for which, source in ((2, fk), (3, grad))
    ]
    whole = [
        pltpu.make_async_copy(wq_up, wq_up_v, row_sems.at[0]),
        pltpu.make_async_copy(fq, fq_v, row_sems.at[1]),
        pltpu.make_async_copy(wv_up, wv_up_v, row_sems.at[2]),
        pltpu.make_async_copy(fv, fv_v, row_sems.at[3]),
    ]
    for copy in downs + hiddens + through + whole:
        copy.start()

    def leave(device, begin, size, number):
        at = (device, slice(None), pl.ds(begin, size))
        copy = pltpu.make_async_copy(out_v.at[at], out.at[at], out_sems.at[number, device])
        copy.start()
        return copy

    for copy in downs:
        copy.wait()
    total = jnp.zeros((rows, 2 * RANK), jnp.float32)
    for index in range(HIDDEN_PARTS):
        hiddens[index].wait()
        total += dot_nt(hidden_v[:, part(index)], down_v[:, part(index)])
    low[...] = total.astype(jnp.bfloat16)
    half = other.shape[1]
    begin = pl.multiple_of((1 - core[0]) * half, half)
    other_copy = pltpu.make_async_copy(hidden_v.at[:, pl.ds(begin, half)], other, other_sem)
    other_copy.start()
    upper, lower = total[: rows // 2], total[rows // 2 :]
    left = lax.broadcasted_iota(jnp.int32, upper.shape, 1) < RANK
    sides = (
        jnp.where(left, upper, pltpu.roll(lower, RANK, 1)).astype(jnp.bfloat16),
        jnp.where(left, pltpu.roll(upper, RANK, 1), lower).astype(jnp.bfloat16),
    )
    outs = []
    for device in range(devices):
        for piece in range(rows // 2 // LOW_ROWS):
            out_v[device, rows:, piece * 2 * RANK : (piece + 1) * 2 * RANK] = sides[device % 2][
                piece * LOW_ROWS : (piece + 1) * LOW_ROWS
            ]
        through[2 * device].wait()
        through[2 * device + 1].wait()
        outs.append(leave(device, 2 * width, 2 * width, 0))
    for copy in whole:
        copy.wait()
    for device in range(devices):
        at = slice(device * width, (device + 1) * width)
        for which, (frozen, weight) in enumerate(((fq_v, wq_up_v), (fv_v, wv_up_v))):
            added = ADAPTER_SCALE * dot(low[:, which * RANK : (which + 1) * RANK], weight[:, at])
            out_v[device, :rows, which * width : (which + 1) * width] = (
                frozen[:, at].astype(jnp.float32) + added
            ).astype(jnp.bfloat16)
        outs.append(leave(device, 0, 2 * width, 1))
    for copy in outs:
        copy.wait()
    other_copy.wait()


def pack(core, hidden, wq_down_t, wv_down_t, fq, fk, fv, grad, wq_up, wv_up, seq_size):
    rows, model = hidden.shape
    columns = fq.shape[1]
    width = columns // seq_size
    bf16 = jnp.bfloat16
    return pl.pallas_call(
        pack_kernel,
        in_specs=[SMEM] + [ANY] * 9,
        out_specs=[ANY] * 2,
        out_shape=[
            jax.ShapeDtypeStruct((seq_size, rows + LOW_ROWS, 4 * width), bf16),
            jax.ShapeDtypeStruct((rows, model // 2), bf16),
        ],
        scratch_shapes=[
            pltpu.VMEM((rows, model), bf16),
            pltpu.VMEM((2 * RANK, model), bf16),
            pltpu.VMEM((rows, columns), bf16),
            pltpu.VMEM((rows, columns), bf16),
            pltpu.VMEM((RANK, columns), bf16),
            pltpu.VMEM((RANK, columns), bf16),
            pltpu.VMEM((seq_size, rows + LOW_ROWS, 4 * width), bf16),
            pltpu.VMEM((rows, 2 * RANK), bf16),
            pltpu.SemaphoreType.DMA((2,)),
            pltpu.SemaphoreType.DMA((HIDDEN_PARTS,)),
            pltpu.SemaphoreType.DMA((4,)),
            pltpu.SemaphoreType.DMA((2, seq_size)),
            pltpu.SemaphoreType.DMA((2, seq_size)),
            pltpu.SemaphoreType.DMA,
        ],
        compiler_params=pltpu.CompilerParams(vmem_limit_bytes=PACK_VMEM),
        name="pack",
    )(core, hidden, wq_down_t, wv_down_t, fq, fk, fv, grad, wq_up, wv_up)


def attention_kernel(
    lengths, chip, core, received, wq_up, wv_up, *refs
):
    *outs, dq_t, dv_t, low, q_t, k_t, v_t, g_t, dv, returned, out = refs[1:-5]
    packed, wq_v, wv_v, sems, up_sems = refs[-5:]
    outs, backs = outs[: len(outs) // 2], outs[len(outs) // 2 :]
    length = out.shape[0]
    heads = out.shape[1] // HEAD_SIZE
    width = heads * HEAD_SIZE
    blocks = length // TILE
    chip, core = chip[0], core[0]
    own_columns = pl.ds(pl.multiple_of((chip * 2 + core) * width, width), width)
    span = [slice(head * HEAD_SIZE, (head + 1) * HEAD_SIZE) for head in range(heads)]

    def columns(which, head):
        begin = which * width + head * HEAD_SIZE
        return slice(begin, begin + HEAD_SIZE)

    def tiles_of(first, count, which, head):
        rows = packed[pl.ds(first, count), :TILE, columns(which, head)]
        return rows.reshape(count * TILE, HEAD_SIZE)

    sections = []
    for which in range(4):
        for device in range(blocks):
            at = (device, slice(None), pl.ds(which * width, width))
            sections.append(
                pltpu.make_async_copy(received.at[at], packed.at[at], sems.at[which, device])
            )
    ups = [
        pltpu.make_async_copy(wq_up.at[:, own_columns], wq_v, up_sems.at[0]),
        pltpu.make_async_copy(wv_up.at[:, own_columns], wv_v, up_sems.at[1]),
    ]
    for copy in sections + ups:
        copy.start()
    dv[...] = jnp.zeros_like(dv)
    for which, turned in enumerate((q_t, v_t, k_t, g_t)):
        for copy in sections[which * blocks : (which + 1) * blocks]:
            copy.wait()
        for head in range(heads):
            turned[span[head], :] = tiles_of(0, blocks, which, head).T

    def block(index, _):
        row0 = pl.multiple_of(index * TILE, TILE)
        q_rows = pl.ds(row0, TILE)
        position = row0 + lax.broadcasted_iota(jnp.int32, (1, TILE), 1)
        begin = jnp.zeros((1, TILE), jnp.int32)
        first = jnp.int32(0)
        end = jnp.int32(0)
        for doc in range(NDOC):
            end = end + lengths[0, doc]
            begin = jnp.where(position >= end, end, begin)
            first = jnp.where(row0 >= end, end, first)
        tiles = index - lax.div(first, TILE) + 1

        def body(count):
            tile0 = index + 1 - count
            key0 = pl.multiple_of(tile0 * TILE, TILE)
            k_rows = pl.ds(key0, count * TILE)
            key_index = lax.broadcasted_iota(jnp.int32, (count * TILE, TILE), 0)
            in_document = key_index >= begin - key0
            causal = lax.broadcasted_iota(jnp.int32, (TILE, TILE), 0) <= (
                lax.broadcasted_iota(jnp.int32, (TILE, TILE), 1)
            )
            held = []
            for head in range(heads):
                scores = dot(tiles_of(tile0, count, 2, head), q_t[span[head], q_rows])
                prob_grad = dot(tiles_of(tile0, count, 1, head), g_t[span[head], q_rows])
                scores = jnp.where(in_document, scores, NEG_FILL)
                last = jnp.where(causal, scores[(count - 1) * TILE :], NEG_FILL)
                if count > 1:
                    scores = jnp.concatenate([scores[: (count - 1) * TILE], last], axis=0)
                else:
                    scores = last
                maximum = jnp.max(scores, axis=0, keepdims=True)
                powers = jnp.exp2((scores - maximum) * (SCALING * LOG2_E))
                inverse = 1.0 / jnp.sum(powers, axis=0, keepdims=True)
                held.append((prob_grad, powers.astype(jnp.bfloat16), inverse))
            for head in range(heads):
                prob_grad, rounded, inverse = held[head]
                powers = rounded.astype(jnp.float32)
                result = (dot(v_t[span[head], k_rows], rounded) * inverse).astype(jnp.bfloat16)
                row_dot = jnp.sum(powers * prob_grad, axis=0, keepdims=True) * inverse
                g_wide = g_t[span[head], q_rows].astype(jnp.float32)
                score_grad = rounded * (prob_grad - row_dot).astype(jnp.bfloat16)
                query_grad = dot(k_t[span[head], k_rows], score_grad) * (inverse * SCALING)
                dq_t[span[head], q_rows] = query_grad.astype(jnp.bfloat16)
                out[q_rows, span[head]] = result.T
                g_scaled = (g_wide * inverse).astype(jnp.bfloat16).T
                dv[head, k_rows, :] += dot(rounded, g_scaled)

        for count in range(1, min(MAX_TILES, blocks) + 1):
            pl.when(tiles == count)(functools.partial(body, count))
        return 0

    lax.fori_loop(0, blocks, block, 0)
    for head in range(heads):
        dv_t[span[head], :] = dv[head].astype(jnp.bfloat16).T

    for copy in ups:
        copy.wait()
    for part, (grads, weight) in enumerate(((dq_t, wq_v), (dv_t, wv_v))):
        returned[part * RANK : (part + 1) * RANK, :] = (
            ADAPTER_SCALE * dot(weight[...], grads[...])
        ).astype(jnp.bfloat16)
    for piece in range(low.shape[1] // LOW_ROWS):
        low[:, piece * LOW_ROWS : (piece + 1) * LOW_ROWS, :] = packed[
            :, TILE:, piece * 2 * RANK : (piece + 1) * 2 * RANK
        ]
    rows = backs[0].shape[2]
    for step in range(len(backs)):
        target = lax.rem(chip + step, len(backs))
        for holder in range(2):
            begin = pl.multiple_of((target * 2 + holder) * rows, rows)
            backs[step][holder] = returned[:, pl.ds(begin, rows)]
            outs[step][holder] = out[pl.ds(begin, rows), :]


def attention(lengths, chip, core, packed, wq_up, wv_up, after):
    seq_size = packed.shape[0]
    rows = packed.shape[1] - LOW_ROWS
    length = seq_size * rows
    width = packed.shape[2] // 4
    heads = width // HEAD_SIZE
    chips = seq_size // 2
    wide_t = pltpu.VMEM((width, length), jnp.bfloat16)
    back = jax.ShapeDtypeStruct((2, 2 * RANK, rows), jnp.bfloat16)
    grad_t = jax.ShapeDtypeStruct((width, length), jnp.bfloat16)
    return pl.pallas_call(
        attention_kernel,
        in_specs=[SMEM] * 3 + [ANY] * 3 + [VMEM],
        out_specs=[VMEM] * (3 + 2 * chips),
        scratch_shapes=[
            wide_t,
            wide_t,
            wide_t,
            wide_t,
            pltpu.VMEM((heads, length, HEAD_SIZE), jnp.float32),
            pltpu.VMEM((2 * RANK, length), jnp.bfloat16),
            pltpu.VMEM((length, width), jnp.bfloat16),
            pltpu.VMEM(packed.shape, jnp.bfloat16),
            pltpu.VMEM((RANK, width), jnp.bfloat16),
            pltpu.VMEM((RANK, width), jnp.bfloat16),
            pltpu.SemaphoreType.DMA((4, seq_size)),
            pltpu.SemaphoreType.DMA((2,)),
        ],
        out_shape=[jax.ShapeDtypeStruct((2, rows, width), jnp.bfloat16)] * chips
        + [back] * chips
        + [grad_t, grad_t]
        + [jax.ShapeDtypeStruct((seq_size, rows // 2, 2 * RANK), jnp.bfloat16)],
        compiler_params=pltpu.CompilerParams(vmem_limit_bytes=32 << 20),
        cost_estimate=pl.CostEstimate(
            flops=8 << 30, bytes_accessed=16 << 20, transcendentals=4 << 20
        ),
        name="attention",
    )(lengths, chip, core, packed, wq_up, wv_up, after)


def up_kernel(core, low, low_other, dq_t, dv_t, up, lows):
    lows[core[0]] = low[...]
    lows[1 - core[0]] = low_other[...]
    devices, half, _ = low.shape
    for part, grads in enumerate((dq_t, dv_t)):
        upper = lower = jnp.zeros((grads.shape[0], 2 * RANK), jnp.float32)
        for device in range(devices):
            begin = 2 * device * half
            upper += dot(grads[:, begin : begin + half], lows[part, device])
            lower += dot(grads[:, begin + half : begin + 2 * half], lows[part, device])
        share = ADAPTER_SCALE * (upper.T[:RANK] + lower.T[RANK:])
        up[part * RANK : (part + 1) * RANK, :] = share.astype(jnp.bfloat16)


def up_gradient(core, low, low_other, dq_t, dv_t):
    return pl.pallas_call(
        up_kernel,
        in_specs=[SMEM] + [VMEM] * 4,
        out_specs=VMEM,
        out_shape=jax.ShapeDtypeStruct((2 * RANK, dq_t.shape[0]), jnp.bfloat16),
        scratch_shapes=[pltpu.VMEM((2,) + low.shape, jnp.bfloat16)],
        compiler_params=pltpu.CompilerParams(vmem_limit_bytes=16 << 20),
        name="up_gradient",
    )(core, low, low_other, dq_t, dv_t)


def pick_kernel(core, part_0, part_1, part_2, part_3, out):
    core = core[0]
    for step, part in enumerate((part_0, part_1, part_2, part_3)):
        out[step] = part[1 - core]


def pick(core, parts):
    return pl.pallas_call(
        pick_kernel,
        in_specs=[SMEM] + [VMEM] * len(parts),
        out_specs=VMEM,
        out_shape=jax.ShapeDtypeStruct((len(parts),) + parts[0].shape[1:], parts[0].dtype),
        compiler_params=pltpu.CompilerParams(vmem_limit_bytes=SMALL_VMEM),
        name="pick",
    )(core, *parts)


def arrive_kernel(chip, core, part_0, part_1, part_2, part_3, other, out, done):
    chip, core = chip[0], core[0]
    parts = (part_0, part_1, part_2, part_3)
    width = part_0.shape[2]
    for step in range(len(parts)):
        origin = lax.rem(chip + len(parts) - step, len(parts))
        here = pl.multiple_of((origin * 2 + core) * width, width)
        there = pl.multiple_of((origin * 2 + 1 - core) * width, width)
        out[0, :, pl.ds(here, width)] = parts[step][core]
        out[0, :, pl.ds(there, width)] = other[step]
    done[...] = jnp.zeros_like(done)


def arrive(chip, core, parts, other):
    _, rows, width = parts[0].shape
    return pl.pallas_call(
        arrive_kernel,
        in_specs=[SMEM] * 2 + [VMEM] * (len(parts) + 1),
        out_specs=[VMEM] * 2,
        out_shape=[
            jax.ShapeDtypeStruct((1, rows, 2 * len(parts) * width), parts[0].dtype),
            DONE,
        ],
        compiler_params=pltpu.CompilerParams(vmem_limit_bytes=SMALL_VMEM),
        name="arrive",
    )(chip, core, *parts, other)


def backs_kernel(part_0, part_1, part_2, part_3, *refs):
    out = refs[len(refs) // 2]
    total = part_0[...].astype(jnp.float32)
    for part in (part_1, part_2, part_3):
        total += part[...].astype(jnp.float32)
    out[...] = total.astype(out.dtype)


def sum_backs(parts, held):
    count = len(parts)
    return pl.pallas_call(
        backs_kernel,
        in_specs=[VMEM] * (count + len(held)),
        out_specs=[VMEM] * (1 + len(held)),
        out_shape=[
            jax.ShapeDtypeStruct(part.shape, part.dtype) for part in [parts[0]] + list(held)
        ],
        input_output_aliases={count + index: 1 + index for index in range(len(held))},
        compiler_params=pltpu.CompilerParams(vmem_limit_bytes=SMALL_VMEM),
        name="sum_backs",
    )(*parts, *held)


def halves_kernel(core, hidden, other, out, done):
    rows, half = other.shape
    out[:rows] = hidden[:, pl.ds(pl.multiple_of(core[0] * half, half), half)]
    out[rows:] = other[...]
    done[...] = jnp.zeros_like(done)


def halves(core, hidden, other):
    rows, half = other.shape
    return pl.pallas_call(
        halves_kernel,
        in_specs=[SMEM, VMEM, VMEM],
        out_specs=[VMEM] * 2,
        out_shape=[jax.ShapeDtypeStruct((2 * rows, half), hidden.dtype), DONE],
        compiler_params=pltpu.CompilerParams(vmem_limit_bytes=SMALL_VMEM),
        name="halves",
    )(core, hidden, other)


def down_kernel(core, *refs):
    *parts, hidden, up, out, back = refs
    rows = parts[0].shape[2]

    @pl.when(pl.program_id(0) == 0)
    def _():
        total = parts[0][...].astype(jnp.float32)
        for part in parts[1:]:
            total += part[...].astype(jnp.float32)
        back[...] = total.astype(jnp.bfloat16)

    grad = dot(back[core[0]], hidden[:rows]) + dot(back[1 - core[0]], hidden[rows:])
    grad = grad.astype(out.dtype)
    for row in range(out.shape[0]):
        across = slice(row * SHARE_ROWS, (row + 1) * SHARE_ROWS)
        out[row, 0, :, :DOWN_COLS] = grad[across, :]
        out[row, 0, :, DOWN_COLS:] = up[across, :]


def down_gradient(core, parts, hidden, up):
    rows, half = hidden.shape
    steps = half // DOWN_COLS
    across = 2 * RANK // SHARE_ROWS
    shape = parts[0].shape
    return pl.pallas_call(
        down_kernel,
        grid_spec=pltpu.PrefetchScalarGridSpec(
            num_scalar_prefetch=1,
            grid=(steps,),
            in_specs=[pl.BlockSpec(shape, lambda i, core: (0, 0, 0))] * len(parts)
            + [
                pl.BlockSpec((rows, DOWN_COLS), lambda i, core: (0, i)),
                pl.BlockSpec((2 * RANK, UP_COLS), lambda i, core: (0, i)),
            ],
            out_specs=pl.BlockSpec(
                (across, 1, SHARE_ROWS, DOWN_COLS + UP_COLS), lambda i, core: (0, i, 0, 0)
            ),
            scratch_shapes=[pltpu.VMEM(shape, jnp.bfloat16)],
        ),
        out_shape=jax.ShapeDtypeStruct(
            (across, steps, SHARE_ROWS, DOWN_COLS + UP_COLS), jnp.bfloat16
        ),
        compiler_params=pltpu.CompilerParams(vmem_limit_bytes=24 << 20),
        name="down_gradient",
    )(core, *parts, hidden, up)


def share_kernel(parts, *refs):
    out = refs[-1]
    total = parts[0].astype(jnp.float32)
    for part in range(1, parts.shape[0]):
        total += parts[part].astype(jnp.float32)
    out[...] = total.astype(out.dtype)


def sum_share(parts, after):
    return pl.pallas_call(
        share_kernel,
        in_specs=[VMEM] + [VMEM] * len(after),
        out_specs=VMEM,
        out_shape=jax.ShapeDtypeStruct(parts.shape[1:], parts.dtype),
        compiler_params=pltpu.CompilerParams(vmem_limit_bytes=SMALL_VMEM),
        name="sum_share",
    )(parts, *after)


def chips_kernel(chip, *refs):
    *parts, out = refs
    chip = chip[0]
    total = parts[0][:, :DOWN_COLS].astype(jnp.float32)
    for part in parts[1:]:
        total += part[:, :DOWN_COLS].astype(jnp.float32)
    total = total.astype(out.dtype)
    for device in range(out.shape[0]):
        out[device, :, :DOWN_COLS] = total
    for step, part in enumerate(parts):
        origin = lax.rem(chip + len(parts) - step, len(parts))
        begin = pl.multiple_of(DOWN_COLS + origin * UP_COLS, UP_COLS)
        for device in range(out.shape[0]):
            out[device, :, pl.ds(begin, UP_COLS)] = part[:, DOWN_COLS:]


def sum_chips(chip, parts, devices):
    shape = (devices, SHARE_ROWS, DOWN_COLS + len(parts) * UP_COLS)
    return pl.pallas_call(
        chips_kernel,
        in_specs=[SMEM] + [VMEM] * len(parts),
        out_specs=VMEM,
        out_shape=jax.ShapeDtypeStruct(shape, parts[0].dtype),
        compiler_params=pltpu.CompilerParams(vmem_limit_bytes=SMALL_VMEM),
        name="sum_chips",
    )(chip, *parts)


def place_kernel(which, shares, *refs):
    *outs, downs, ups, sems = refs[-7:]
    which = which[0]
    half = shares.shape[0] // 2
    columns = shares.shape[1]
    copies = []

    def send(source, target, begin, size):
        begin = pl.multiple_of(begin, size)
        copies.append(
            pltpu.make_async_copy(source, target.at[:, pl.ds(begin, size)], sems.at[len(copies)])
        )
        copies[-1].start()

    chips, _, width = ups.shape
    for row in range(2 * half):
        part, across = row // half, slice(row % half * SHARE_ROWS, (row % half + 1) * SHARE_ROWS)
        for column in range(columns):
            share = shares[row, column]
            downs[part, across, column * DOWN_COLS : (column + 1) * DOWN_COLS] = share[
                :, :DOWN_COLS
            ].astype(jnp.float32)
            for chip in range(chips):
                begin = DOWN_COLS + chip * UP_COLS
                ups[
                    chip,
                    row * SHARE_ROWS : (row + 1) * SHARE_ROWS,
                    column * UP_COLS : (column + 1) * UP_COLS,
                ] = share[:, begin : begin + UP_COLS].astype(jnp.float32)
        if row % half == half - 1:
            send(downs.at[part], outs[2 * part], which * downs.shape[2], downs.shape[2])
            for chip in range(chips):
                send(
                    ups.at[chip, part * RANK : (part + 1) * RANK, :],
                    outs[2 * part + 1],
                    (2 * chip + which) * width,
                    width,
                )
    for copy in copies:
        copy.wait()


def place(which, shares, model, width, earlier=()):
    shapes = [(RANK, model), (RANK, width), (RANK, model), (RANK, width)]
    columns = shares.shape[1]
    chips = (shares.shape[3] - DOWN_COLS) // UP_COLS
    return pl.pallas_call(
        place_kernel,
        in_specs=[SMEM, VMEM] + [ANY] * len(earlier),
        out_specs=[ANY] * 4,
        out_shape=[jax.ShapeDtypeStruct(shape, jnp.float32) for shape in shapes],
        scratch_shapes=[
            pltpu.VMEM((2, RANK, columns * DOWN_COLS), jnp.float32),
            pltpu.VMEM((chips, 2 * RANK, columns * UP_COLS), jnp.float32),
            pltpu.SemaphoreType.DMA((2 + 2 * chips,)),
        ],
        input_output_aliases={2 + index: index for index in range(len(earlier))},
        compiler_params=pltpu.CompilerParams(vmem_limit_bytes=16 << 20),
        name="place",
    )(which, shares, *earlier)


def swap(x, axes):
    return lax.all_to_all(x, axes, 0, 0, tiled=True)


def to_other_core(x):
    return lax.ppermute(x, "core", [(0, 1), (1, 0)])


def per_device(
    sizes,
    hidden,
    frozen_queries,
    frozen_keys,
    frozen_values,
    document_length_list,
    query_down_weight,
    query_up_weight,
    value_down_weight,
    value_up_weight,
    output_gradient,
):
    dp_size, seq_size = sizes
    chips = seq_size // 2
    rows, model = hidden.shape[1:]
    half = model // 2
    chip = lax.axis_index("y").astype(jnp.int32)[None]
    core = lax.axis_index("core").astype(jnp.int32)[None]
    width = frozen_queries.shape[2] // seq_size

    def to_chip(x, step):
        return lax.ppermute(x, "y", [(c, (c + step) % chips) for c in range(chips)])

    packed, hidden_leaving = pack(
        core,
        hidden[0],
        query_down_weight.T,
        value_down_weight.T,
        frozen_queries[0],
        frozen_keys[0],
        frozen_values[0],
        output_gradient[0],
        query_up_weight,
        value_up_weight,
        seq_size,
    )
    received = swap(packed, SEQ)
    hidden_other = to_other_core(hidden_leaving)
    hidden_half, halves_done = halves(core, hidden[0], hidden_other)
    *outs, dq_t, dv_t, low = attention(
        document_length_list,
        chip,
        core,
        received,
        query_up_weight,
        value_up_weight,
        after=halves_done,
    )
    parts, backs = outs[:chips], outs[chips:]

    backs = [backs[0]] + [to_chip(backs[step], step) for step in range(1, chips)]
    back, *held = sum_backs(backs, parts[-2:])
    parts = parts[:-2] + held
    back_other = to_other_core(back)
    parts = [parts[0]] + [to_chip(parts[step], step) for step in range(1, chips)]
    up = up_gradient(core, low, to_other_core(low), dq_t, dv_t)
    down = down_gradient(core, [back, back_other], hidden_half, up)

    other = to_other_core(pick(core, parts))
    attended, attended_done = arrive(chip, core, parts, other)

    shares = swap(down.reshape((-1,) + down.shape[2:]), DP)
    share = sum_share(shares, after=[attended_done])
    share = [share] + [to_chip(share, step) for step in range(1, chips)]
    shares = swap(sum_chips(chip, share, shares.shape[0]), DP)
    shares = shares.reshape(down.shape[:2] + shares.shape[1:])
    shares_other = to_other_core(shares)
    grads = place(core, shares, model, seq_size * width)
    grad_a_q, up_q, grad_a_v, up_v = place(
        1 - core, shares_other, model, seq_size * width, earlier=grads
    )
    return attended, grad_a_q.T, up_q, grad_a_v.T, up_v


def solution(mesh):
    dp_size, seq_size = mesh.shape["dp"], mesh.shape["seq"]
    fine = Mesh(mesh.devices.reshape(4, 4, 4, 2), ALL)
    rows = P(DP, SEQ, None)
    in_specs = (rows, rows, rows, rows, P(DP, None), P(), P(), P(), P(), rows)
    out_specs = (rows, P(), P(), P(), P())
    return jax.shard_map(
        functools.partial(per_device, (dp_size, seq_size)),
        mesh=fine,
        in_specs=in_specs,
        out_specs=out_specs,
        check_vma=False,
    )
```

```python
import functools

import jax
import jax.numpy as jnp
from jax import lax
from jax.experimental import pallas as pl
from jax.experimental.pallas import tpu as pltpu
from jax.sharding import Mesh
from jax.sharding import PartitionSpec as P

HEAD_COUNT = 16
HEAD_SIZE = 128
RANK = 64
NDOC = 8
TILE = 256
MAX_TILES = 5
ADAPTER_SCALE = 2.0
NEG_FILL = -1e30
SCALING = HEAD_SIZE ** (-0.5)
LOG2_E = 1.4426950408889634

SHARE_ROWS = 16
DOWN_COLS = 1024
UP_COLS = 128

DP = ("x", "z")
SEQ = ("y", "core")
ALL = ("x", "z", "y", "core")
NT = (((1,), (1,)), ((), ()))


def dot(a, b):
    return jnp.dot(a, b, preferred_element_type=jnp.float32)


def dot_nt(a, b):
    return lax.dot_general(a, b, NT, preferred_element_type=jnp.float32)


LOW_ROWS = 16

HIDDEN_PARTS = 4
PACK_VMEM = 56 << 20
SMALL_VMEM = 8 << 20
VMEM = pl.BlockSpec(memory_space=pltpu.VMEM)
SMEM = pl.BlockSpec(memory_space=pltpu.SMEM)
ANY = pl.BlockSpec(memory_space=pl.ANY)
DONE = jax.ShapeDtypeStruct((8, 128), jnp.float32)


def pack_kernel(
    core, hidden, wq_down, wv_down, fq, fk, fv, grad, wq_up, wv_up, out, other,
    hidden_v, down_v, fq_v, fv_v, wq_up_v, wv_up_v, out_v, low,
    down_sems, hidden_sems, row_sems, through_sems, out_sems, other_sem,
):
    devices, _, packed = out.shape
    width = packed // 4
    rows, model = hidden.shape
    step = model // HIDDEN_PARTS

    def part(index):
        return pl.ds(index * step, step)

    def columns(index):
        return pl.ds(index * width, width)

    downs = [
        pltpu.make_async_copy(wq_down, down_v.at[pl.ds(0, RANK)], down_sems.at[0]),
        pltpu.make_async_copy(wv_down, down_v.at[pl.ds(RANK, RANK)], down_sems.at[1]),
    ]
    hiddens = [
        pltpu.make_async_copy(
            hidden.at[:, part(index)], hidden_v.at[:, part(index)], hidden_sems.at[index]
        )
        for index in range(HIDDEN_PARTS)
    ]
    through = [
        pltpu.make_async_copy(
            source.at[:, columns(device)],
            out_v.at[device, pl.ds(0, rows), columns(which)],
            through_sems.at[which - 2, device],
        )
        for device in range(devices)
        for which, source in ((2, fk), (3, grad))
    ]
    whole = [
        pltpu.make_async_copy(wq_up, wq_up_v, row_sems.at[0]),
        pltpu.make_async_copy(fq, fq_v, row_sems.at[1]),
        pltpu.make_async_copy(wv_up, wv_up_v, row_sems.at[2]),
        pltpu.make_async_copy(fv, fv_v, row_sems.at[3]),
    ]
    for copy in downs + hiddens + through + whole:
        copy.start()

    def leave(device, begin, size, number):
        at = (device, slice(None), pl.ds(begin, size))
        copy = pltpu.make_async_copy(out_v.at[at], out.at[at], out_sems.at[number, device])
        copy.start()
        return copy

    for copy in downs:
        copy.wait()
    total = jnp.zeros((rows, 2 * RANK), jnp.float32)
    for index in range(HIDDEN_PARTS):
        hiddens[index].wait()
        total += dot_nt(hidden_v[:, part(index)], down_v[:, part(index)])
    low[...] = total.astype(jnp.bfloat16)
    half = other.shape[1]
    begin = pl.multiple_of((1 - core[0]) * half, half)
    other_copy = pltpu.make_async_copy(hidden_v.at[:, pl.ds(begin, half)], other, other_sem)
    other_copy.start()
    upper, lower = total[: rows // 2], total[rows // 2 :]
    left = lax.broadcasted_iota(jnp.int32, upper.shape, 1) < RANK
    sides = (
        jnp.where(left, upper, pltpu.roll(lower, RANK, 1)).astype(jnp.bfloat16),
        jnp.where(left, pltpu.roll(upper, RANK, 1), lower).astype(jnp.bfloat16),
    )
    outs = []
    for device in range(devices):
        for piece in range(rows // 2 // LOW_ROWS):
            out_v[device, rows:, piece * 2 * RANK : (piece + 1) * 2 * RANK] = sides[device % 2][
                piece * LOW_ROWS : (piece + 1) * LOW_ROWS
            ]
        through[2 * device].wait()
        through[2 * device + 1].wait()
        outs.append(leave(device, 2 * width, 2 * width, 0))
    for copy in whole:
        copy.wait()
    for device in range(devices):
        at = slice(device * width, (device + 1) * width)
        for which, (frozen, weight) in enumerate(((fq_v, wq_up_v), (fv_v, wv_up_v))):
            added = ADAPTER_SCALE * dot(low[:, which * RANK : (which + 1) * RANK], weight[:, at])
            out_v[device, :rows, which * width : (which + 1) * width] = (
                frozen[:, at].astype(jnp.float32) + added
            ).astype(jnp.bfloat16)
        outs.append(leave(device, 0, 2 * width, 1))
    for copy in outs:
        copy.wait()
    other_copy.wait()


def pack(core, hidden, wq_down_t, wv_down_t, fq, fk, fv, grad, wq_up, wv_up, seq_size):
    rows, model = hidden.shape
    columns = fq.shape[1]
    width = columns // seq_size
    bf16 = jnp.bfloat16
    return pl.pallas_call(
        pack_kernel,
        in_specs=[SMEM] + [ANY] * 9,
        out_specs=[ANY] * 2,
        out_shape=[
            jax.ShapeDtypeStruct((seq_size, rows + LOW_ROWS, 4 * width), bf16),
            jax.ShapeDtypeStruct((rows, model // 2), bf16),
        ],
        scratch_shapes=[
            pltpu.VMEM((rows, model), bf16),
            pltpu.VMEM((2 * RANK, model), bf16),
            pltpu.VMEM((rows, columns), bf16),
            pltpu.VMEM((rows, columns), bf16),
            pltpu.VMEM((RANK, columns), bf16),
            pltpu.VMEM((RANK, columns), bf16),
            pltpu.VMEM((seq_size, rows + LOW_ROWS, 4 * width), bf16),
            pltpu.VMEM((rows, 2 * RANK), bf16),
            pltpu.SemaphoreType.DMA((2,)),
            pltpu.SemaphoreType.DMA((HIDDEN_PARTS,)),
            pltpu.SemaphoreType.DMA((4,)),
            pltpu.SemaphoreType.DMA((2, seq_size)),
            pltpu.SemaphoreType.DMA((2, seq_size)),
            pltpu.SemaphoreType.DMA,
        ],
        compiler_params=pltpu.CompilerParams(vmem_limit_bytes=PACK_VMEM),
        name="pack",
    )(core, hidden, wq_down_t, wv_down_t, fq, fk, fv, grad, wq_up, wv_up)


def attention_kernel(
    lengths, chip, packed, ups, *refs
):
    *outs, dq_t, dv_t, low, q_t, k_t, v_t, g_t, dv, returned, out = refs
    outs, backs = outs[: len(outs) // 2], outs[len(outs) // 2 :]
    length = out.shape[0]
    heads = out.shape[1] // HEAD_SIZE
    width = heads * HEAD_SIZE
    blocks = length // TILE
    chip = chip[0]
    span = [slice(head * HEAD_SIZE, (head + 1) * HEAD_SIZE) for head in range(heads)]

    def columns(which, head):
        begin = which * width + head * HEAD_SIZE
        return slice(begin, begin + HEAD_SIZE)

    def tiles_of(first, count, which, head):
        rows = packed[pl.ds(first, count), :TILE, columns(which, head)]
        return rows.reshape(count * TILE, HEAD_SIZE)

    for head in range(heads):
        q_t[span[head], :] = tiles_of(0, blocks, 0, head).T
        v_t[span[head], :] = tiles_of(0, blocks, 1, head).T
        k_t[span[head], :] = tiles_of(0, blocks, 2, head).T
        g_t[span[head], :] = tiles_of(0, blocks, 3, head).T
    dv[...] = jnp.zeros_like(dv)

    def block(index, _):
        row0 = pl.multiple_of(index * TILE, TILE)
        q_rows = pl.ds(row0, TILE)
        position = row0 + lax.broadcasted_iota(jnp.int32, (1, TILE), 1)
        begin = jnp.zeros((1, TILE), jnp.int32)
        first = jnp.int32(0)
        end = jnp.int32(0)
        for doc in range(NDOC):
            end = end + lengths[0, doc]
            begin = jnp.where(position >= end, end, begin)
            first = jnp.where(row0 >= end, end, first)
        tiles = index - lax.div(first, TILE) + 1

        def body(count):
            tile0 = index + 1 - count
            key0 = pl.multiple_of(tile0 * TILE, TILE)
            k_rows = pl.ds(key0, count * TILE)
            key_index = lax.broadcasted_iota(jnp.int32, (count * TILE, TILE), 0)
            in_document = key_index >= begin - key0
            causal = lax.broadcasted_iota(jnp.int32, (TILE, TILE), 0) <= (
                lax.broadcasted_iota(jnp.int32, (TILE, TILE), 1)
            )
            held = []
            for head in range(heads):
                scores = dot(tiles_of(tile0, count, 2, head), q_t[span[head], q_rows])
                prob_grad = dot(tiles_of(tile0, count, 1, head), g_t[span[head], q_rows])
                scores = jnp.where(in_document, scores, NEG_FILL)
                last = jnp.where(causal, scores[(count - 1) * TILE :], NEG_FILL)
                if count > 1:
                    scores = jnp.concatenate([scores[: (count - 1) * TILE], last], axis=0)
                else:
                    scores = last
                maximum = jnp.max(scores, axis=0, keepdims=True)
                powers = jnp.exp2((scores - maximum) * (SCALING * LOG2_E))
                inverse = 1.0 / jnp.sum(powers, axis=0, keepdims=True)
                held.append((prob_grad, powers.astype(jnp.bfloat16), inverse))
            for head in range(heads):
                prob_grad, rounded, inverse = held[head]
                powers = rounded.astype(jnp.float32)
                result = (dot(v_t[span[head], k_rows], rounded) * inverse).astype(jnp.bfloat16)
                row_dot = jnp.sum(powers * prob_grad, axis=0, keepdims=True) * inverse
                g_wide = g_t[span[head], q_rows].astype(jnp.float32)
                score_grad = rounded * (prob_grad - row_dot).astype(jnp.bfloat16)
                query_grad = dot(k_t[span[head], k_rows], score_grad) * (inverse * SCALING)
                dq_t[span[head], q_rows] = query_grad.astype(jnp.bfloat16)
                out[q_rows, span[head]] = result.T
                g_scaled = (g_wide * inverse).astype(jnp.bfloat16).T
                dv[head, k_rows, :] += dot(rounded, g_scaled)

        for count in range(1, min(MAX_TILES, blocks) + 1):
            pl.when(tiles == count)(functools.partial(body, count))
        return 0

    lax.fori_loop(0, blocks, block, 0)
    for head in range(heads):
        dv_t[span[head], :] = dv[head].astype(jnp.bfloat16).T

    for part, grads in enumerate((dq_t, dv_t)):
        returned[part * RANK : (part + 1) * RANK, :] = (
            ADAPTER_SCALE * dot(ups[part * RANK : (part + 1) * RANK, :], grads[...])
        ).astype(jnp.bfloat16)
    for piece in range(low.shape[1] // LOW_ROWS):
        low[:, piece * LOW_ROWS : (piece + 1) * LOW_ROWS, :] = packed[
            :, TILE:, piece * 2 * RANK : (piece + 1) * 2 * RANK
        ]
    rows = backs[0].shape[2]
    for step in range(len(backs)):
        target = lax.rem(chip + step, len(backs))
        for holder in range(2):
            begin = pl.multiple_of((target * 2 + holder) * rows, rows)
            backs[step][holder] = returned[:, pl.ds(begin, rows)]
            outs[step][holder] = out[pl.ds(begin, rows), :]


def attention(lengths, chip, packed, ups):
    seq_size = packed.shape[0]
    rows = packed.shape[1] - LOW_ROWS
    length = seq_size * rows
    width = packed.shape[2] // 4
    heads = width // HEAD_SIZE
    chips = seq_size // 2
    wide_t = pltpu.VMEM((width, length), jnp.bfloat16)
    back = jax.ShapeDtypeStruct((2, 2 * RANK, rows), jnp.bfloat16)
    grad_t = jax.ShapeDtypeStruct((width, length), jnp.bfloat16)
    return pl.pallas_call(
        attention_kernel,
        in_specs=[SMEM] * 2 + [VMEM] * 2,
        out_specs=[VMEM] * (3 + 2 * chips),
        scratch_shapes=[
            wide_t,
            wide_t,
            wide_t,
            wide_t,
            pltpu.VMEM((heads, length, HEAD_SIZE), jnp.float32),
            pltpu.VMEM((2 * RANK, length), jnp.bfloat16),
            pltpu.VMEM((length, width), jnp.bfloat16),
        ],
        out_shape=[jax.ShapeDtypeStruct((2, rows, width), jnp.bfloat16)] * chips
        + [back] * chips
        + [grad_t, grad_t]
        + [jax.ShapeDtypeStruct((seq_size, rows // 2, 2 * RANK), jnp.bfloat16)],
        compiler_params=pltpu.CompilerParams(vmem_limit_bytes=32 << 20),
        cost_estimate=pl.CostEstimate(
            flops=8 << 30, bytes_accessed=16 << 20, transcendentals=4 << 20
        ),
        name="attention",
    )(lengths, chip, packed, ups)


def up_kernel(core, low, low_other, dq_t, dv_t, up, lows):
    lows[core[0]] = low[...]
    lows[1 - core[0]] = low_other[...]
    devices, half, _ = low.shape
    for part, grads in enumerate((dq_t, dv_t)):
        upper = lower = jnp.zeros((grads.shape[0], 2 * RANK), jnp.float32)
        for device in range(devices):
            begin = 2 * device * half
            upper += dot(grads[:, begin : begin + half], lows[part, device])
            lower += dot(grads[:, begin + half : begin + 2 * half], lows[part, device])
        share = ADAPTER_SCALE * (upper.T[:RANK] + lower.T[RANK:])
        up[part * RANK : (part + 1) * RANK, :] = share.astype(jnp.bfloat16)


def up_gradient(core, low, low_other, dq_t, dv_t):
    return pl.pallas_call(
        up_kernel,
        in_specs=[SMEM] + [VMEM] * 4,
        out_specs=VMEM,
        out_shape=jax.ShapeDtypeStruct((2 * RANK, dq_t.shape[0]), jnp.bfloat16),
        scratch_shapes=[pltpu.VMEM((2,) + low.shape, jnp.bfloat16)],
        compiler_params=pltpu.CompilerParams(vmem_limit_bytes=16 << 20),
        name="up_gradient",
    )(core, low, low_other, dq_t, dv_t)


def pick_kernel(core, part_0, part_1, part_2, part_3, out):
    core = core[0]
    for step, part in enumerate((part_0, part_1, part_2, part_3)):
        out[step] = part[1 - core]


def pick(core, parts):
    return pl.pallas_call(
        pick_kernel,
        in_specs=[SMEM] + [VMEM] * len(parts),
        out_specs=VMEM,
        out_shape=jax.ShapeDtypeStruct((len(parts),) + parts[0].shape[1:], parts[0].dtype),
        compiler_params=pltpu.CompilerParams(vmem_limit_bytes=SMALL_VMEM),
        name="pick",
    )(core, *parts)


def arrive_kernel(chip, core, part_0, part_1, part_2, part_3, other, out, done):
    chip, core = chip[0], core[0]
    parts = (part_0, part_1, part_2, part_3)
    width = part_0.shape[2]
    for step in range(len(parts)):
        origin = lax.rem(chip + len(parts) - step, len(parts))
        here = pl.multiple_of((origin * 2 + core) * width, width)
        there = pl.multiple_of((origin * 2 + 1 - core) * width, width)
        out[0, :, pl.ds(here, width)] = parts[step][core]
        out[0, :, pl.ds(there, width)] = other[step]
    done[...] = jnp.zeros_like(done)


def arrive(chip, core, parts, other):
    _, rows, width = parts[0].shape
    return pl.pallas_call(
        arrive_kernel,
        in_specs=[SMEM] * 2 + [VMEM] * (len(parts) + 1),
        out_specs=[VMEM] * 2,
        out_shape=[
            jax.ShapeDtypeStruct((1, rows, 2 * len(parts) * width), parts[0].dtype),
            DONE,
        ],
        compiler_params=pltpu.CompilerParams(vmem_limit_bytes=SMALL_VMEM),
        name="arrive",
    )(chip, core, *parts, other)


def backs_kernel(part_0, part_1, part_2, part_3, *refs):
    out = refs[len(refs) // 2]
    total = part_0[...].astype(jnp.float32)
    for part in (part_1, part_2, part_3):
        total += part[...].astype(jnp.float32)
    out[...] = total.astype(out.dtype)


def sum_backs(parts, held):
    count = len(parts)
    return pl.pallas_call(
        backs_kernel,
        in_specs=[VMEM] * (count + len(held)),
        out_specs=[VMEM] * (1 + len(held)),
        out_shape=[
            jax.ShapeDtypeStruct(part.shape, part.dtype) for part in [parts[0]] + list(held)
        ],
        input_output_aliases={count + index: 1 + index for index in range(len(held))},
        compiler_params=pltpu.CompilerParams(vmem_limit_bytes=SMALL_VMEM),
        name="sum_backs",
    )(*parts, *held)


def halves_kernel(chip, core, hidden, other, wq_up, wv_up, out, ups):
    rows, half = other.shape
    out[:rows] = hidden[:, pl.ds(pl.multiple_of(core[0] * half, half), half)]
    out[rows:] = other[...]
    width = ups.shape[1]
    columns = pl.ds(pl.multiple_of((chip[0] * 2 + core[0]) * width, width), width)
    ups[:RANK] = wq_up[:, columns]
    ups[RANK:] = wv_up[:, columns]


def halves(chip, core, hidden, other, wq_up, wv_up, width):
    rows, half = other.shape
    return pl.pallas_call(
        halves_kernel,
        in_specs=[SMEM] * 2 + [VMEM] * 4,
        out_specs=[VMEM] * 2,
        out_shape=[
            jax.ShapeDtypeStruct((2 * rows, half), hidden.dtype),
            jax.ShapeDtypeStruct((2 * RANK, width), wq_up.dtype),
        ],
        compiler_params=pltpu.CompilerParams(vmem_limit_bytes=SMALL_VMEM),
        name="halves",
    )(chip, core, hidden, other, wq_up, wv_up)


def down_kernel(core, *refs):
    *parts, hidden, up, out, back = refs
    rows = parts[0].shape[2]

    @pl.when(pl.program_id(0) == 0)
    def _():
        total = parts[0][...].astype(jnp.float32)
        for part in parts[1:]:
            total += part[...].astype(jnp.float32)
        back[...] = total.astype(jnp.bfloat16)

    grad = dot(back[core[0]], hidden[:rows]) + dot(back[1 - core[0]], hidden[rows:])
    grad = grad.astype(out.dtype)
    for row in range(out.shape[0]):
        across = slice(row * SHARE_ROWS, (row + 1) * SHARE_ROWS)
        out[row, 0, :, :DOWN_COLS] = grad[across, :]
        out[row, 0, :, DOWN_COLS:] = up[across, :]


def down_gradient(core, parts, hidden, up):
    rows, half = hidden.shape
    steps = half // DOWN_COLS
    across = 2 * RANK // SHARE_ROWS
    shape = parts[0].shape
    return pl.pallas_call(
        down_kernel,
        grid_spec=pltpu.PrefetchScalarGridSpec(
            num_scalar_prefetch=1,
            grid=(steps,),
            in_specs=[pl.BlockSpec(shape, lambda i, core: (0, 0, 0))] * len(parts)
            + [
                pl.BlockSpec((rows, DOWN_COLS), lambda i, core: (0, i)),
                pl.BlockSpec((2 * RANK, UP_COLS), lambda i, core: (0, i)),
            ],
            out_specs=pl.BlockSpec(
                (across, 1, SHARE_ROWS, DOWN_COLS + UP_COLS), lambda i, core: (0, i, 0, 0)
            ),
            scratch_shapes=[pltpu.VMEM(shape, jnp.bfloat16)],
        ),
        out_shape=jax.ShapeDtypeStruct(
            (across, steps, SHARE_ROWS, DOWN_COLS + UP_COLS), jnp.bfloat16
        ),
        compiler_params=pltpu.CompilerParams(vmem_limit_bytes=24 << 20),
        name="down_gradient",
    )(core, *parts, hidden, up)


def share_kernel(parts, *refs):
    out = refs[-1]
    total = parts[0].astype(jnp.float32)
    for part in range(1, parts.shape[0]):
        total += parts[part].astype(jnp.float32)
    out[...] = total.astype(out.dtype)


def sum_share(parts, after):
    return pl.pallas_call(
        share_kernel,
        in_specs=[VMEM] + [VMEM] * len(after),
        out_specs=VMEM,
        out_shape=jax.ShapeDtypeStruct(parts.shape[1:], parts.dtype),
        compiler_params=pltpu.CompilerParams(vmem_limit_bytes=SMALL_VMEM),
        name="sum_share",
    )(parts, *after)


def chips_kernel(chip, *refs):
    *parts, out = refs
    chip = chip[0]
    total = parts[0][:, :DOWN_COLS].astype(jnp.float32)
    for part in parts[1:]:
        total += part[:, :DOWN_COLS].astype(jnp.float32)
    total = total.astype(out.dtype)
    for device in range(out.shape[0]):
        out[device, :, :DOWN_COLS] = total
    for step, part in enumerate(parts):
        origin = lax.rem(chip + len(parts) - step, len(parts))
        begin = pl.multiple_of(DOWN_COLS + origin * UP_COLS, UP_COLS)
        for device in range(out.shape[0]):
            out[device, :, pl.ds(begin, UP_COLS)] = part[:, DOWN_COLS:]


def sum_chips(chip, parts, devices):
    shape = (devices, SHARE_ROWS, DOWN_COLS + len(parts) * UP_COLS)
    return pl.pallas_call(
        chips_kernel,
        in_specs=[SMEM] + [VMEM] * len(parts),
        out_specs=VMEM,
        out_shape=jax.ShapeDtypeStruct(shape, parts[0].dtype),
        compiler_params=pltpu.CompilerParams(vmem_limit_bytes=SMALL_VMEM),
        name="sum_chips",
    )(chip, *parts)


def place_kernel(which, shares, *refs):
    *outs, downs, ups, sems = refs[-7:]
    which = which[0]
    half = shares.shape[0] // 2
    columns = shares.shape[1]
    copies = []

    def send(source, target, begin, size):
        begin = pl.multiple_of(begin, size)
        copies.append(
            pltpu.make_async_copy(source, target.at[:, pl.ds(begin, size)], sems.at[len(copies)])
        )
        copies[-1].start()

    chips, _, width = ups.shape
    for row in range(2 * half):
        part, across = row // half, slice(row % half * SHARE_ROWS, (row % half + 1) * SHARE_ROWS)
        for column in range(columns):
            share = shares[row, column]
            downs[part, across, column * DOWN_COLS : (column + 1) * DOWN_COLS] = share[
                :, :DOWN_COLS
            ].astype(jnp.float32)
            for chip in range(chips):
                begin = DOWN_COLS + chip * UP_COLS
                ups[
                    chip,
                    row * SHARE_ROWS : (row + 1) * SHARE_ROWS,
                    column * UP_COLS : (column + 1) * UP_COLS,
                ] = share[:, begin : begin + UP_COLS].astype(jnp.float32)
        if row % half == half - 1:
            send(downs.at[part], outs[2 * part], which * downs.shape[2], downs.shape[2])
            for chip in range(chips):
                send(
                    ups.at[chip, part * RANK : (part + 1) * RANK, :],
                    outs[2 * part + 1],
                    (2 * chip + which) * width,
                    width,
                )
    for copy in copies:
        copy.wait()


def place(which, shares, model, width, earlier=()):
    shapes = [(RANK, model), (RANK, width), (RANK, model), (RANK, width)]
    columns = shares.shape[1]
    chips = (shares.shape[3] - DOWN_COLS) // UP_COLS
    return pl.pallas_call(
        place_kernel,
        in_specs=[SMEM, VMEM] + [ANY] * len(earlier),
        out_specs=[ANY] * 4,
        out_shape=[jax.ShapeDtypeStruct(shape, jnp.float32) for shape in shapes],
        scratch_shapes=[
            pltpu.VMEM((2, RANK, columns * DOWN_COLS), jnp.float32),
            pltpu.VMEM((chips, 2 * RANK, columns * UP_COLS), jnp.float32),
            pltpu.SemaphoreType.DMA((2 + 2 * chips,)),
        ],
        input_output_aliases={2 + index: index for index in range(len(earlier))},
        compiler_params=pltpu.CompilerParams(vmem_limit_bytes=16 << 20),
        name="place",
    )(which, shares, *earlier)


def swap(x, axes):
    return lax.all_to_all(x, axes, 0, 0, tiled=True)


def to_other_core(x):
    return lax.ppermute(x, "core", [(0, 1), (1, 0)])


def per_device(
    sizes,
    hidden,
    frozen_queries,
    frozen_keys,
    frozen_values,
    document_length_list,
    query_down_weight,
    query_up_weight,
    value_down_weight,
    value_up_weight,
    output_gradient,
):
    dp_size, seq_size = sizes
    chips = seq_size // 2
    rows, model = hidden.shape[1:]
    half = model // 2
    chip = lax.axis_index("y").astype(jnp.int32)[None]
    core = lax.axis_index("core").astype(jnp.int32)[None]
    width = frozen_queries.shape[2] // seq_size

    def to_chip(x, step):
        return lax.ppermute(x, "y", [(c, (c + step) % chips) for c in range(chips)])

    packed, hidden_leaving = pack(
        core,
        hidden[0],
        query_down_weight.T,
        value_down_weight.T,
        frozen_queries[0],
        frozen_keys[0],
        frozen_values[0],
        output_gradient[0],
        query_up_weight,
        value_up_weight,
        seq_size,
    )
    received = swap(packed, SEQ)
    hidden_other = to_other_core(hidden_leaving)
    hidden_half, ups = halves(
        chip, core, hidden[0], hidden_other, query_up_weight, value_up_weight, width
    )
    *outs, dq_t, dv_t, low = attention(
        document_length_list,
        chip,
        received,
        ups,
    )
    parts, backs = outs[:chips], outs[chips:]

    backs = [backs[0]] + [to_chip(backs[step], step) for step in range(1, chips)]
    back, *held = sum_backs(backs, parts[-2:])
    parts = parts[:-2] + held
    back_other = to_other_core(back)
    parts = [parts[0]] + [to_chip(parts[step], step) for step in range(1, chips)]
    up = up_gradient(core, low, to_other_core(low), dq_t, dv_t)
    down = down_gradient(core, [back, back_other], hidden_half, up)

    other = to_other_core(pick(core, parts))
    attended, attended_done = arrive(chip, core, parts, other)

    shares = swap(down.reshape((-1,) + down.shape[2:]), DP)
    share = sum_share(shares, after=[attended_done])
    share = [share] + [to_chip(share, step) for step in range(1, chips)]
    shares = swap(sum_chips(chip, share, shares.shape[0]), DP)
    shares = shares.reshape(down.shape[:2] + shares.shape[1:])
    shares_other = to_other_core(shares)
    grads = place(core, shares, model, seq_size * width)
    grad_a_q, up_q, grad_a_v, up_v = place(
        1 - core, shares_other, model, seq_size * width, earlier=grads
    )
    return attended, grad_a_q.T, up_q, grad_a_v.T, up_v


def solution(mesh):
    dp_size, seq_size = mesh.shape["dp"], mesh.shape["seq"]
    fine = Mesh(mesh.devices.reshape(4, 4, 4, 2), ALL)
    rows = P(DP, SEQ, None)
    in_specs = (rows, rows, rows, rows, P(DP, None), P(), P(), P(), P(), rows)
    out_specs = (rows, P(), P(), P(), P())
    return jax.shard_map(
        functools.partial(per_device, (dp_size, seq_size)),
        mesh=fine,
        in_specs=in_specs,
        out_specs=out_specs,
        check_vma=False,
    )
```

```python
import functools

import jax
import jax.numpy as jnp
from jax import lax
from jax.experimental import pallas as pl
from jax.experimental.pallas import tpu as pltpu
from jax.sharding import Mesh
from jax.sharding import PartitionSpec as P

HEAD_COUNT = 16
HEAD_SIZE = 128
RANK = 64
NDOC = 8
TILE = 256
MAX_TILES = 5
ADAPTER_SCALE = 2.0
NEG_FILL = -1e30
SCALING = HEAD_SIZE ** (-0.5)
LOG2_E = 1.4426950408889634

SHARE_ROWS = 16
DOWN_COLS = 1024
UP_COLS = 128

DP = ("x", "z")
SEQ = ("y", "core")
ALL = ("x", "z", "y", "core")
NT = (((1,), (1,)), ((), ()))


def dot(a, b):
    return jnp.dot(a, b, preferred_element_type=jnp.float32)


def dot_nt(a, b):
    return lax.dot_general(a, b, NT, preferred_element_type=jnp.float32)


LOW_ROWS = 16

HIDDEN_PARTS = 4
PACK_VMEM = 56 << 20
SMALL_VMEM = 8 << 20
VMEM = pl.BlockSpec(memory_space=pltpu.VMEM)
SMEM = pl.BlockSpec(memory_space=pltpu.SMEM)
ANY = pl.BlockSpec(memory_space=pl.ANY)
DONE = jax.ShapeDtypeStruct((8, 128), jnp.float32)


def pack_kernel(
    core, hidden, wq_down, wv_down, fq, fk, fv, grad, wq_up, wv_up, out, other,
    hidden_v, down_v, fq_v, fv_v, wq_up_v, wv_up_v, out_v, low,
    down_sems, hidden_sems, row_sems, through_sems, out_sems, other_sem,
):
    devices, _, packed = out.shape
    width = packed // 4
    rows, model = hidden.shape
    step = model // HIDDEN_PARTS

    def part(index):
        return pl.ds(index * step, step)

    def columns(index):
        return pl.ds(index * width, width)

    downs = [
        pltpu.make_async_copy(wq_down, down_v.at[pl.ds(0, RANK)], down_sems.at[0]),
        pltpu.make_async_copy(wv_down, down_v.at[pl.ds(RANK, RANK)], down_sems.at[1]),
    ]
    hiddens = [
        pltpu.make_async_copy(
            hidden.at[:, part(index)], hidden_v.at[:, part(index)], hidden_sems.at[index]
        )
        for index in range(HIDDEN_PARTS)
    ]
    through = [
        pltpu.make_async_copy(
            source.at[:, columns(device)],
            out_v.at[device, pl.ds(0, rows), columns(which)],
            through_sems.at[which - 2, device],
        )
        for device in range(devices)
        for which, source in ((2, fk), (3, grad))
    ]
    whole = [
        pltpu.make_async_copy(wq_up, wq_up_v, row_sems.at[0]),
        pltpu.make_async_copy(fq, fq_v, row_sems.at[1]),
        pltpu.make_async_copy(wv_up, wv_up_v, row_sems.at[2]),
        pltpu.make_async_copy(fv, fv_v, row_sems.at[3]),
    ]
    for copy in downs + hiddens + whole:
        copy.start()

    def leave(device, begin, size, number):
        at = (device, slice(None), pl.ds(begin, size))
        copy = pltpu.make_async_copy(out_v.at[at], out.at[at], out_sems.at[number, device])
        copy.start()
        return copy

    for copy in downs:
        copy.wait()
    total = jnp.zeros((rows, 2 * RANK), jnp.float32)
    for index in range(HIDDEN_PARTS):
        hiddens[index].wait()
        if index == 0:
            for copy in through:
                copy.start()
        total += dot_nt(hidden_v[:, part(index)], down_v[:, part(index)])
    low[...] = total.astype(jnp.bfloat16)
    half = other.shape[1]
    begin = pl.multiple_of((1 - core[0]) * half, half)
    other_copy = pltpu.make_async_copy(hidden_v.at[:, pl.ds(begin, half)], other, other_sem)
    other_copy.start()
    upper, lower = total[: rows // 2], total[rows // 2 :]
    left = lax.broadcasted_iota(jnp.int32, upper.shape, 1) < RANK
    sides = (
        jnp.where(left, upper, pltpu.roll(lower, RANK, 1)).astype(jnp.bfloat16),
        jnp.where(left, pltpu.roll(upper, RANK, 1), lower).astype(jnp.bfloat16),
    )
    outs = []
    for device in range(devices):
        for piece in range(rows // 2 // LOW_ROWS):
            out_v[device, rows:, piece * 2 * RANK : (piece + 1) * 2 * RANK] = sides[device % 2][
                piece * LOW_ROWS : (piece + 1) * LOW_ROWS
            ]
        through[2 * device].wait()
        through[2 * device + 1].wait()
        outs.append(leave(device, 2 * width, 2 * width, 0))
    for copy in whole:
        copy.wait()
    for device in range(devices):
        at = slice(device * width, (device + 1) * width)
        for which, (frozen, weight) in enumerate(((fq_v, wq_up_v), (fv_v, wv_up_v))):
            added = ADAPTER_SCALE * dot(low[:, which * RANK : (which + 1) * RANK], weight[:, at])
            out_v[device, :rows, which * width : (which + 1) * width] = (
                frozen[:, at].astype(jnp.float32) + added
            ).astype(jnp.bfloat16)
        outs.append(leave(device, 0, 2 * width, 1))
    for copy in outs:
        copy.wait()
    other_copy.wait()


def pack(core, hidden, wq_down_t, wv_down_t, fq, fk, fv, grad, wq_up, wv_up, seq_size):
    rows, model = hidden.shape
    columns = fq.shape[1]
    width = columns // seq_size
    bf16 = jnp.bfloat16
    return pl.pallas_call(
        pack_kernel,
        in_specs=[SMEM] + [ANY] * 9,
        out_specs=[ANY] * 2,
        out_shape=[
            jax.ShapeDtypeStruct((seq_size, rows + LOW_ROWS, 4 * width), bf16),
            jax.ShapeDtypeStruct((rows, model // 2), bf16),
        ],
        scratch_shapes=[
            pltpu.VMEM((rows, model), bf16),
            pltpu.VMEM((2 * RANK, model), bf16),
            pltpu.VMEM((rows, columns), bf16),
            pltpu.VMEM((rows, columns), bf16),
            pltpu.VMEM((RANK, columns), bf16),
            pltpu.VMEM((RANK, columns), bf16),
            pltpu.VMEM((seq_size, rows + LOW_ROWS, 4 * width), bf16),
            pltpu.VMEM((rows, 2 * RANK), bf16),
            pltpu.SemaphoreType.DMA((2,)),
            pltpu.SemaphoreType.DMA((HIDDEN_PARTS,)),
            pltpu.SemaphoreType.DMA((4,)),
            pltpu.SemaphoreType.DMA((2, seq_size)),
            pltpu.SemaphoreType.DMA((2, seq_size)),
            pltpu.SemaphoreType.DMA,
        ],
        compiler_params=pltpu.CompilerParams(vmem_limit_bytes=PACK_VMEM),
        name="pack",
    )(core, hidden, wq_down_t, wv_down_t, fq, fk, fv, grad, wq_up, wv_up)


def attention_kernel(
    lengths, chip, packed, ups, *refs
):
    *outs, dq_t, dv_t, low, q_t, k_t, v_t, g_t, dv, returned, out = refs
    outs, backs = outs[: len(outs) // 2], outs[len(outs) // 2 :]
    length = out.shape[0]
    heads = out.shape[1] // HEAD_SIZE
    width = heads * HEAD_SIZE
    blocks = length // TILE
    chip = chip[0]
    span = [slice(head * HEAD_SIZE, (head + 1) * HEAD_SIZE) for head in range(heads)]

    def columns(which, head):
        begin = which * width + head * HEAD_SIZE
        return slice(begin, begin + HEAD_SIZE)

    def tiles_of(first, count, which, head):
        rows = packed[pl.ds(first, count), :TILE, columns(which, head)]
        return rows.reshape(count * TILE, HEAD_SIZE)

    for head in range(heads):
        q_t[span[head], :] = tiles_of(0, blocks, 0, head).T
        v_t[span[head], :] = tiles_of(0, blocks, 1, head).T
        k_t[span[head], :] = tiles_of(0, blocks, 2, head).T
        g_t[span[head], :] = tiles_of(0, blocks, 3, head).T
    dv[...] = jnp.zeros_like(dv)

    def block(index, _):
        row0 = pl.multiple_of(index * TILE, TILE)
        q_rows = pl.ds(row0, TILE)
        position = row0 + lax.broadcasted_iota(jnp.int32, (1, TILE), 1)
        begin = jnp.zeros((1, TILE), jnp.int32)
        first = jnp.int32(0)
        end = jnp.int32(0)
        for doc in range(NDOC):
            end = end + lengths[0, doc]
            begin = jnp.where(position >= end, end, begin)
            first = jnp.where(row0 >= end, end, first)
        tiles = index - lax.div(first, TILE) + 1

        def body(count):
            tile0 = index + 1 - count
            key0 = pl.multiple_of(tile0 * TILE, TILE)
            k_rows = pl.ds(key0, count * TILE)
            key_index = lax.broadcasted_iota(jnp.int32, (count * TILE, TILE), 0)
            in_document = key_index >= begin - key0
            causal = lax.broadcasted_iota(jnp.int32, (TILE, TILE), 0) <= (
                lax.broadcasted_iota(jnp.int32, (TILE, TILE), 1)
            )
            held = []
            for head in range(heads):
                scores = dot(tiles_of(tile0, count, 2, head), q_t[span[head], q_rows])
                prob_grad = dot(tiles_of(tile0, count, 1, head), g_t[span[head], q_rows])
                scores = jnp.where(in_document, scores, NEG_FILL)
                last = jnp.where(causal, scores[(count - 1) * TILE :], NEG_FILL)
                if count > 1:
                    scores = jnp.concatenate([scores[: (count - 1) * TILE], last], axis=0)
                else:
                    scores = last
                maximum = jnp.max(scores, axis=0, keepdims=True)
                powers = jnp.exp2((scores - maximum) * (SCALING * LOG2_E))
                inverse = 1.0 / jnp.sum(powers, axis=0, keepdims=True)
                held.append((prob_grad, powers.astype(jnp.bfloat16), inverse))
            for head in range(heads):
                prob_grad, rounded, inverse = held[head]
                powers = rounded.astype(jnp.float32)
                result = (dot(v_t[span[head], k_rows], rounded) * inverse).astype(jnp.bfloat16)
                row_dot = jnp.sum(powers * prob_grad, axis=0, keepdims=True) * inverse
                g_wide = g_t[span[head], q_rows].astype(jnp.float32)
                score_grad = rounded * (prob_grad - row_dot).astype(jnp.bfloat16)
                query_grad = dot(k_t[span[head], k_rows], score_grad) * (inverse * SCALING)
                dq_t[span[head], q_rows] = query_grad.astype(jnp.bfloat16)
                out[q_rows, span[head]] = result.T
                g_scaled = (g_wide * inverse).astype(jnp.bfloat16).T
                dv[head, k_rows, :] += dot(rounded, g_scaled)

        for count in range(1, min(MAX_TILES, blocks) + 1):
            pl.when(tiles == count)(functools.partial(body, count))
        return 0

    lax.fori_loop(0, blocks, block, 0)
    for head in range(heads):
        dv_t[span[head], :] = dv[head].astype(jnp.bfloat16).T

    for part, grads in enumerate((dq_t, dv_t)):
        returned[part * RANK : (part + 1) * RANK, :] = (
            ADAPTER_SCALE * dot(ups[part * RANK : (part + 1) * RANK, :], grads[...])
        ).astype(jnp.bfloat16)
    for piece in range(low.shape[1] // LOW_ROWS):
        low[:, piece * LOW_ROWS : (piece + 1) * LOW_ROWS, :] = packed[
            :, TILE:, piece * 2 * RANK : (piece + 1) * 2 * RANK
        ]
    rows = backs[0].shape[2]
    for step in range(len(backs)):
        target = lax.rem(chip + step, len(backs))
        for holder in range(2):
            begin = pl.multiple_of((target * 2 + holder) * rows, rows)
            backs[step][holder] = returned[:, pl.ds(begin, rows)]
            outs[step][holder] = out[pl.ds(begin, rows), :]


def attention(lengths, chip, packed, ups):
    seq_size = packed.shape[0]
    rows = packed.shape[1] - LOW_ROWS
    length = seq_size * rows
    width = packed.shape[2] // 4
    heads = width // HEAD_SIZE
    chips = seq_size // 2
    wide_t = pltpu.VMEM((width, length), jnp.bfloat16)
    back = jax.ShapeDtypeStruct((2, 2 * RANK, rows), jnp.bfloat16)
    grad_t = jax.ShapeDtypeStruct((width, length), jnp.bfloat16)
    return pl.pallas_call(
        attention_kernel,
        in_specs=[SMEM] * 2 + [VMEM] * 2,
        out_specs=[VMEM] * (3 + 2 * chips),
        scratch_shapes=[
            wide_t,
            wide_t,
            wide_t,
            wide_t,
            pltpu.VMEM((heads, length, HEAD_SIZE), jnp.float32),
            pltpu.VMEM((2 * RANK, length), jnp.bfloat16),
            pltpu.VMEM((length, width), jnp.bfloat16),
        ],
        out_shape=[jax.ShapeDtypeStruct((2, rows, width), jnp.bfloat16)] * chips
        + [back] * chips
        + [grad_t, grad_t]
        + [jax.ShapeDtypeStruct((seq_size, rows // 2, 2 * RANK), jnp.bfloat16)],
        compiler_params=pltpu.CompilerParams(vmem_limit_bytes=32 << 20),
        cost_estimate=pl.CostEstimate(
            flops=8 << 30, bytes_accessed=16 << 20, transcendentals=4 << 20
        ),
        name="attention",
    )(lengths, chip, packed, ups)


def up_kernel(core, low, low_other, dq_t, dv_t, up, lows):
    lows[core[0]] = low[...]
    lows[1 - core[0]] = low_other[...]
    devices, half, _ = low.shape
    for part, grads in enumerate((dq_t, dv_t)):
        upper = lower = jnp.zeros((grads.shape[0], 2 * RANK), jnp.float32)
        for device in range(devices):
            begin = 2 * device * half
            upper += dot(grads[:, begin : begin + half], lows[part, device])
            lower += dot(grads[:, begin + half : begin + 2 * half], lows[part, device])
        share = ADAPTER_SCALE * (upper.T[:RANK] + lower.T[RANK:])
        up[part * RANK : (part + 1) * RANK, :] = share.astype(jnp.bfloat16)


def up_gradient(core, low, low_other, dq_t, dv_t):
    return pl.pallas_call(
        up_kernel,
        in_specs=[SMEM] + [VMEM] * 4,
        out_specs=VMEM,
        out_shape=jax.ShapeDtypeStruct((2 * RANK, dq_t.shape[0]), jnp.bfloat16),
        scratch_shapes=[pltpu.VMEM((2,) + low.shape, jnp.bfloat16)],
        compiler_params=pltpu.CompilerParams(vmem_limit_bytes=16 << 20),
        name="up_gradient",
    )(core, low, low_other, dq_t, dv_t)


def pick_kernel(core, part_0, part_1, part_2, part_3, out):
    core = core[0]
    for step, part in enumerate((part_0, part_1, part_2, part_3)):
        out[step] = part[1 - core]


def pick(core, parts):
    return pl.pallas_call(
        pick_kernel,
        in_specs=[SMEM] + [VMEM] * len(parts),
        out_specs=VMEM,
        out_shape=jax.ShapeDtypeStruct((len(parts),) + parts[0].shape[1:], parts[0].dtype),
        compiler_params=pltpu.CompilerParams(vmem_limit_bytes=SMALL_VMEM),
        name="pick",
    )(core, *parts)


def arrive_kernel(chip, core, part_0, part_1, part_2, part_3, other, out, done):
    chip, core = chip[0], core[0]
    parts = (part_0, part_1, part_2, part_3)
    width = part_0.shape[2]
    for step in range(len(parts)):
        origin = lax.rem(chip + len(parts) - step, len(parts))
        here = pl.multiple_of((origin * 2 + core) * width, width)
        there = pl.multiple_of((origin * 2 + 1 - core) * width, width)
        out[0, :, pl.ds(here, width)] = parts[step][core]
        out[0, :, pl.ds(there, width)] = other[step]
    done[...] = jnp.zeros_like(done)


def arrive(chip, core, parts, other):
    _, rows, width = parts[0].shape
    return pl.pallas_call(
        arrive_kernel,
        in_specs=[SMEM] * 2 + [VMEM] * (len(parts) + 1),
        out_specs=[VMEM] * 2,
        out_shape=[
            jax.ShapeDtypeStruct((1, rows, 2 * len(parts) * width), parts[0].dtype),
            DONE,
        ],
        compiler_params=pltpu.CompilerParams(vmem_limit_bytes=SMALL_VMEM),
        name="arrive",
    )(chip, core, *parts, other)


def backs_kernel(part_0, part_1, part_2, part_3, *refs):
    out = refs[len(refs) // 2]
    total = part_0[...].astype(jnp.float32)
    for part in (part_1, part_2, part_3):
        total += part[...].astype(jnp.float32)
    out[...] = total.astype(out.dtype)


def sum_backs(parts, held):
    count = len(parts)
    return pl.pallas_call(
        backs_kernel,
        in_specs=[VMEM] * (count + len(held)),
        out_specs=[VMEM] * (1 + len(held)),
        out_shape=[
            jax.ShapeDtypeStruct(part.shape, part.dtype) for part in [parts[0]] + list(held)
        ],
        input_output_aliases={count + index: 1 + index for index in range(len(held))},
        compiler_params=pltpu.CompilerParams(vmem_limit_bytes=SMALL_VMEM),
        name="sum_backs",
    )(*parts, *held)


def halves_kernel(chip, core, hidden, other, wq_up, wv_up, out, ups):
    rows, half = other.shape
    out[:rows] = hidden[:, pl.ds(pl.multiple_of(core[0] * half, half), half)]
    out[rows:] = other[...]
    width = ups.shape[1]
    columns = pl.ds(pl.multiple_of((chip[0] * 2 + core[0]) * width, width), width)
    ups[:RANK] = wq_up[:, columns]
    ups[RANK:] = wv_up[:, columns]


def halves(chip, core, hidden, other, wq_up, wv_up, width):
    rows, half = other.shape
    return pl.pallas_call(
        halves_kernel,
        in_specs=[SMEM] * 2 + [VMEM] * 4,
        out_specs=[VMEM] * 2,
        out_shape=[
            jax.ShapeDtypeStruct((2 * rows, half), hidden.dtype),
            jax.ShapeDtypeStruct((2 * RANK, width), wq_up.dtype),
        ],
        compiler_params=pltpu.CompilerParams(vmem_limit_bytes=SMALL_VMEM),
        name="halves",
    )(chip, core, hidden, other, wq_up, wv_up)


def down_kernel(core, *refs):
    *parts, hidden, up, out, back = refs
    rows = parts[0].shape[2]

    @pl.when(pl.program_id(0) == 0)
    def _():
        total = parts[0][...].astype(jnp.float32)
        for part in parts[1:]:
            total += part[...].astype(jnp.float32)
        back[...] = total.astype(jnp.bfloat16)

    grad = dot(back[core[0]], hidden[:rows]) + dot(back[1 - core[0]], hidden[rows:])
    grad = grad.astype(out.dtype)
    for row in range(out.shape[0]):
        across = slice(row * SHARE_ROWS, (row + 1) * SHARE_ROWS)
        out[row, 0, :, :DOWN_COLS] = grad[across, :]
        out[row, 0, :, DOWN_COLS:] = up[across, :]


def down_gradient(core, parts, hidden, up):
    rows, half = hidden.shape
    steps = half // DOWN_COLS
    across = 2 * RANK // SHARE_ROWS
    shape = parts[0].shape
    return pl.pallas_call(
        down_kernel,
        grid_spec=pltpu.PrefetchScalarGridSpec(
            num_scalar_prefetch=1,
            grid=(steps,),
            in_specs=[pl.BlockSpec(shape, lambda i, core: (0, 0, 0))] * len(parts)
            + [
                pl.BlockSpec((rows, DOWN_COLS), lambda i, core: (0, i)),
                pl.BlockSpec((2 * RANK, UP_COLS), lambda i, core: (0, i)),
            ],
            out_specs=pl.BlockSpec(
                (across, 1, SHARE_ROWS, DOWN_COLS + UP_COLS), lambda i, core: (0, i, 0, 0)
            ),
            scratch_shapes=[pltpu.VMEM(shape, jnp.bfloat16)],
        ),
        out_shape=jax.ShapeDtypeStruct(
            (across, steps, SHARE_ROWS, DOWN_COLS + UP_COLS), jnp.bfloat16
        ),
        compiler_params=pltpu.CompilerParams(vmem_limit_bytes=24 << 20),
        name="down_gradient",
    )(core, *parts, hidden, up)


def share_kernel(parts, *refs):
    out = refs[-1]
    total = parts[0].astype(jnp.float32)
    for part in range(1, parts.shape[0]):
        total += parts[part].astype(jnp.float32)
    out[...] = total.astype(out.dtype)


def sum_share(parts, after):
    return pl.pallas_call(
        share_kernel,
        in_specs=[VMEM] + [VMEM] * len(after),
        out_specs=VMEM,
        out_shape=jax.ShapeDtypeStruct(parts.shape[1:], parts.dtype),
        compiler_params=pltpu.CompilerParams(vmem_limit_bytes=SMALL_VMEM),
        name="sum_share",
    )(parts, *after)


def chips_kernel(chip, *refs):
    *parts, out = refs
    chip = chip[0]
    total = parts[0][:, :DOWN_COLS].astype(jnp.float32)
    for part in parts[1:]:
        total += part[:, :DOWN_COLS].astype(jnp.float32)
    total = total.astype(out.dtype)
    for device in range(out.shape[0]):
        out[device, :, :DOWN_COLS] = total
    for step, part in enumerate(parts):
        origin = lax.rem(chip + len(parts) - step, len(parts))
        begin = pl.multiple_of(DOWN_COLS + origin * UP_COLS, UP_COLS)
        for device in range(out.shape[0]):
            out[device, :, pl.ds(begin, UP_COLS)] = part[:, DOWN_COLS:]


def sum_chips(chip, parts, devices):
    shape = (devices, SHARE_ROWS, DOWN_COLS + len(parts) * UP_COLS)
    return pl.pallas_call(
        chips_kernel,
        in_specs=[SMEM] + [VMEM] * len(parts),
        out_specs=VMEM,
        out_shape=jax.ShapeDtypeStruct(shape, parts[0].dtype),
        compiler_params=pltpu.CompilerParams(vmem_limit_bytes=SMALL_VMEM),
        name="sum_chips",
    )(chip, *parts)


def place_kernel(which, shares, *refs):
    *outs, downs, ups, sems = refs[-7:]
    which = which[0]
    half = shares.shape[0] // 2
    columns = shares.shape[1]
    copies = []

    def send(source, target, begin, size):
        begin = pl.multiple_of(begin, size)
        copies.append(
            pltpu.make_async_copy(source, target.at[:, pl.ds(begin, size)], sems.at[len(copies)])
        )
        copies[-1].start()

    chips, _, width = ups.shape
    for row in range(2 * half):
        part, across = row // half, slice(row % half * SHARE_ROWS, (row % half + 1) * SHARE_ROWS)
        for column in range(columns):
            share = shares[row, column]
            downs[part, across, column * DOWN_COLS : (column + 1) * DOWN_COLS] = share[
                :, :DOWN_COLS
            ].astype(jnp.float32)
            for chip in range(chips):
                begin = DOWN_COLS + chip * UP_COLS
                ups[
                    chip,
                    row * SHARE_ROWS : (row + 1) * SHARE_ROWS,
                    column * UP_COLS : (column + 1) * UP_COLS,
                ] = share[:, begin : begin + UP_COLS].astype(jnp.float32)
        if row % half == half - 1:
            send(downs.at[part], outs[2 * part], which * downs.shape[2], downs.shape[2])
            for chip in range(chips):
                send(
                    ups.at[chip, part * RANK : (part + 1) * RANK, :],
                    outs[2 * part + 1],
                    (2 * chip + which) * width,
                    width,
                )
    for copy in copies:
        copy.wait()


def place(which, shares, model, width, earlier=()):
    shapes = [(RANK, model), (RANK, width), (RANK, model), (RANK, width)]
    columns = shares.shape[1]
    chips = (shares.shape[3] - DOWN_COLS) // UP_COLS
    return pl.pallas_call(
        place_kernel,
        in_specs=[SMEM, VMEM] + [ANY] * len(earlier),
        out_specs=[ANY] * 4,
        out_shape=[jax.ShapeDtypeStruct(shape, jnp.float32) for shape in shapes],
        scratch_shapes=[
            pltpu.VMEM((2, RANK, columns * DOWN_COLS), jnp.float32),
            pltpu.VMEM((chips, 2 * RANK, columns * UP_COLS), jnp.float32),
            pltpu.SemaphoreType.DMA((2 + 2 * chips,)),
        ],
        input_output_aliases={2 + index: index for index in range(len(earlier))},
        compiler_params=pltpu.CompilerParams(vmem_limit_bytes=16 << 20),
        name="place",
    )(which, shares, *earlier)


def swap(x, axes):
    return lax.all_to_all(x, axes, 0, 0, tiled=True)


def to_other_core(x):
    return lax.ppermute(x, "core", [(0, 1), (1, 0)])


def per_device(
    sizes,
    hidden,
    frozen_queries,
    frozen_keys,
    frozen_values,
    document_length_list,
    query_down_weight,
    query_up_weight,
    value_down_weight,
    value_up_weight,
    output_gradient,
):
    dp_size, seq_size = sizes
    chips = seq_size // 2
    rows, model = hidden.shape[1:]
    half = model // 2
    chip = lax.axis_index("y").astype(jnp.int32)[None]
    core = lax.axis_index("core").astype(jnp.int32)[None]
    width = frozen_queries.shape[2] // seq_size

    def to_chip(x, step):
        return lax.ppermute(x, "y", [(c, (c + step) % chips) for c in range(chips)])

    packed, hidden_leaving = pack(
        core,
        hidden[0],
        query_down_weight.T,
        value_down_weight.T,
        frozen_queries[0],
        frozen_keys[0],
        frozen_values[0],
        output_gradient[0],
        query_up_weight,
        value_up_weight,
        seq_size,
    )
    received = swap(packed, SEQ)
    hidden_other = to_other_core(hidden_leaving)
    hidden_half, ups = halves(
        chip, core, hidden[0], hidden_other, query_up_weight, value_up_weight, width
    )
    *outs, dq_t, dv_t, low = attention(
        document_length_list,
        chip,
        received,
        ups,
    )
    parts, backs = outs[:chips], outs[chips:]

    backs = [backs[0]] + [to_chip(backs[step], step) for step in range(1, chips)]
    back, *held = sum_backs(backs, parts[-2:])
    parts = parts[:-2] + held
    back_other = to_other_core(back)
    parts = [parts[0]] + [to_chip(parts[step], step) for step in range(1, chips)]
    up = up_gradient(core, low, to_other_core(low), dq_t, dv_t)
    down = down_gradient(core, [back, back_other], hidden_half, up)

    other = to_other_core(pick(core, parts))
    attended, attended_done = arrive(chip, core, parts, other)

    shares = swap(down.reshape((-1,) + down.shape[2:]), DP)
    share = sum_share(shares, after=[attended_done])
    share = [share] + [to_chip(share, step) for step in range(1, chips)]
    shares = swap(sum_chips(chip, share, shares.shape[0]), DP)
    shares = shares.reshape(down.shape[:2] + shares.shape[1:])
    shares_other = to_other_core(shares)
    grads = place(core, shares, model, seq_size * width)
    grad_a_q, up_q, grad_a_v, up_v = place(
        1 - core, shares_other, model, seq_size * width, earlier=grads
    )
    return attended, grad_a_q.T, up_q, grad_a_v.T, up_v


def solution(mesh):
    dp_size, seq_size = mesh.shape["dp"], mesh.shape["seq"]
    fine = Mesh(mesh.devices.reshape(4, 4, 4, 2), ALL)
    rows = P(DP, SEQ, None)
    in_specs = (rows, rows, rows, rows, P(DP, None), P(), P(), P(), P(), rows)
    out_specs = (rows, P(), P(), P(), P())
    return jax.shard_map(
        functools.partial(per_device, (dp_size, seq_size)),
        mesh=fine,
        in_specs=in_specs,
        out_specs=out_specs,
        check_vma=False,
    )
```

```python
import functools

import jax
import jax.numpy as jnp
from jax import lax
from jax.experimental import pallas as pl
from jax.experimental.pallas import tpu as pltpu
from jax.sharding import Mesh
from jax.sharding import PartitionSpec as P

HEAD_COUNT = 16
HEAD_SIZE = 128
RANK = 64
NDOC = 8
TILE = 256
MAX_TILES = 5
ADAPTER_SCALE = 2.0
NEG_FILL = -1e30
SCALING = HEAD_SIZE ** (-0.5)
LOG2_E = 1.4426950408889634

SHARE_ROWS = 16
DOWN_COLS = 1024
UP_COLS = 128

DP = ("x", "z")
SEQ = ("y", "core")
ALL = ("x", "z", "y", "core")
NT = (((1,), (1,)), ((), ()))


def dot(a, b):
    return jnp.dot(a, b, preferred_element_type=jnp.float32)


def dot_nt(a, b):
    return lax.dot_general(a, b, NT, preferred_element_type=jnp.float32)


LOW_ROWS = 16

HIDDEN_PARTS = 4
PACK_VMEM = 56 << 20
SMALL_VMEM = 8 << 20
VMEM = pl.BlockSpec(memory_space=pltpu.VMEM)
SMEM = pl.BlockSpec(memory_space=pltpu.SMEM)
ANY = pl.BlockSpec(memory_space=pl.ANY)
DONE = jax.ShapeDtypeStruct((8, 128), jnp.float32)


def pack_kernel(
    core, hidden, wq_down, wv_down, fq, fk, fv, grad, wq_up, wv_up, out, other,
    hidden_v, down_v, fq_v, fv_v, wq_up_v, wv_up_v, out_v, low,
    down_sems, hidden_sems, row_sems, through_sems, out_sems, other_sem,
):
    devices, _, packed = out.shape
    width = packed // 4
    rows, model = hidden.shape
    step = model // HIDDEN_PARTS

    def part(index):
        return pl.ds(index * step, step)

    def columns(index):
        return pl.ds(index * width, width)

    downs = [
        pltpu.make_async_copy(wq_down, down_v.at[pl.ds(0, RANK)], down_sems.at[0]),
        pltpu.make_async_copy(wv_down, down_v.at[pl.ds(RANK, RANK)], down_sems.at[1]),
    ]
    hiddens = [
        pltpu.make_async_copy(
            hidden.at[:, part(index)], hidden_v.at[:, part(index)], hidden_sems.at[index]
        )
        for index in range(HIDDEN_PARTS)
    ]
    through = [
        pltpu.make_async_copy(
            source.at[:, columns(device)],
            out_v.at[device, pl.ds(0, rows), columns(which)],
            through_sems.at[which - 2, device],
        )
        for device in range(devices)
        for which, source in ((2, fk), (3, grad))
    ]
    whole = [
        pltpu.make_async_copy(wq_up, wq_up_v, row_sems.at[0]),
        pltpu.make_async_copy(fq, fq_v, row_sems.at[1]),
        pltpu.make_async_copy(wv_up, wv_up_v, row_sems.at[2]),
        pltpu.make_async_copy(fv, fv_v, row_sems.at[3]),
    ]
    for copy in downs + hiddens + whole:
        copy.start()

    def leave(device, begin, size, number):
        at = (device, slice(None), pl.ds(begin, size))
        copy = pltpu.make_async_copy(out_v.at[at], out.at[at], out_sems.at[number, device])
        copy.start()
        return copy

    for copy in downs:
        copy.wait()
    total = jnp.zeros((rows, 2 * RANK), jnp.float32)
    for index in range(HIDDEN_PARTS):
        hiddens[index].wait()
        if index == 0:
            for copy in through:
                copy.start()
        total += dot_nt(hidden_v[:, part(index)], down_v[:, part(index)])
    low[...] = total.astype(jnp.bfloat16)
    half = other.shape[1]
    begin = pl.multiple_of((1 - core[0]) * half, half)
    other_copy = pltpu.make_async_copy(hidden_v.at[:, pl.ds(begin, half)], other, other_sem)
    other_copy.start()
    upper, lower = total[: rows // 2], total[rows // 2 :]
    left = lax.broadcasted_iota(jnp.int32, upper.shape, 1) < RANK
    sides = (
        jnp.where(left, upper, pltpu.roll(lower, RANK, 1)).astype(jnp.bfloat16),
        jnp.where(left, pltpu.roll(upper, RANK, 1), lower).astype(jnp.bfloat16),
    )
    outs = []
    for device in range(devices):
        for piece in range(rows // 2 // LOW_ROWS):
            out_v[device, rows:, piece * 2 * RANK : (piece + 1) * 2 * RANK] = sides[device % 2][
                piece * LOW_ROWS : (piece + 1) * LOW_ROWS
            ]
        through[2 * device].wait()
        through[2 * device + 1].wait()
        outs.append(leave(device, 2 * width, 2 * width, 0))
    for copy in whole:
        copy.wait()
    for device in range(devices):
        at = slice(device * width, (device + 1) * width)
        for which, (frozen, weight) in enumerate(((fq_v, wq_up_v), (fv_v, wv_up_v))):
            added = ADAPTER_SCALE * dot(low[:, which * RANK : (which + 1) * RANK], weight[:, at])
            out_v[device, :rows, which * width : (which + 1) * width] = (
                frozen[:, at].astype(jnp.float32) + added
            ).astype(jnp.bfloat16)
        outs.append(leave(device, 0, 2 * width, 1))
    for copy in outs:
        copy.wait()
    other_copy.wait()


def pack(core, hidden, wq_down_t, wv_down_t, fq, fk, fv, grad, wq_up, wv_up, seq_size):
    rows, model = hidden.shape
    columns = fq.shape[1]
    width = columns // seq_size
    bf16 = jnp.bfloat16
    return pl.pallas_call(
        pack_kernel,
        in_specs=[SMEM] + [ANY] * 9,
        out_specs=[ANY] * 2,
        out_shape=[
            jax.ShapeDtypeStruct((seq_size, rows + LOW_ROWS, 4 * width), bf16),
            jax.ShapeDtypeStruct((rows, model // 2), bf16),
        ],
        scratch_shapes=[
            pltpu.VMEM((rows, model), bf16),
            pltpu.VMEM((2 * RANK, model), bf16),
            pltpu.VMEM((rows, columns), bf16),
            pltpu.VMEM((rows, columns), bf16),
            pltpu.VMEM((RANK, columns), bf16),
            pltpu.VMEM((RANK, columns), bf16),
            pltpu.VMEM((seq_size, rows + LOW_ROWS, 4 * width), bf16),
            pltpu.VMEM((rows, 2 * RANK), bf16),
            pltpu.SemaphoreType.DMA((2,)),
            pltpu.SemaphoreType.DMA((HIDDEN_PARTS,)),
            pltpu.SemaphoreType.DMA((4,)),
            pltpu.SemaphoreType.DMA((2, seq_size)),
            pltpu.SemaphoreType.DMA((2, seq_size)),
            pltpu.SemaphoreType.DMA,
        ],
        compiler_params=pltpu.CompilerParams(vmem_limit_bytes=PACK_VMEM),
        name="pack",
    )(core, hidden, wq_down_t, wv_down_t, fq, fk, fv, grad, wq_up, wv_up)


def attention_kernel(
    lengths, chip, packed, ups, *refs
):
    *outs, dq_t, dv_t, low, q_t, k_t, v_t, g_t, dv, returned, out = refs
    outs, backs = outs[: len(outs) // 2], outs[len(outs) // 2 :]
    length = out.shape[0]
    heads = out.shape[1] // HEAD_SIZE
    width = heads * HEAD_SIZE
    blocks = length // TILE
    chip = chip[0]
    span = [slice(head * HEAD_SIZE, (head + 1) * HEAD_SIZE) for head in range(heads)]

    def columns(which, head):
        begin = which * width + head * HEAD_SIZE
        return slice(begin, begin + HEAD_SIZE)

    def tiles_of(first, count, which, head):
        rows = packed[pl.ds(first, count), :TILE, columns(which, head)]
        return rows.reshape(count * TILE, HEAD_SIZE)

    for head in range(heads):
        q_t[span[head], :] = tiles_of(0, blocks, 0, head).T
        v_t[span[head], :] = tiles_of(0, blocks, 1, head).T
        k_t[span[head], :] = tiles_of(0, blocks, 2, head).T
        g_t[span[head], :] = tiles_of(0, blocks, 3, head).T
    dv[...] = jnp.zeros_like(dv)

    def block(index, _):
        row0 = pl.multiple_of(index * TILE, TILE)
        q_rows = pl.ds(row0, TILE)
        position = row0 + lax.broadcasted_iota(jnp.int32, (1, TILE), 1)
        begin = jnp.zeros((1, TILE), jnp.int32)
        first = jnp.int32(0)
        end = jnp.int32(0)
        for doc in range(NDOC):
            end = end + lengths[0, doc]
            begin = jnp.where(position >= end, end, begin)
            first = jnp.where(row0 >= end, end, first)
        tiles = index - lax.div(first, TILE) + 1

        def body(count):
            tile0 = index + 1 - count
            key0 = pl.multiple_of(tile0 * TILE, TILE)
            k_rows = pl.ds(key0, count * TILE)
            key_index = lax.broadcasted_iota(jnp.int32, (count * TILE, TILE), 0)
            in_document = key_index >= begin - key0
            causal = lax.broadcasted_iota(jnp.int32, (TILE, TILE), 0) <= (
                lax.broadcasted_iota(jnp.int32, (TILE, TILE), 1)
            )
            held = []
            for head in range(heads):
                scores = dot(tiles_of(tile0, count, 2, head), q_t[span[head], q_rows])
                prob_grad = dot(tiles_of(tile0, count, 1, head), g_t[span[head], q_rows])
                scores = jnp.where(in_document, scores, NEG_FILL)
                last = jnp.where(causal, scores[(count - 1) * TILE :], NEG_FILL)
                if count > 1:
                    scores = jnp.concatenate([scores[: (count - 1) * TILE], last], axis=0)
                else:
                    scores = last
                maximum = jnp.max(scores, axis=0, keepdims=True)
                powers = jnp.exp2((scores - maximum) * (SCALING * LOG2_E))
                inverse = 1.0 / jnp.sum(powers, axis=0, keepdims=True)
                held.append((prob_grad, powers.astype(jnp.bfloat16), inverse))
            for head in range(heads):
                prob_grad, rounded, inverse = held[head]
                powers = rounded.astype(jnp.float32)
                result = (dot(v_t[span[head], k_rows], rounded) * inverse).astype(jnp.bfloat16)
                row_dot = jnp.sum(powers * prob_grad, axis=0, keepdims=True) * inverse
                g_wide = g_t[span[head], q_rows].astype(jnp.float32)
                score_grad = rounded * (prob_grad - row_dot).astype(jnp.bfloat16)
                query_grad = dot(k_t[span[head], k_rows], score_grad) * (inverse * SCALING)
                dq_t[span[head], q_rows] = query_grad.astype(jnp.bfloat16)
                out[q_rows, span[head]] = result.T
                g_scaled = (g_wide * inverse).astype(jnp.bfloat16).T
                dv[head, k_rows, :] += dot(rounded, g_scaled)

        for count in range(1, min(MAX_TILES, blocks) + 1):
            pl.when(tiles == count)(functools.partial(body, count))
        return 0

    lax.fori_loop(0, blocks, block, 0)
    for head in range(heads):
        dv_t[span[head], :] = dv[head].astype(jnp.bfloat16).T

    for part, grads in enumerate((dq_t, dv_t)):
        returned[part * RANK : (part + 1) * RANK, :] = (
            ADAPTER_SCALE * dot(ups[part * RANK : (part + 1) * RANK, :], grads[...])
        ).astype(jnp.bfloat16)
    for piece in range(low.shape[1] // LOW_ROWS):
        low[:, piece * LOW_ROWS : (piece + 1) * LOW_ROWS, :] = packed[
            :, TILE:, piece * 2 * RANK : (piece + 1) * 2 * RANK
        ]
    rows = backs[0].shape[2]
    for step in range(len(backs)):
        target = lax.rem(chip + step, len(backs))
        for holder in range(2):
            begin = pl.multiple_of((target * 2 + holder) * rows, rows)
            backs[step][holder] = returned[:, pl.ds(begin, rows)]
            outs[step][holder] = out[pl.ds(begin, rows), :]


def attention(lengths, chip, packed, ups):
    seq_size = packed.shape[0]
    rows = packed.shape[1] - LOW_ROWS
    length = seq_size * rows
    width = packed.shape[2] // 4
    heads = width // HEAD_SIZE
    chips = seq_size // 2
    wide_t = pltpu.VMEM((width, length), jnp.bfloat16)
    back = jax.ShapeDtypeStruct((2, 2 * RANK, rows), jnp.bfloat16)
    grad_t = jax.ShapeDtypeStruct((width, length), jnp.bfloat16)
    return pl.pallas_call(
        attention_kernel,
        in_specs=[SMEM] * 2 + [VMEM] * 2,
        out_specs=[VMEM] * (3 + 2 * chips),
        scratch_shapes=[
            wide_t,
            wide_t,
            wide_t,
            wide_t,
            pltpu.VMEM((heads, length, HEAD_SIZE), jnp.float32),
            pltpu.VMEM((2 * RANK, length), jnp.bfloat16),
            pltpu.VMEM((length, width), jnp.bfloat16),
        ],
        out_shape=[jax.ShapeDtypeStruct((2, rows, width), jnp.bfloat16)] * chips
        + [back] * chips
        + [grad_t, grad_t]
        + [jax.ShapeDtypeStruct((seq_size, rows // 2, 2 * RANK), jnp.bfloat16)],
        compiler_params=pltpu.CompilerParams(vmem_limit_bytes=32 << 20),
        cost_estimate=pl.CostEstimate(
            flops=8 << 30, bytes_accessed=16 << 20, transcendentals=4 << 20
        ),
        name="attention",
    )(lengths, chip, packed, ups)


def up_kernel(core, low, low_other, dq_t, dv_t, up, lows):
    lows[core[0]] = low[...]
    lows[1 - core[0]] = low_other[...]
    devices, half, _ = low.shape
    for part, grads in enumerate((dq_t, dv_t)):
        upper = lower = jnp.zeros((grads.shape[0], 2 * RANK), jnp.float32)
        for device in range(devices):
            begin = 2 * device * half
            upper += dot(grads[:, begin : begin + half], lows[part, device])
            lower += dot(grads[:, begin + half : begin + 2 * half], lows[part, device])
        share = ADAPTER_SCALE * (upper.T[:RANK] + lower.T[RANK:])
        up[part * RANK : (part + 1) * RANK, :] = share.astype(jnp.bfloat16)


def up_gradient(core, low, low_other, dq_t, dv_t):
    return pl.pallas_call(
        up_kernel,
        in_specs=[SMEM] + [VMEM] * 4,
        out_specs=VMEM,
        out_shape=jax.ShapeDtypeStruct((2 * RANK, dq_t.shape[0]), jnp.bfloat16),
        scratch_shapes=[pltpu.VMEM((2,) + low.shape, jnp.bfloat16)],
        compiler_params=pltpu.CompilerParams(vmem_limit_bytes=16 << 20),
        name="up_gradient",
    )(core, low, low_other, dq_t, dv_t)


def pick_kernel(core, part_0, part_1, part_2, part_3, out):
    core = core[0]
    for step, part in enumerate((part_0, part_1, part_2, part_3)):
        out[step] = part[1 - core]


def pick(core, parts):
    return pl.pallas_call(
        pick_kernel,
        in_specs=[SMEM] + [VMEM] * len(parts),
        out_specs=VMEM,
        out_shape=jax.ShapeDtypeStruct((len(parts),) + parts[0].shape[1:], parts[0].dtype),
        compiler_params=pltpu.CompilerParams(vmem_limit_bytes=SMALL_VMEM),
        name="pick",
    )(core, *parts)


def arrive_kernel(chip, core, part_0, part_1, part_2, part_3, other, out, done):
    chip, core = chip[0], core[0]
    parts = (part_0, part_1, part_2, part_3)
    width = part_0.shape[2]
    for step in range(len(parts)):
        origin = lax.rem(chip + len(parts) - step, len(parts))
        here = pl.multiple_of((origin * 2 + core) * width, width)
        there = pl.multiple_of((origin * 2 + 1 - core) * width, width)
        out[0, :, pl.ds(here, width)] = parts[step][core]
        out[0, :, pl.ds(there, width)] = other[step]
    done[...] = jnp.zeros_like(done)


def arrive(chip, core, parts, other):
    _, rows, width = parts[0].shape
    return pl.pallas_call(
        arrive_kernel,
        in_specs=[SMEM] * 2 + [VMEM] * (len(parts) + 1),
        out_specs=[VMEM] * 2,
        out_shape=[
            jax.ShapeDtypeStruct((1, rows, 2 * len(parts) * width), parts[0].dtype),
            DONE,
        ],
        compiler_params=pltpu.CompilerParams(vmem_limit_bytes=SMALL_VMEM),
        name="arrive",
    )(chip, core, *parts, other)


def backs_kernel(part_0, part_1, part_2, part_3, *refs):
    out = refs[len(refs) // 2]
    total = part_0[...].astype(jnp.float32)
    for part in (part_1, part_2, part_3):
        total += part[...].astype(jnp.float32)
    out[...] = total.astype(out.dtype)


def sum_backs(parts, held):
    count = len(parts)
    return pl.pallas_call(
        backs_kernel,
        in_specs=[VMEM] * (count + len(held)),
        out_specs=[VMEM] * (1 + len(held)),
        out_shape=[
            jax.ShapeDtypeStruct(part.shape, part.dtype) for part in [parts[0]] + list(held)
        ],
        input_output_aliases={count + index: 1 + index for index in range(len(held))},
        compiler_params=pltpu.CompilerParams(vmem_limit_bytes=SMALL_VMEM),
        name="sum_backs",
    )(*parts, *held)


def halves_kernel(chip, core, hidden, other, wq_up, wv_up, out, ups):
    rows, half = other.shape
    out[:rows] = hidden[:, pl.ds(pl.multiple_of(core[0] * half, half), half)]
    out[rows:] = other[...]
    width = ups.shape[1]
    columns = pl.ds(pl.multiple_of((chip[0] * 2 + core[0]) * width, width), width)
    ups[:RANK] = wq_up[:, columns]
    ups[RANK:] = wv_up[:, columns]


def halves(chip, core, hidden, other, wq_up, wv_up, width):
    rows, half = other.shape
    return pl.pallas_call(
        halves_kernel,
        in_specs=[SMEM] * 2 + [VMEM] * 4,
        out_specs=[VMEM] * 2,
        out_shape=[
            jax.ShapeDtypeStruct((2 * rows, half), hidden.dtype),
            jax.ShapeDtypeStruct((2 * RANK, width), wq_up.dtype),
        ],
        compiler_params=pltpu.CompilerParams(vmem_limit_bytes=SMALL_VMEM),
        name="halves",
    )(chip, core, hidden, other, wq_up, wv_up)


def down_kernel(core, *refs):
    *parts, hidden, up, out, back = refs
    rows = parts[0].shape[2]

    @pl.when(pl.program_id(0) == 0)
    def _():
        total = parts[0][...].astype(jnp.float32)
        for part in parts[1:]:
            total += part[...].astype(jnp.float32)
        back[...] = total.astype(jnp.bfloat16)

    grad = dot(back[core[0]], hidden[:rows]) + dot(back[1 - core[0]], hidden[rows:])
    grad = grad.astype(out.dtype)
    for row in range(out.shape[0]):
        across = slice(row * SHARE_ROWS, (row + 1) * SHARE_ROWS)
        out[row, 0, :, :DOWN_COLS] = grad[across, :]
        out[row, 0, :, DOWN_COLS:] = up[across, :]


def down_gradient(core, parts, hidden, up):
    rows, half = hidden.shape
    steps = half // DOWN_COLS
    across = 2 * RANK // SHARE_ROWS
    shape = parts[0].shape
    return pl.pallas_call(
        down_kernel,
        grid_spec=pltpu.PrefetchScalarGridSpec(
            num_scalar_prefetch=1,
            grid=(steps,),
            in_specs=[pl.BlockSpec(shape, lambda i, core: (0, 0, 0))] * len(parts)
            + [
                pl.BlockSpec((rows, DOWN_COLS), lambda i, core: (0, i)),
                pl.BlockSpec((2 * RANK, UP_COLS), lambda i, core: (0, i)),
            ],
            out_specs=pl.BlockSpec(
                (across, 1, SHARE_ROWS, DOWN_COLS + UP_COLS), lambda i, core: (0, i, 0, 0)
            ),
            scratch_shapes=[pltpu.VMEM(shape, jnp.bfloat16)],
        ),
        out_shape=jax.ShapeDtypeStruct(
            (across, steps, SHARE_ROWS, DOWN_COLS + UP_COLS), jnp.bfloat16
        ),
        compiler_params=pltpu.CompilerParams(vmem_limit_bytes=24 << 20),
        name="down_gradient",
    )(core, *parts, hidden, up)


def share_kernel(parts, *refs):
    out = refs[-1]
    total = parts[0].astype(jnp.float32)
    for part in range(1, parts.shape[0]):
        total += parts[part].astype(jnp.float32)
    out[...] = total.astype(out.dtype)


def sum_share(parts, after):
    return pl.pallas_call(
        share_kernel,
        in_specs=[VMEM] + [VMEM] * len(after),
        out_specs=VMEM,
        out_shape=jax.ShapeDtypeStruct(parts.shape[1:], parts.dtype),
        compiler_params=pltpu.CompilerParams(vmem_limit_bytes=SMALL_VMEM),
        name="sum_share",
    )(parts, *after)


def chips_kernel(chip, *refs):
    *parts, out = refs
    chip = chip[0]
    total = parts[0][:, :DOWN_COLS].astype(jnp.float32)
    for part in parts[1:]:
        total += part[:, :DOWN_COLS].astype(jnp.float32)
    total = total.astype(out.dtype)
    for device in range(out.shape[0]):
        out[device, :, :DOWN_COLS] = total
    for step, part in zip((0, 2, 1, 3), parts):
        origin = lax.rem(chip + len(parts) - step, len(parts))
        begin = pl.multiple_of(DOWN_COLS + origin * UP_COLS, UP_COLS)
        for device in range(out.shape[0]):
            out[device, :, pl.ds(begin, UP_COLS)] = part[:, DOWN_COLS:]


def sum_chips(chip, parts, devices):
    shape = (devices, SHARE_ROWS, DOWN_COLS + len(parts) * UP_COLS)
    return pl.pallas_call(
        chips_kernel,
        in_specs=[SMEM] + [VMEM] * len(parts),
        out_specs=VMEM,
        out_shape=jax.ShapeDtypeStruct(shape, parts[0].dtype),
        compiler_params=pltpu.CompilerParams(vmem_limit_bytes=SMALL_VMEM),
        name="sum_chips",
    )(chip, *parts)


def place_kernel(which, shares, *refs):
    *outs, downs, ups, sems = refs[-7:]
    which = which[0]
    half = shares.shape[0] // 2
    columns = shares.shape[1]
    copies = []

    def send(source, target, begin, size):
        begin = pl.multiple_of(begin, size)
        copies.append(
            pltpu.make_async_copy(source, target.at[:, pl.ds(begin, size)], sems.at[len(copies)])
        )
        copies[-1].start()

    chips, _, width = ups.shape
    for row in range(2 * half):
        part, across = row // half, slice(row % half * SHARE_ROWS, (row % half + 1) * SHARE_ROWS)
        for column in range(columns):
            share = shares[row, column]
            downs[part, across, column * DOWN_COLS : (column + 1) * DOWN_COLS] = share[
                :, :DOWN_COLS
            ].astype(jnp.float32)
            for chip in range(chips):
                begin = DOWN_COLS + chip * UP_COLS
                ups[
                    chip,
                    row * SHARE_ROWS : (row + 1) * SHARE_ROWS,
                    column * UP_COLS : (column + 1) * UP_COLS,
                ] = share[:, begin : begin + UP_COLS].astype(jnp.float32)
        if row % half == half - 1:
            send(downs.at[part], outs[2 * part], which * downs.shape[2], downs.shape[2])
            for chip in range(chips):
                send(
                    ups.at[chip, part * RANK : (part + 1) * RANK, :],
                    outs[2 * part + 1],
                    (2 * chip + which) * width,
                    width,
                )
    for copy in copies:
        copy.wait()


def place(which, shares, model, width, earlier=()):
    shapes = [(RANK, model), (RANK, width), (RANK, model), (RANK, width)]
    columns = shares.shape[1]
    chips = (shares.shape[3] - DOWN_COLS) // UP_COLS
    return pl.pallas_call(
        place_kernel,
        in_specs=[SMEM, VMEM] + [ANY] * len(earlier),
        out_specs=[ANY] * 4,
        out_shape=[jax.ShapeDtypeStruct(shape, jnp.float32) for shape in shapes],
        scratch_shapes=[
            pltpu.VMEM((2, RANK, columns * DOWN_COLS), jnp.float32),
            pltpu.VMEM((chips, 2 * RANK, columns * UP_COLS), jnp.float32),
            pltpu.SemaphoreType.DMA((2 + 2 * chips,)),
        ],
        input_output_aliases={2 + index: index for index in range(len(earlier))},
        compiler_params=pltpu.CompilerParams(vmem_limit_bytes=16 << 20),
        name="place",
    )(which, shares, *earlier)


def swap(x, axes):
    return lax.all_to_all(x, axes, 0, 0, tiled=True)


def to_other_core(x):
    return lax.ppermute(x, "core", [(0, 1), (1, 0)])


def per_device(
    sizes,
    hidden,
    frozen_queries,
    frozen_keys,
    frozen_values,
    document_length_list,
    query_down_weight,
    query_up_weight,
    value_down_weight,
    value_up_weight,
    output_gradient,
):
    dp_size, seq_size = sizes
    chips = seq_size // 2
    rows, model = hidden.shape[1:]
    half = model // 2
    chip = lax.axis_index("y").astype(jnp.int32)[None]
    core = lax.axis_index("core").astype(jnp.int32)[None]
    width = frozen_queries.shape[2] // seq_size

    def to_chip(x, step):
        return lax.ppermute(x, "y", [(c, (c + step) % chips) for c in range(chips)])

    packed, hidden_leaving = pack(
        core,
        hidden[0],
        query_down_weight.T,
        value_down_weight.T,
        frozen_queries[0],
        frozen_keys[0],
        frozen_values[0],
        output_gradient[0],
        query_up_weight,
        value_up_weight,
        seq_size,
    )
    received = swap(packed, SEQ)
    hidden_other = to_other_core(hidden_leaving)
    hidden_half, ups = halves(
        chip, core, hidden[0], hidden_other, query_up_weight, value_up_weight, width
    )
    *outs, dq_t, dv_t, low = attention(
        document_length_list,
        chip,
        received,
        ups,
    )
    parts, backs = outs[:chips], outs[chips:]

    backs = [backs[0]] + [to_chip(backs[step], step) for step in range(1, chips)]
    back, *held = sum_backs([backs[0], backs[2], backs[1], backs[3]], parts[-2:])
    parts = parts[:-2] + held
    back_other = to_other_core(back)
    parts = [parts[0]] + [to_chip(parts[step], step) for step in range(1, chips)]
    up = up_gradient(core, low, to_other_core(low), dq_t, dv_t)
    down = down_gradient(core, [back, back_other], hidden_half, up)

    other = to_other_core(pick(core, parts))
    attended, attended_done = arrive(chip, core, parts, other)

    shares = swap(down.reshape((-1,) + down.shape[2:]), DP)
    share = sum_share(shares, after=[attended_done])
    share = [share] + [to_chip(share, step) for step in (2, 1, 3)]
    shares = swap(sum_chips(chip, share, shares.shape[0]), DP)
    shares = shares.reshape(down.shape[:2] + shares.shape[1:])
    shares_other = to_other_core(shares)
    grads = place(core, shares, model, seq_size * width)
    grad_a_q, up_q, grad_a_v, up_v = place(
        1 - core, shares_other, model, seq_size * width, earlier=grads
    )
    return attended, grad_a_q.T, up_q, grad_a_v.T, up_v


def solution(mesh):
    dp_size, seq_size = mesh.shape["dp"], mesh.shape["seq"]
    fine = Mesh(mesh.devices.reshape(4, 4, 4, 2), ALL)
    rows = P(DP, SEQ, None)
    in_specs = (rows, rows, rows, rows, P(DP, None), P(), P(), P(), P(), rows)
    out_specs = (rows, P(), P(), P(), P())
    return jax.shard_map(
        functools.partial(per_device, (dp_size, seq_size)),
        mesh=fine,
        in_specs=in_specs,
        out_specs=out_specs,
        check_vma=False,
    )
```
